128 devices in a mesh: date: 8 (over y, z_hi), rng: 16 (over z_lo, x, core).
Axes of the slice: x: 4, y: 4, z: 4 (z_hi: 2, z_lo: 2; z = z_hi * 2 + z_lo), core: 2. Of those that a mesh axis runs over, the one named last changes fastest.
Arguments:
- raw_echoes: bfloat16 [8, 2, 1024, 16384], P('date', None, 'rng'), may hold values from -6 to 6
- range_filter: float32 [2, 16384], replicated, may hold values from -4 to 4
- azimuth_filter: bfloat16 [2, 1024, 16384], P(None, None, 'rng'), may hold values from -4 to 4
- partner_date: int32 [8], replicated, may hold values from 0 to 7, as said below
- chip_lines: int32 [64], P('rng'), may hold values from 0 to 896
- chip_bins: int32 [64], P('rng'), may hold values from 0 to 896
- chip_offsets: int32 [64, 2], P('rng'), may hold values from 0 to 64
Outputs:
- focused_image: bfloat16 [8, 2, 1024, 16384], P('date', None, None, 'rng')
- correlation: float32 [8, 64, 64, 128], P('date', 'rng')
The draws below stay inside these ranges and needn't reach their ends.
Inputs may be any that keep to these rules, and one draw needn't show every extreme that they name: partner_date runs through all 8 dates in a single cycle; no date is its own partner.
All inputs are finite; a program needn't handle non-finite values.
Results may differ from the reference program's by a relative error of at most 0.03.
Values may be sent and summed in bfloat16 or wider, within the bound.
No kernel may reach another device: no remote copies, remote signals or barrier semaphores. Data moves between devices by JAX's collectives and lax.ppermute only.
A program may use at most 128 MiB of HBM per device.

```python
import math
import jax
import jax.numpy as jnp
from jax import lax

LINES = 1024
BINS = 16384
CHIP = 64
CHIPS = 4
WIN = 128
DATES = 8
CH_ALL = 64
N_RNG = 16


def draw_partner_date(key, part):
    key = jax.random.fold_in(key, 7)
    order = jax.random.permutation(key, DATES).astype(jnp.int32)
    following = jnp.roll(order, -1)
    return jnp.zeros((DATES,), jnp.int32).at[order].set(following)


def touch_ends(values, rng, least, largest):
    index_at = [jax.random.randint(jax.random.fold_in(rng, axis), (), 0, length) for axis, length in enumerate(values.shape)]
    main_axis = values.shape.index(max(values.shape))
    beside = index_at[:main_axis] + [(index_at[main_axis] + 1) % values.shape[main_axis]] + index_at[main_axis + 1:]
    return values.at[tuple(index_at)].set(least).at[tuple(beside)].set(largest)


def block_scale(key, shape, cuts, least, top_value):
    factor_of = 1.0
    for dim, parts in cuts:
        heights = jax.random.uniform(jax.random.fold_in(jax.random.fold_in(key, 6), dim), (parts,), jnp.float32, least / len(cuts), top_value / len(cuts))
        factor_of = factor_of * jnp.repeat(jnp.exp(heights), shape[dim] // parts).reshape((-1,) + (1,) * (len(shape) - 1 - dim))
    return factor_of


def normal_values(key, dims, width, bound, cuts=(), held_as=jnp.bfloat16):
    factor_of = block_scale(key, dims, cuts, -0.22, 0.18) if cuts else 1.0
    values = jax.random.normal(key, dims, jnp.float32) * width * factor_of
    return jnp.minimum(jnp.maximum(values, -bound), bound).astype(held_as)


def setup_inputs(seed: int = 0) -> dict:
    key_list = jax.random.split(jax.random.key(seed), 8)
    return {
        "raw_echoes": normal_values(key_list[0], (DATES, 2, LINES, BINS), 1.0, 6.0, ((0, 8), (2, 16))),
        "range_filter": normal_values(key_list[1], (2, BINS), 0.7071, 4.0, (), jnp.float32),
        "azimuth_filter": normal_values(key_list[2], (2, LINES, BINS), 0.7071, 4.0, ((2, 16),)),
        "partner_date": draw_partner_date(jax.random.fold_in(key_list[7], 71), 0),
        "chip_lines": touch_ends(jax.random.randint(key_list[4], (CH_ALL,), 0, LINES - WIN + 1), jax.random.fold_in(key_list[4], 1), 0, LINES - WIN).astype(jnp.int32),
        "chip_bins": touch_ends(jax.random.randint(key_list[5], (CH_ALL,), 0, BINS // N_RNG - WIN + 1), jax.random.fold_in(key_list[5], 1), 0, (BINS // N_RNG - WIN + 1) - 1).astype(jnp.int32),
        "chip_offsets": touch_ends(jax.random.randint(key_list[6], (CH_ALL, 2), 0, CHIP + 1), jax.random.fold_in(key_list[6], 1), 0, CHIP).astype(jnp.int32),
    }


def dft_table(length, sign):
    index = jnp.arange(length, dtype=jnp.int32)
    phase = index[:, None] * index[None, :] % length
    angle = sign * 2.0 * math.pi * phase.astype(jnp.float32) / length
    factor = 1.0 / math.sqrt(length)
    return (jnp.cos(angle) * factor, jnp.sin(angle) * factor)

def twiddle_table(count, length, sign):
    index = jnp.arange(count, dtype=jnp.int32)
    phase = index[:, None] * index[None, :] % length
    angle = sign * 2.0 * math.pi * phase.astype(jnp.float32) / length
    return (jnp.cos(angle), jnp.sin(angle))

def complex_product(form, left, right):
    left_real = left[0].astype(jnp.bfloat16)
    left_imag = left[1].astype(jnp.bfloat16)
    right_real = right[0].astype(jnp.bfloat16)
    right_imag = right[1].astype(jnp.bfloat16)

    def single(first, second):
        return jnp.einsum(form, first.astype(jnp.float32), second.astype(jnp.float32))
    return (single(left_real, right_real) - single(left_imag, right_imag), single(left_real, right_imag) + single(left_imag, right_real))

def complex_times(left, right):
    return (left[0] * right[0] - left[1] * right[1], left[0] * right[1] + left[1] * right[0])

def compress_range(echo_pair, range_filter):
    lines = echo_pair.shape[1]
    bins = echo_pair.shape[2]
    split = math.isqrt(bins)
    forward = dft_table(split, -1.0)
    backward = dft_table(split, 1.0)
    signal = tuple((echo_pair[part].astype(jnp.float32).reshape(lines, split, split) for part in range(2)))
    section = complex_product('kn,lnm->lkm', forward, signal)
    section = complex_times(section, twiddle_table(split, bins, -1.0))
    spectrum = complex_product('lkn,nm->lkm', section, forward)
    response = tuple((range_filter[part].astype(jnp.float32).reshape(split, split).T for part in range(2)))
    spectrum = complex_times(spectrum, response)
    section = complex_product('lkm,mb->lkb', spectrum, backward)
    section = complex_times(section, twiddle_table(split, bins, 1.0))
    result = complex_product('ak,lkb->lab', backward, section)
    return jnp.stack([part.reshape(lines, bins) for part in result]).astype(jnp.bfloat16)

def focus_azimuth(turned, azimuth_filter):
    lines = turned.shape[1]
    block = turned.shape[2]
    split = math.isqrt(lines)
    forward = dft_table(split, -1.0)
    backward = dft_table(split, 1.0)
    signal = tuple((turned[part].astype(jnp.float32).reshape(split, split, block) for part in range(2)))
    section = complex_product('kn,nmb->kmb', forward, signal)
    section = complex_times(section, tuple((table[:, :, None] for table in twiddle_table(split, lines, -1.0))))
    spectrum = complex_product('jn,knb->kjb', forward, section)
    response = tuple((azimuth_filter[part].astype(jnp.float32).reshape(split, split, block).transpose(1, 0, 2) for part in range(2)))
    spectrum = complex_times(spectrum, response)
    section = complex_product('pj,kjb->kpb', backward, spectrum)
    section = complex_times(section, tuple((table[:, :, None] for table in twiddle_table(split, lines, 1.0))))
    result = complex_product('ak,kpb->apb', backward, section)
    return jnp.stack([part.reshape(lines, block) for part in result]).astype(jnp.bfloat16)

def cut_windows(image, rows, cols, size):

    def one(row, col):
        return lax.dynamic_slice(image, (jnp.zeros((), jnp.int32), row.astype(jnp.int32), col.astype(jnp.int32)), (2, size, size))
    return jax.vmap(one)(rows, cols)

def correlate(own_windows, partner_windows, offsets, chip):
    window = own_windows.shape[-1]

    def primary_of(piece, offset):
        return lax.dynamic_slice(piece, (jnp.zeros((), jnp.int32), offset[0].astype(jnp.int32), offset[1].astype(jnp.int32)), (2, chip, chip))
    primary = jax.vmap(primary_of)(own_windows, offsets)
    padded = jnp.pad(primary, ((0, 0), (0, 0), (0, window - chip), (0, window - chip)))
    table = dft_table(window, -1.0)

    def transform(pair):
        section = complex_product('ij,cjk->cik', table, pair)
        return complex_product('cik,kl->cil', section, table)
    first = transform((padded[:, 0].astype(jnp.float32), padded[:, 1].astype(jnp.float32)))
    second = transform((partner_windows[:, 0].astype(jnp.float32), partner_windows[:, 1].astype(jnp.float32)))
    product = (first[0] * second[0] + first[1] * second[1], first[1] * second[0] - first[0] * second[1])
    surface = transform(product)
    factor = window / chip
    return jnp.concatenate([surface[0][:, :chip, :chip], surface[1][:, :chip, :chip]], axis=2) * factor

def reference(raw_echoes, range_filter, azimuth_filter, partner_date, chip_lines, chip_bins, chip_offsets):
    images = []
    for date in range(DATES):
        compressed = compress_range(raw_echoes[date], range_filter)
        images.append(focus_azimuth(compressed, azimuth_filter))
    focused_image = jnp.stack(images)
    block = BINS // N_RNG
    owners = jnp.arange(CH_ALL, dtype=jnp.int32) // CHIPS
    columns = owners * block + chip_bins.astype(jnp.int32)
    results = []
    for date in range(DATES):
        own = cut_windows(focused_image[date], chip_lines, columns, WIN)
        other = cut_windows(focused_image[partner_date[date]], chip_lines, columns, WIN)
        results.append(correlate(own, other, chip_offsets, CHIP).astype(jnp.float32))
    return (focused_image, jnp.stack(results))
```

```python
import functools
import math

import jax
import jax.numpy as jnp
import ml_dtypes
import numpy as np
from jax import lax
from jax.experimental import pallas as pl
from jax.experimental.pallas import tpu as pltpu
from jax.sharding import PartitionSpec as P

LINES = 1024
BINS = 16384
CHIP = 64
CHIPS = 4
WIN = 128
DATES = 8
N_RNG = 16
SIDE = 128
FAN = 8
BLOCK = BINS // N_RNG
OWN = LINES // N_RNG
GROUP = 16
SPAN = 256
VMEM = 56 * 1024 * 1024


def dft(length, sign):
    phase = np.outer(np.arange(length), np.arange(length)) % length
    return np.exp(sign * 2j * math.pi * phase / length) / math.sqrt(length)


def twiddles(count, other, sign):
    phase = np.outer(np.arange(count), np.arange(other))
    return np.exp(sign * 2j * math.pi * phase / (count * other))


def from_left(table):
    return np.block([[table.real, -table.imag], [table.imag, table.real]])


def from_right(table):
    return np.block([[table.real, table.imag], [-table.imag, table.real]])


def as_bf16(table):
    return jnp.asarray(np.asarray(table, np.float32).astype(ml_dtypes.bfloat16))


def parts_of(table):
    return jnp.asarray(np.stack([table.real, table.imag]).astype(np.float32))


def times(a, b):
    return (a[0] * b[0] - a[1] * b[1], a[0] * b[1] + a[1] * b[0])


def dot(a, b):
    return jnp.dot(a, b, preferred_element_type=jnp.float32)


def bf16(x):
    return x.astype(jnp.bfloat16)


def range_kernel(x_ref, h_ref, w_ref, t1_ref, t2_ref, t3_ref, t4_ref, out_ref, xs, ys):
    s = SIDE
    for part in range(2):
        for n in range(s):
            row = (part * s + n) * GROUP
            xs[row : row + GROUP, :] = x_ref[0, part, :, n * s : (n + 1) * s].astype(jnp.float32)
    w = (w_ref[0], w_ref[1])
    wc = (w[0], -w[1])
    h = (h_ref[0], h_ref[1])
    for line in range(0, GROUP, 2):
        pair = []
        for one in (line, line + 1):
            pair.append(
                jnp.concatenate(
                    [bf16(xs[pl.ds(part * s * GROUP + one, s, stride=GROUP), :]) for part in (0, 1)],
                    axis=0,
                )
            )
        y = dot(t1_ref[...], jnp.concatenate(pair, axis=1))
        rows = []
        for one in (0, 1):
            cut = y[:, one * s : (one + 1) * s]
            z = times((cut[:s], cut[s:]), w)
            rows.append(jnp.concatenate([bf16(z[0]), bf16(z[1])], axis=1))
        y = dot(jnp.concatenate(rows, axis=0), t2_ref[...])
        rows = []
        for one in (0, 1):
            cut = y[one * s : (one + 1) * s]
            z = times((cut[:, :s], cut[:, s:]), h)
            rows.append(jnp.concatenate([bf16(z[0]), bf16(z[1])], axis=1))
        y = dot(jnp.concatenate(rows, axis=0), t3_ref[...])
        pair = []
        for one in (0, 1):
            cut = y[one * s : (one + 1) * s]
            z = times((cut[:, :s], cut[:, s:]), wc)
            pair.append(jnp.concatenate([bf16(z[0]), bf16(z[1])], axis=0))
        y = dot(t4_ref[...], jnp.concatenate(pair, axis=1))
        for one in (0, 1):
            for part in (0, 1):
                ys[pl.ds(part * GROUP + line + one, s, stride=2 * GROUP), :] = y[
                    part * s : (part + 1) * s, one * s : (one + 1) * s
                ]
    per = BLOCK // s
    for a in range(s):
        for part in (0, 1):
            row = (a * 2 + part) * GROUP
            out_ref[a // per, part, :, (a % per) * s : (a % per + 1) * s] = bf16(
                ys[row : row + GROUP, :]
            )


def whole(shape):
    return pl.BlockSpec(shape, lambda *_: (0,) * len(shape))


def compress_range(raw_echoes, response):
    forward = dft(SIDE, -1)
    backward = dft(SIDE, 1)
    tables = [
        as_bf16(from_left(forward)),
        as_bf16(from_right(forward)),
        as_bf16(from_right(backward)),
        as_bf16(from_left(backward)),
    ]
    turn = parts_of(twiddles(SIDE, SIDE, -1))
    table = whole((2 * SIDE, 2 * SIDE))
    return pl.pallas_call(
        range_kernel,
        grid=(OWN // GROUP,),
        in_specs=[
            pl.BlockSpec((1, 2, GROUP, BINS), lambda i: (0, 0, i, 0)),
            whole((2, SIDE, SIDE)),
            whole((2, SIDE, SIDE)),
            table,
            table,
            table,
            table,
        ],
        out_specs=pl.BlockSpec((N_RNG, 2, GROUP, BLOCK), lambda i: (0, 0, i, 0)),
        out_shape=jax.ShapeDtypeStruct((N_RNG, 2, OWN, BLOCK), jnp.bfloat16),
        scratch_shapes=[
            pltpu.VMEM((2 * SIDE * GROUP, SIDE), jnp.float32),
            pltpu.VMEM((2 * SIDE * GROUP, SIDE), jnp.float32),
        ],
        compiler_params=pltpu.CompilerParams(vmem_limit_bytes=VMEM),
        name="compress_range",
    )(raw_echoes, response, turn, *tables)


def add(a, b):
    return (a[0] + b[0], a[1] + b[1])


def sub(a, b):
    return (a[0] - b[0], a[1] - b[1])


def fan_dft(x, sign):
    root = math.sqrt(0.5)

    def quarter(a):
        return (-sign * a[1], sign * a[0]) if sign > 0 else (a[1], -a[0])

    def eighth(a):
        if sign > 0:
            return ((a[0] - a[1]) * root, (a[0] + a[1]) * root)
        return ((a[0] + a[1]) * root, (a[1] - a[0]) * root)

    def four(a, b, c, d):
        e, f, g, h = add(a, c), sub(a, c), add(b, d), quarter(sub(b, d))
        return add(e, g), add(f, h), sub(e, g), sub(f, h)

    even = four(x[0], x[2], x[4], x[6])
    odd = four(x[1], x[3], x[5], x[7])
    odd = (odd[0], eighth(odd[1]), quarter(odd[2]), quarter(eighth(odd[3])))
    return [add(p, q) for p, q in zip(even, odd)] + [sub(p, q) for p, q in zip(even, odd)]


def azimuth_kernel(r_ref, f_ref, w_ref, t5_ref, t6_ref, out_ref, spread, mixed):
    m = LINES // FAN
    for half in range(2):
        for tile in range(OWN // 16):
            for lane in range(SPAN // 128):
                lanes = slice(lane * 128, (lane + 1) * 128)
                points = []
                for n in range(FAN):
                    points.append(
                        tuple(
                            r_ref[
                                2 * n + half, part * OWN + tile * 16 : part * OWN + tile * 16 + 16, lanes
                            ].astype(jnp.float32)
                            for part in (0, 1)
                        )
                    )
                line = half * OWN + tile * 16
                for k, value in enumerate(fan_dft(points, -1)):
                    if k:
                        row = k * m + line
                        value = times(value, (w_ref[0, row : row + 16], w_ref[1, row : row + 16]))
                    for part in (0, 1):
                        row = (half * 2 + part) * OWN + tile * 16
                        spread[k, row : row + 16, lanes] = bf16(value[part])
    for k in range(FAN):
        y = dot(t5_ref[...], spread[k])
        f = (f_ref[k, 0].astype(jnp.float32), f_ref[k, 1].astype(jnp.float32))
        z = times((y[:m], y[m:]), f)
        y = dot(t6_ref[...], jnp.concatenate([bf16(z[0]), bf16(z[1])], axis=0))
        for lane in range(SPAN // 128):
            lanes = slice(lane * 128, (lane + 1) * 128)
            value = (y[:m, lanes], y[m:, lanes])
            if k:
                w = (w_ref[0, k * m : (k + 1) * m], -w_ref[1, k * m : (k + 1) * m])
                value = times(value, w)
            for part in (0, 1):
                mixed[k, part * m : (part + 1) * m, lanes] = value[part]
    for tile in range(m // 16):
        for lane in range(SPAN // 128):
            lanes = slice(lane * 128, (lane + 1) * 128)
            points = [
                tuple(mixed[k, part * m + tile * 16 : part * m + tile * 16 + 16, lanes] for part in (0, 1))
                for k in range(FAN)
            ]
            for p, value in enumerate(fan_dft(points, 1)):
                row = p * m + tile * 16
                for part in (0, 1):
                    out_ref[0, part, row : row + 16, lanes] = bf16(value[part])


def focus_azimuth(turned, response):
    m = LINES // FAN
    forward = np.exp(-2j * math.pi * np.outer(np.arange(m), np.arange(m)) / m) / math.sqrt(LINES)
    backward = forward.conj()
    first = from_left(forward).reshape(2 * m, 2, 2, OWN).transpose(0, 2, 1, 3).reshape(2 * m, 2 * m)
    turn = twiddles(FAN, m, -1).reshape(LINES, 1) * np.ones((1, 128))
    table = whole((2 * m, 2 * m))
    return pl.pallas_call(
        azimuth_kernel,
        grid=(BLOCK // SPAN,),
        in_specs=[
            pl.BlockSpec((N_RNG, 2 * OWN, SPAN), lambda i: (0, 0, i)),
            pl.BlockSpec((FAN, 2, m, SPAN), lambda i: (0, 0, 0, i)),
            whole((2, LINES, 128)),
            table,
            table,
        ],
        out_specs=pl.BlockSpec((1, 2, LINES, SPAN), lambda i: (0, 0, 0, i)),
        out_shape=jax.ShapeDtypeStruct((1, 2, LINES, BLOCK), jnp.bfloat16),
        scratch_shapes=[
            pltpu.VMEM((FAN, 2 * m, SPAN), jnp.bfloat16),
            pltpu.VMEM((FAN, 2 * m, SPAN), jnp.float32),
        ],
        compiler_params=pltpu.CompilerParams(vmem_limit_bytes=VMEM),
        name="focus_azimuth",
    )(turned, response, parts_of(turn), as_bf16(first), as_bf16(from_left(backward)))


def regroup_kernel(f_ref, out_ref, wide):
    m = LINES // FAN
    for part in (0, 1):
        wide[...] = f_ref[part].astype(jnp.float32)
        for k in range(FAN):
            out_ref[k, part] = bf16(wide[pl.ds(k, m, stride=FAN), :])


def regroup_filter(azimuth_filter):
    m = LINES // FAN
    return pl.pallas_call(
        regroup_kernel,
        grid=(BLOCK // 128,),
        in_specs=[pl.BlockSpec((2, LINES, 128), lambda i: (0, 0, i))],
        out_specs=pl.BlockSpec((FAN, 2, m, 128), lambda i: (0, 0, 0, i)),
        out_shape=jax.ShapeDtypeStruct((FAN, 2, m, BLOCK), jnp.bfloat16),
        scratch_shapes=[pltpu.VMEM((LINES, 128), jnp.float32)],
        compiler_params=pltpu.CompilerParams(vmem_limit_bytes=VMEM),
        cost_estimate=pl.CostEstimate(flops=10**7, bytes_accessed=2**23, transcendentals=0),
        name="regroup_filter",
    )(azimuth_filter)


ROWS = WIN + 16
COLS = 2 * WIN


def window_kernel(lines_ref, bins_ref, image_ref, out_ref, held, sems):
    copies = []
    corners = []
    for chip in range(CHIPS):
        line = lines_ref[chip]
        at_bin = bins_ref[chip]
        row = jnp.minimum(line // 16 * 16, LINES - ROWS)
        col = jnp.minimum(at_bin // WIN * WIN, BLOCK - COLS)
        copy = pltpu.make_async_copy(
            image_ref.at[0, :, pl.ds(pl.multiple_of(row, 16), ROWS), pl.ds(pl.multiple_of(col, WIN), COLS)],
            held.at[chip],
            sems.at[chip],
        )
        copy.start()
        copies.append(copy)
        corners.append((line - row, at_bin - col))
    for chip in range(CHIPS):
        copies[chip].wait()
        row, col = corners[chip]
        for part in (0, 1):
            cut = held[chip, part].astype(jnp.float32)
            cut = pltpu.roll(cut, lax.rem(ROWS - row, ROWS), 0)[:WIN]
            cut = pltpu.roll(cut, lax.rem(COLS - col, COLS), 1)
            out_ref[chip * 2 + part] = bf16(cut[:, :WIN])


def cut_windows(image, chip_lines, chip_bins):
    return pl.pallas_call(
        window_kernel,
        in_specs=[
            pl.BlockSpec(memory_space=pltpu.SMEM),
            pl.BlockSpec(memory_space=pltpu.SMEM),
            pl.BlockSpec(memory_space=pl.ANY),
        ],
        out_specs=pl.BlockSpec(memory_space=pltpu.VMEM),
        out_shape=jax.ShapeDtypeStruct((CHIPS * 2, WIN, WIN), jnp.bfloat16),
        scratch_shapes=[
            pltpu.VMEM((CHIPS, 2, ROWS, COLS), jnp.bfloat16),
            pltpu.SemaphoreType.DMA((CHIPS,)),
        ],
        compiler_params=pltpu.CompilerParams(vmem_limit_bytes=VMEM),
        name="cut_windows",
    )(chip_lines, chip_bins, image)


def reorder_kernel(order_ref, x_ref, out_ref):
    for date in range(DATES):
        out_ref[date] = x_ref[order_ref[date]]


def reorder(x, order):
    return pl.pallas_call(
        reorder_kernel,
        in_specs=[pl.BlockSpec(memory_space=pltpu.SMEM), pl.BlockSpec(memory_space=pltpu.VMEM)],
        out_specs=pl.BlockSpec(memory_space=pltpu.VMEM),
        out_shape=jax.ShapeDtypeStruct(x.shape, x.dtype),
        name="reorder",
    )(order, x)


def transform(stacked, left, right):
    y = dot(left, jnp.concatenate(stacked, axis=1))
    half = y.shape[0] // 2
    rows = []
    for chip in range(CHIPS):
        cut = y[:, chip * WIN : (chip + 1) * WIN]
        rows.append(jnp.concatenate([bf16(cut[:half]), bf16(cut[half:])], axis=1))
    return dot(jnp.concatenate(rows, axis=0), right)


def correlate_kernel(
    offsets_ref, own_ref, their_ref, left_ref, right_ref, left3_ref, right3_ref, out_ref
):
    left, right = left_ref[...], right_ref[...]
    inside = lax.broadcasted_iota(jnp.int32, (CHIP, WIN), 1) < CHIP
    empty = jnp.zeros((WIN - CHIP, WIN), jnp.bfloat16)
    primary = []
    for chip in range(CHIPS):
        row, col = offsets_ref[chip, 0], offsets_ref[chip, 1]
        pieces = []
        for part in (0, 1):
            cut = own_ref[chip * 2 + part].astype(jnp.float32)
            cut = pltpu.roll(cut, lax.rem(WIN - row, WIN), 0)[:CHIP]
            cut = pltpu.roll(cut, lax.rem(WIN - col, WIN), 1)
            pieces += [bf16(jnp.where(inside, cut, 0.0)), empty]
        primary.append(jnp.concatenate(pieces, axis=0))
    first = transform(primary, left, right)
    second = transform(
        [jnp.concatenate([their_ref[2 * chip], their_ref[2 * chip + 1]], axis=0) for chip in range(CHIPS)],
        left,
        right,
    )
    a = (first[:, :WIN], first[:, WIN:])
    b = (second[:, :WIN], second[:, WIN:])
    product = (a[0] * b[0] + a[1] * b[1], a[1] * b[0] - a[0] * b[1])
    product = [bf16(part) for part in product]
    surface = transform(
        [
            jnp.concatenate([part[chip * WIN : (chip + 1) * WIN] for part in product], axis=0)
            for chip in range(CHIPS)
        ],
        left3_ref[...],
        right3_ref[...],
    )
    for chip in range(CHIPS):
        out_ref[0, chip] = surface[chip * CHIP : (chip + 1) * CHIP]


def correlate(own, theirs, offsets):
    table = dft(WIN, -1)
    left, right = from_left(table), from_right(table)
    factor = WIN // CHIP
    keep = np.concatenate([np.arange(CHIP), WIN + np.arange(CHIP)])
    vmem = pl.BlockSpec(memory_space=pltpu.VMEM)
    return pl.pallas_call(
        correlate_kernel,
        in_specs=[pl.BlockSpec(memory_space=pltpu.SMEM)] + [vmem] * 6,
        out_specs=vmem,
        out_shape=jax.ShapeDtypeStruct((1, CHIPS, CHIP, 2 * CHIP), jnp.float32),
        compiler_params=pltpu.CompilerParams(vmem_limit_bytes=VMEM),
        name="correlate",
    )(
        offsets,
        own,
        theirs,
        as_bf16(left),
        as_bf16(right),
        as_bf16(left[keep]),
        as_bf16(right[:, keep] * factor),
    )


def local(
    raw_echoes, range_filter, azimuth_filter, partner_date, chip_lines, chip_bins, chip_offsets
):
    response = range_filter.reshape(2, SIDE, SIDE).transpose(0, 2, 1)
    compressed = compress_range(raw_echoes, response).reshape(N_RNG, 2 * OWN, BLOCK)
    turned = lax.all_to_all(compressed, "rng", split_axis=0, concat_axis=0, tiled=True)
    image = focus_azimuth(turned, regroup_filter(azimuth_filter))
    own = cut_windows(image, chip_lines, chip_bins)
    spread = lax.all_to_all(own, "date", split_axis=0, concat_axis=0, tiled=True)
    theirs = lax.all_to_all(
        reorder(spread, partner_date), "date", split_axis=0, concat_axis=0, tiled=True
    )
    return (image, correlate(own, theirs, chip_offsets))


def solution(mesh):
    in_specs = (
        P("date", None, "rng", None),
        P(),
        P(None, None, "rng"),
        P(),
        P("rng"),
        P("rng"),
        P("rng", None),
    )
    out_specs = (P("date", None, None, "rng"), P("date", "rng", None, None))
    return jax.shard_map(local, mesh=mesh, in_specs=in_specs, out_specs=out_specs, check_vma=False)
```

```python
import functools
import math

import jax
import jax.numpy as jnp
import ml_dtypes
import numpy as np
from jax import lax
from jax.experimental import pallas as pl
from jax.experimental.pallas import tpu as pltpu
from jax.sharding import PartitionSpec as P

LINES = 1024
BINS = 16384
CHIP = 64
CHIPS = 4
WIN = 128
DATES = 8
N_RNG = 16
SIDE = 128
FAN = 8
BLOCK = BINS // N_RNG
OWN = LINES // N_RNG
SLOTS = 8
HALF = 4
PART = HALF * 128
SORT = ((0, 1), (2, 3), (0, 2), (1, 3), (1, 2))
NETWORK = SORT + tuple((i + 4, j + 4) for i, j in SORT) + ((0, 7), (1, 6), (2, 5), (3, 4))
GROUP = 16
BATCH = 16
SPAN = 256
WIDE = GROUP + 8
LONG = SIDE + 8
VMEM = 56 * 1024 * 1024


def dft(length, sign):
    phase = np.outer(np.arange(length), np.arange(length)) % length
    return np.exp(sign * 2j * math.pi * phase / length) / math.sqrt(length)


def twiddles(count, other, sign):
    phase = np.outer(np.arange(count), np.arange(other))
    return np.exp(sign * 2j * math.pi * phase / (count * other))


def from_left(table):
    return np.block([[table.real, -table.imag], [table.imag, table.real]])


def from_right(table):
    return np.block([[table.real, table.imag], [-table.imag, table.real]])


def as_bf16(table):
    return jnp.asarray(np.asarray(table, np.float32).astype(ml_dtypes.bfloat16))


def parts_of(table):
    return jnp.asarray(np.stack([table.real, table.imag]).astype(np.float32))


def times(a, b):
    return (a[0] * b[0] - a[1] * b[1], a[0] * b[1] + a[1] * b[0])


def dot(a, b):
    return jnp.dot(a, b, preferred_element_type=jnp.float32)


def bf16(x):
    return x.astype(jnp.bfloat16)


def swapped(slots, swaps, pairs):
    slots = list(slots)
    for swap, (i, j) in zip(swaps, pairs):
        slots[i], slots[j] = (
            jnp.where(swap, slots[j], slots[i]),
            jnp.where(swap, slots[i], slots[j]),
        )
    return slots


def masks(ref):
    return [jnp.broadcast_to(ref[at : at + 1, :], (16, SIDE)) > 0.5 for at in range(len(NETWORK))]


def plan_kernel(me_ref, near_ref, *refs):
    far_refs, (swap_ref, own_ref, pick_ref) = refs[:3], refs[3:]
    me = me_ref[0]
    lane = lax.broadcasted_iota(jnp.int32, (N_RNG, SIDE), 1)
    device = lax.broadcasted_iota(jnp.int32, (N_RNG, SIDE), 0)
    runs = []
    for chip in range(CHIPS):
        first = jnp.zeros((N_RNG, SIDE), jnp.int32)
        for far, ref in zip((0, *FAR), (near_ref, *far_refs)):
            for at, near in enumerate((0, *NEAR)):
                first = jnp.where(device == (me ^ far ^ near), ref[at * CHIPS + chip], first)
        runs.append(first // SIDE + jnp.where(lane < first % SIDE, 1, 0))
    holds = [[jnp.where(run == slot, 1.0, 0.0) for slot in range(SLOTS)] for run in runs]
    wanted = [functools.reduce(jnp.maximum, [hold[slot] for hold in holds]) for slot in range(SLOTS)]
    for at, (i, j) in enumerate(NETWORK):
        swap = wanted[j] > wanted[i]
        swap_ref[at] = jnp.where(swap, 1.0, 0.0)
        wanted = swapped(wanted, [swap], [(i, j)])
        holds = [swapped(hold, [swap], [(i, j)]) for hold in holds]
    for at in range(len(NETWORK)):
        own_ref[at : at + 1, :] = swap_ref[at, pl.ds(me, 1), :]
    for chip in range(CHIPS):
        for slot in range(HALF):
            at = chip * HALF + slot
            pick_ref[at] = holds[chip][slot]


NEAR = (1, 8, 9)
FAR = (2, 4, 6)


def from_ways(x, axis, size, ways):
    return [lax.ppermute(x, axis, [(i, i ^ way) for i in range(size)]) for way in ways]


def plan(me, chip_bins):
    near = jnp.concatenate([chip_bins] + from_ways(chip_bins, "rng", N_RNG, NEAR))
    bins = [near] + from_ways(near, "rng", N_RNG, FAR)
    smem, vmem = pl.BlockSpec(memory_space=pltpu.SMEM), pl.BlockSpec(memory_space=pltpu.VMEM)
    return pl.pallas_call(
        plan_kernel,
        in_specs=[smem] * 5,
        out_specs=[vmem] * 3,
        out_shape=[
            jax.ShapeDtypeStruct((len(NETWORK), N_RNG, SIDE), jnp.float32),
            jax.ShapeDtypeStruct((len(NETWORK) + 2, SIDE), jnp.float32),
            jax.ShapeDtypeStruct((CHIPS * HALF, N_RNG, SIDE), jnp.float32),
        ],
        name="plan",
    )(me, *bins)


def range_kernel(
    x_ref, h_ref, swap_ref, w_ref, t1_ref, t2_ref, t3_ref, t4_ref, out1_ref, out2_ref, xs, ys, hs
):
    s = SIDE

    @pl.when(pl.program_id(0) == 0)
    def _():
        for part in range(2):
            for j in range(s):
                ys[j : j + 1, :] = h_ref[part : part + 1, j * s : (j + 1) * s]
            hs[part] = ys[:s, :].T

    for part in range(2):
        for n in range(s):
            row = (part * s + n) * WIDE
            xs[row : row + GROUP, :] = x_ref[0, part, :, n * s : (n + 1) * s].astype(jnp.float32)
    w = (w_ref[0], w_ref[1])
    wc = (w[0], -w[1])
    h = (hs[0], hs[1])
    for line in range(0, GROUP, BATCH):
        batch = range(line, line + BATCH)
        x = [
            jnp.concatenate(
                [bf16(xs[pl.ds(part * s * WIDE + one, s, stride=WIDE), :]) for part in (0, 1)],
                axis=0,
            )
            for one in batch
        ]
        y = dot(t1_ref[...], jnp.concatenate(x, axis=1))
        x = []
        for one in range(BATCH):
            cut = y[:, one * s : (one + 1) * s]
            z = times((cut[:s], cut[s:]), w)
            x.append(jnp.concatenate([bf16(z[0]), bf16(z[1])], axis=1))
        y = dot(jnp.concatenate(x, axis=0), t2_ref[...])
        x = []
        for one in range(BATCH):
            cut = y[one * s : (one + 1) * s]
            z = times((cut[:, :s], cut[:, s:]), h)
            x.append(jnp.concatenate([bf16(z[0]), bf16(z[1])], axis=1))
        y = dot(jnp.concatenate(x, axis=0), t3_ref[...])
        x = []
        for one in range(BATCH):
            cut = y[one * s : (one + 1) * s]
            z = times((cut[:, :s], cut[:, s:]), wc)
            x.append(jnp.concatenate([bf16(z[0]), bf16(z[1])], axis=0))
        y = dot(t4_ref[...], jnp.concatenate(x, axis=1))
        for one in range(BATCH):
            for part in (0, 1):
                row = (part * GROUP + line + one) * LONG
                ys[row : row + s, :] = y[
                    part * s : (part + 1) * s, one * s : (one + 1) * s
                ]
    for dest in range(N_RNG):
        swaps = masks(swap_ref.at[:, dest])
        for part in (0, 1):
            slots = []
            for slot in range(SLOTS):
                row = part * GROUP * LONG + dest * SLOTS + slot
                slots.append(ys[pl.ds(row, GROUP, stride=LONG), :])
            slots = swapped(slots, swaps, NETWORK)
            for slot in range(HALF):
                lanes = slice(slot * s, (slot + 1) * s)
                out1_ref[dest, part, :, lanes] = bf16(slots[slot])
                out2_ref[dest, part, :, lanes] = bf16(slots[slot + HALF])


def whole(shape):
    return pl.BlockSpec(shape, lambda *_: (0,) * len(shape))


def compress_range(raw_echoes, range_filter, swaps):
    forward = dft(SIDE, -1)
    backward = dft(SIDE, 1)
    tables = [
        as_bf16(from_left(forward)),
        as_bf16(from_right(forward)),
        as_bf16(from_right(backward)),
        as_bf16(from_left(backward)),
    ]
    turn = parts_of(twiddles(SIDE, SIDE, -1))
    table = whole((2 * SIDE, 2 * SIDE))
    return pl.pallas_call(
        range_kernel,
        grid=(OWN // GROUP,),
        in_specs=[
            pl.BlockSpec((1, 2, GROUP, BINS), lambda i: (0, 0, i, 0)),
            whole((2, BINS)),
            whole((len(NETWORK), N_RNG, SIDE)),
            whole((2, SIDE, SIDE)),
            table,
            table,
            table,
            table,
        ],
        out_specs=[pl.BlockSpec((N_RNG, 2, GROUP, PART), lambda i: (0, 0, i, 0))] * 2,
        out_shape=[jax.ShapeDtypeStruct((N_RNG, 2, OWN, PART), jnp.bfloat16)] * 2,
        scratch_shapes=[
            pltpu.VMEM((2 * SIDE * WIDE, SIDE), jnp.float32),
            pltpu.VMEM((2 * LONG * GROUP, SIDE), jnp.float32),
            pltpu.VMEM((2, SIDE, SIDE), jnp.float32),
        ],
        compiler_params=pltpu.CompilerParams(vmem_limit_bytes=VMEM),
        name="compress_range",
    )(raw_echoes, range_filter, swaps, turn, *tables)


def add(a, b):
    return (a[0] + b[0], a[1] + b[1])


def sub(a, b):
    return (a[0] - b[0], a[1] - b[1])


def fan_dft(x, sign):
    root = math.sqrt(0.5)

    def quarter(a):
        return (-sign * a[1], sign * a[0]) if sign > 0 else (a[1], -a[0])

    def eighth(a):
        if sign > 0:
            return ((a[0] - a[1]) * root, (a[0] + a[1]) * root)
        return ((a[0] + a[1]) * root, (a[1] - a[0]) * root)

    def four(a, b, c, d):
        e, f, g, h = add(a, c), sub(a, c), add(b, d), quarter(sub(b, d))
        return add(e, g), add(f, h), sub(e, g), sub(f, h)

    even = four(x[0], x[2], x[4], x[6])
    odd = four(x[1], x[3], x[5], x[7])
    odd = (odd[0], eighth(odd[1]), quarter(odd[2]), quarter(eighth(odd[3])))
    return [add(p, q) for p, q in zip(even, odd)] + [sub(p, q) for p, q in zip(even, odd)]


def azimuth_step(r_ref, f_ref, w_ref, t5_ref, t6_ref, spread, mixed, put):
    m = LINES // FAN
    tiles = [(t, slice(lane * 128, (lane + 1) * 128)) for t in range(m // 16) for lane in range(SPAN // 128)]
    for tile, lanes in tiles:
        half, line = divmod(tile * 16, OWN)
        points = []
        for n in range(FAN):
            rows = [slice(part * OWN + line, part * OWN + line + 16) for part in (0, 1)]
            points.append(tuple(r_ref[2 * n + half, row, lanes].astype(jnp.float32) for row in rows))
        for k, value in enumerate(fan_dft(points, -1)):
            if k:
                row = k * m + tile * 16
                value = times(value, (w_ref[0, row : row + 16], w_ref[1, row : row + 16]))
            for part in (0, 1):
                row = (half * 2 + part) * OWN + line
                at = k * SPAN + lanes.start
                spread[row : row + 16, at : at + 128] = bf16(value[part])
    y = dot(t5_ref[...], spread[...])
    x = []
    for k in range(FAN):
        cut = y[:, k * SPAN : (k + 1) * SPAN]
        f = (f_ref[k, 0].astype(jnp.float32), f_ref[k, 1].astype(jnp.float32))
        z = times((cut[:m], cut[m:]), f)
        x.append(jnp.concatenate([bf16(z[0]), bf16(z[1])], axis=0))
    mixed[...] = dot(t6_ref[...], jnp.concatenate(x, axis=1))
    for tile, lanes in tiles:
        points = []
        for k in range(FAN):
            at = k * SPAN + lanes.start
            row = tile * 16
            value = tuple(mixed[part * m + row : part * m + row + 16, at : at + 128] for part in (0, 1))
            if k:
                row += k * m
                value = times(value, (w_ref[0, row : row + 16], -w_ref[1, row : row + 16]))
            points.append(value)
        for p, value in enumerate(fan_dft(points, 1)):
            row = p * m + tile * 16
            for part in (0, 1):
                put(part, row, lanes, bf16(value[part]))


def azimuth_kernel(r_ref, f_ref, w_ref, t5_ref, t6_ref, out_ref, spread, mixed):
    def put(part, row, lanes, value):
        out_ref[part, row : row + 16, lanes] = value

    azimuth_step(r_ref, f_ref, w_ref, t5_ref, t6_ref, spread, mixed, put)


def azimuth_tables():
    m = LINES // FAN
    forward = np.exp(-2j * math.pi * np.outer(np.arange(m), np.arange(m)) / m) / math.sqrt(LINES)
    backward = forward.conj()
    first = from_left(forward).reshape(2 * m, 2, 2, OWN).transpose(0, 2, 1, 3).reshape(2 * m, 2 * m)
    turn = twiddles(FAN, m, -1).reshape(LINES, 1) * np.ones((1, 128))
    return parts_of(turn), as_bf16(first), as_bf16(from_left(backward))


AZIMUTH_SCRATCH = [
    pltpu.VMEM((2 * LINES // FAN, FAN * SPAN), jnp.bfloat16),
    pltpu.VMEM((2 * LINES // FAN, FAN * SPAN), jnp.float32),
]


def focus_azimuth(turned, response):
    m = LINES // FAN
    table = whole((2 * m, 2 * m))
    return pl.pallas_call(
        azimuth_kernel,
        grid=(PART // SPAN,),
        in_specs=[
            pl.BlockSpec((N_RNG, 2 * OWN, SPAN), lambda i: (0, 0, i)),
            pl.BlockSpec((FAN, 2, m, SPAN), lambda i: (0, 0, 0, i)),
            whole((2, LINES, 128)),
            table,
            table,
        ],
        out_specs=pl.BlockSpec((2, LINES, SPAN), lambda i: (0, 0, i)),
        out_shape=jax.ShapeDtypeStruct((2, LINES, PART), jnp.bfloat16),
        scratch_shapes=AZIMUTH_SCRATCH,
        compiler_params=pltpu.CompilerParams(vmem_limit_bytes=VMEM),
        name="focus_azimuth",
    )(turned, response, *azimuth_tables())


def regroup_kernel(f_ref, own_ref, out1_ref, out2_ref, wide):
    swaps = masks(own_ref)
    for part in (0, 1):
        for slot in range(SLOTS):
            wide[slot] = f_ref[part, :, slot * SIDE : (slot + 1) * SIDE].astype(jnp.float32)
        for k in range(FAN):
            slots = [wide[slot, pl.ds(k, 16, stride=FAN), :] for slot in range(SLOTS)]
            slots = swapped(slots, swaps, NETWORK)
            for slot in range(HALF):
                lanes = slice(slot * SIDE, (slot + 1) * SIDE)
                out1_ref[k, part, :, lanes] = bf16(slots[slot])
                out2_ref[k, part, :, lanes] = bf16(slots[slot + HALF])


def regroup_filter(azimuth_filter, own):
    m = LINES // FAN
    return pl.pallas_call(
        regroup_kernel,
        grid=(FAN,),
        in_specs=[
            pl.BlockSpec((2, 16 * FAN, BLOCK), lambda i: (0, i, 0)),
            whole((len(NETWORK) + 2, SIDE)),
        ],
        out_specs=[pl.BlockSpec((FAN, 2, 16, PART), lambda i: (0, 0, i, 0))] * 2,
        out_shape=[jax.ShapeDtypeStruct((FAN, 2, m, PART), jnp.bfloat16)] * 2,
        scratch_shapes=[pltpu.VMEM((SLOTS, 16 * FAN, SIDE), jnp.float32)],
        compiler_params=pltpu.CompilerParams(vmem_limit_bytes=VMEM),
        cost_estimate=pl.CostEstimate(flops=10**7, bytes_accessed=2**23, transcendentals=0),
        name="regroup_filter",
    )(azimuth_filter, own)


MERGE = 256
STEPS = PART // SPAN


def finish_kernel(
    own_ref, r_ref, f_ref, w_ref, t5_ref, t6_ref, a_ref, out_ref, spread, mixed, held
):
    step = pl.program_id(0)

    @pl.when(step < STEPS)
    def _():
        def put(part, row, lanes, value):
            held[step, part, row : row + 16, lanes] = value

        azimuth_step(r_ref, f_ref, w_ref, t5_ref, t6_ref, spread, mixed, put)

    @pl.when(step >= STEPS)
    def _():
        swaps = masks(own_ref)
        first = (step - STEPS) * MERGE
        for part in (0, 1):
            for row in range(0, MERGE, 16):
                rows = slice(row, row + 16)
                slots = [a_ref[part, rows, slot * SIDE : (slot + 1) * SIDE] for slot in range(HALF)]
                for slot in range(HALF):
                    at, lane = divmod(slot * SIDE, SPAN)
                    from_row = pl.ds(pl.multiple_of(first + row, 16), 16)
                    slots.append(held[at, part, from_row, lane : lane + SIDE])
                slots = [slot.astype(jnp.float32) for slot in slots]
                slots = swapped(slots, swaps[::-1], NETWORK[::-1])
                for slot in range(SLOTS):
                    out_ref[0, part, rows, slot * SIDE : (slot + 1) * SIDE] = bf16(slots[slot])


def finish(own, turned, response, image):
    m = LINES // FAN
    table = whole((2 * m, 2 * m))
    return pl.pallas_call(
        finish_kernel,
        grid=(STEPS + LINES // MERGE,),
        in_specs=[
            whole((len(NETWORK) + 2, SIDE)),
            pl.BlockSpec((N_RNG, 2 * OWN, SPAN), lambda i: (0, 0, jnp.minimum(i, STEPS - 1))),
            pl.BlockSpec((FAN, 2, m, SPAN), lambda i: (0, 0, 0, jnp.minimum(i, STEPS - 1))),
            whole((2, LINES, 128)),
            table,
            table,
            pl.BlockSpec((2, MERGE, PART), lambda i: (0, jnp.maximum(i - STEPS, 0), 0)),
        ],
        out_specs=pl.BlockSpec(
            (1, 2, MERGE, BLOCK), lambda i: (0, 0, jnp.maximum(i - STEPS, 0), 0)
        ),
        out_shape=jax.ShapeDtypeStruct((1, 2, LINES, BLOCK), jnp.bfloat16),
        scratch_shapes=AZIMUTH_SCRATCH + [pltpu.VMEM((STEPS, 2, LINES, SPAN), jnp.bfloat16)],
        compiler_params=pltpu.CompilerParams(vmem_limit_bytes=VMEM),
        name="finish",
    )(own, turned, response, *azimuth_tables(), image)


ROWS = WIN + 16


def window_kernel(me_ref, date_ref, lines_ref, bins_ref, pick_ref, image_ref, *refs):
    *outs, slices, held, sems = refs
    me, date = me_ref[0], date_ref[0]
    copies = []
    shifts = []
    for chip in range(CHIPS):
        line = lines_ref[chip]
        row = jnp.minimum(line // 16 * 16, LINES - ROWS)
        copy = pltpu.make_async_copy(
            image_ref.at[:, pl.ds(pl.multiple_of(row, 16), ROWS), :], held.at[chip], sems.at[chip]
        )
        copy.start()
        copies.append(copy)
        shifts.append(lax.rem(ROWS - (line - row), ROWS))
    for chip in range(CHIPS):
        copies[chip].wait()
        picks = [pick_ref[chip * HALF + slot, pl.ds(me, 1), :] > 0.5 for slot in range(HALF)]
        for part in (0, 1):
            cut = held[chip, part, :, :SIDE].astype(jnp.float32)
            for slot in range(1, HALF):
                other = held[chip, part, :, slot * SIDE : (slot + 1) * SIDE].astype(jnp.float32)
                cut = jnp.where(picks[slot], other, cut)
            cut = pltpu.roll(cut, shifts[chip], 0)[:WIN]
            cut = pltpu.roll(cut, lax.rem(WIN - lax.rem(bins_ref[chip], WIN), WIN), 1)
            slices[chip * 2 + part] = bf16(cut)
    for way in range(CHIPS):
        for part in (0, 1):
            outs[way][part] = slices[2 * (way ^ (date // 2)) + part]


def cut_windows(me, date, chip_lines, chip_bins, picks, image):
    smem, vmem = pl.BlockSpec(memory_space=pltpu.SMEM), pl.BlockSpec(memory_space=pltpu.VMEM)
    return pl.pallas_call(
        window_kernel,
        in_specs=[smem] * 4 + [vmem, pl.BlockSpec(memory_space=pl.ANY)],
        out_specs=[vmem] * (CHIPS + 1),
        out_shape=[jax.ShapeDtypeStruct((count, WIN, WIN), jnp.bfloat16) for count in (2, 2, 2, 2, 8)],
        scratch_shapes=[
            pltpu.VMEM((CHIPS, 2, ROWS, PART), jnp.bfloat16),
            pltpu.SemaphoreType.DMA((CHIPS,)),
        ],
        compiler_params=pltpu.CompilerParams(vmem_limit_bytes=VMEM),
        name="cut_windows",
    )(me, date, chip_lines, chip_bins, picks, image)


def pass_kernel(date_ref, mate_ref, *refs):
    ins, outs, (held,) = refs[:DATES], refs[DATES : DATES + CHIPS], refs[DATES + CHIPS :]
    date = date_ref[0]
    for way in range(CHIPS):
        for other in (0, 1):
            held[2 * way + other] = ins[CHIPS * other + way][...]
    for way in range(CHIPS):
        outs[way][...] = held[mate_ref[(2 * way) ^ date] ^ date]


def pass_on(date, partner_date, held):
    smem, vmem = pl.BlockSpec(memory_space=pltpu.SMEM), pl.BlockSpec(memory_space=pltpu.VMEM)
    return pl.pallas_call(
        pass_kernel,
        in_specs=[smem] * 2 + [vmem] * DATES,
        out_specs=[vmem] * CHIPS,
        out_shape=[jax.ShapeDtypeStruct((2, WIN, WIN), jnp.bfloat16)] * CHIPS,
        scratch_shapes=[pltpu.VMEM((DATES, 2, WIN, WIN), jnp.bfloat16)],
        name="pass_on",
    )(date, partner_date, *held)


def along_y(chips):
    return [chips[0]] + [from_ways(chips[way], "date", DATES, (2 * way,))[0] for way in (1, 2, 3)]


def exchange(date, partner_date, chips):
    held = along_y(chips)
    held += [from_ways(chip, "date", DATES, (1,))[0] for chip in held]
    return along_y(pass_on(date, partner_date, held))


def transform(stacked, left, right):
    y = dot(left, jnp.concatenate(stacked, axis=1))
    half = y.shape[0] // 2
    rows = []
    for chip in range(CHIPS):
        cut = y[:, chip * WIN : (chip + 1) * WIN]
        rows.append(jnp.concatenate([bf16(cut[:half]), bf16(cut[half:])], axis=1))
    return dot(jnp.concatenate(rows, axis=0), right)


def correlate_kernel(
    date_ref, offsets_ref, own_ref, left_ref, right_ref, left3_ref, right3_ref, *refs
):
    ins, (out_ref, their_ref) = refs[:CHIPS], refs[CHIPS:]
    for way in range(CHIPS):
        their_ref[way ^ (date_ref[0] // 2)] = ins[way][...]
    left, right = left_ref[...], right_ref[...]
    inside = lax.broadcasted_iota(jnp.int32, (CHIP, WIN), 1) < CHIP
    empty = jnp.zeros((WIN - CHIP, WIN), jnp.bfloat16)
    primary = []
    for chip in range(CHIPS):
        row, col = offsets_ref[chip, 0], offsets_ref[chip, 1]
        pieces = []
        for part in (0, 1):
            cut = own_ref[chip * 2 + part].astype(jnp.float32)
            cut = pltpu.roll(cut, lax.rem(WIN - row, WIN), 0)[:CHIP]
            cut = pltpu.roll(cut, lax.rem(WIN - col, WIN), 1)
            pieces += [bf16(jnp.where(inside, cut, 0.0)), empty]
        primary.append(jnp.concatenate(pieces, axis=0))
    first = transform(primary, left, right)
    second = transform(
        [jnp.concatenate([their_ref[chip, 0], their_ref[chip, 1]], axis=0) for chip in range(CHIPS)],
        left,
        right,
    )
    a = (first[:, :WIN], first[:, WIN:])
    b = (second[:, :WIN], second[:, WIN:])
    product = (a[0] * b[0] + a[1] * b[1], a[1] * b[0] - a[0] * b[1])
    product = [bf16(part) for part in product]
    surface = transform(
        [
            jnp.concatenate([part[chip * WIN : (chip + 1) * WIN] for part in product], axis=0)
            for chip in range(CHIPS)
        ],
        left3_ref[...],
        right3_ref[...],
    )
    for chip in range(CHIPS):
        out_ref[0, chip] = surface[chip * CHIP : (chip + 1) * CHIP]


def correlate(date, offsets, own, theirs):
    table = dft(WIN, -1)
    left, right = from_left(table), from_right(table)
    factor = WIN // CHIP
    keep = np.concatenate([np.arange(CHIP), WIN + np.arange(CHIP)])
    vmem = pl.BlockSpec(memory_space=pltpu.VMEM)
    return pl.pallas_call(
        correlate_kernel,
        in_specs=[pl.BlockSpec(memory_space=pltpu.SMEM)] * 2 + [vmem] * (5 + CHIPS),
        out_specs=vmem,
        out_shape=jax.ShapeDtypeStruct((1, CHIPS, CHIP, 2 * CHIP), jnp.float32),
        scratch_shapes=[pltpu.VMEM((CHIPS, 2, WIN, WIN), jnp.bfloat16)],
        compiler_params=pltpu.CompilerParams(vmem_limit_bytes=VMEM),
        name="correlate",
    )(
        date,
        offsets,
        own,
        as_bf16(left),
        as_bf16(right),
        as_bf16(left[keep]),
        as_bf16(right[:, keep] * factor),
        *theirs,
    )


def local(
    raw_echoes, range_filter, azimuth_filter, partner_date, chip_lines, chip_bins, chip_offsets
):
    me = lax.axis_index("rng").astype(jnp.int32).reshape(1)
    date = lax.axis_index("date").astype(jnp.int32).reshape(1)
    swaps, own, picks = plan(me, chip_bins)
    parts = compress_range(raw_echoes, range_filter, swaps)
    one, two = [part.reshape(N_RNG, 2 * OWN, PART) for part in parts]
    one, own = lax.optimization_barrier((one, own))
    response, response_two = regroup_filter(azimuth_filter, own)
    two, response_two = lax.optimization_barrier((two, response_two))
    one = lax.all_to_all(one, "rng", split_axis=0, concat_axis=0, tiled=True)
    two = lax.all_to_all(two, "rng", split_axis=0, concat_axis=0, tiled=True)
    first = focus_azimuth(one, response)
    *chips, windows = cut_windows(me, date, chip_lines, chip_bins, picks, first)
    theirs = exchange(date, partner_date, chips)
    correlation = correlate(date, chip_offsets, windows, theirs)
    return (finish(own, two, response_two, first), correlation)


def solution(mesh):
    in_specs = (
        P("date", None, "rng", None),
        P(),
        P(None, None, "rng"),
        P(),
        P("rng"),
        P("rng"),
        P("rng", None),
    )
    out_specs = (P("date", None, None, "rng"), P("date", "rng", None, None))
    return jax.shard_map(local, mesh=mesh, in_specs=in_specs, out_specs=out_specs, check_vma=False)
```

```python
import functools
import math

import jax
import jax.numpy as jnp
import ml_dtypes
import numpy as np
from jax import lax
from jax.experimental import pallas as pl
from jax.experimental.pallas import tpu as pltpu
from jax.sharding import PartitionSpec as P

LINES = 1024
BINS = 16384
CHIP = 64
CHIPS = 4
WIN = 128
DATES = 8
N_RNG = 16
SIDE = 128
FAN = 8
BLOCK = BINS // N_RNG
OWN = LINES // N_RNG
SLOTS = 8
EARLY = 16
LATE = OWN - EARLY
GROUP = 16
BATCH = 16
SPAN = 256
WIDE = GROUP + 8
LONG = SIDE + 8
VMEM = 60 * 1024 * 1024


def dft(length, sign):
    phase = np.outer(np.arange(length), np.arange(length)) % length
    return np.exp(sign * 2j * math.pi * phase / length) / math.sqrt(length)


def twiddles(count, other, sign):
    phase = np.outer(np.arange(count), np.arange(other))
    return np.exp(sign * 2j * math.pi * phase / (count * other))


def from_left(table):
    return np.block([[table.real, -table.imag], [table.imag, table.real]])


def from_right(table):
    return np.block([[table.real, table.imag], [-table.imag, table.real]])


def as_bf16(table):
    return jnp.asarray(np.asarray(table, np.float32).astype(ml_dtypes.bfloat16))


def parts_of(table):
    return jnp.asarray(np.stack([table.real, table.imag]).astype(np.float32))


def times(a, b):
    return (a[0] * b[0] - a[1] * b[1], a[0] * b[1] + a[1] * b[0])


def dot(a, b):
    return jnp.dot(a, b, preferred_element_type=jnp.float32)


def bf16(x):
    return x.astype(jnp.bfloat16)


def from_ways(x, axis, size, ways):
    return [lax.ppermute(x, axis, [(i, i ^ way) for i in range(size)]) for way in ways]


def range_kernel(x_ref, h_ref, w_ref, t1_ref, t2_ref, t3_ref, t4_ref, out_ref, xs, ys, hs):
    s = SIDE

    @pl.when(pl.program_id(0) == 0)
    def _():
        for part in range(2):
            for j in range(s):
                ys[j : j + 1, :] = h_ref[part : part + 1, j * s : (j + 1) * s]
            hs[part] = ys[:s, :].T

    for part in range(2):
        for n in range(s):
            row = (part * s + n) * WIDE
            xs[row : row + GROUP, :] = x_ref[0, part, :, n * s : (n + 1) * s].astype(jnp.float32)
    w = (w_ref[0], w_ref[1])
    wc = (w[0], -w[1])
    h = (hs[0], hs[1])
    for line in range(0, GROUP, BATCH):
        batch = range(line, line + BATCH)
        x = [
            jnp.concatenate(
                [bf16(xs[pl.ds(part * s * WIDE + one, s, stride=WIDE), :]) for part in (0, 1)],
                axis=0,
            )
            for one in batch
        ]
        y = dot(t1_ref[...], jnp.concatenate(x, axis=1))
        x = []
        for one in range(BATCH):
            cut = y[:, one * s : (one + 1) * s]
            z = times((cut[:s], cut[s:]), w)
            x.append(jnp.concatenate([bf16(z[0]), bf16(z[1])], axis=1))
        y = dot(jnp.concatenate(x, axis=0), t2_ref[...])
        x = []
        for one in range(BATCH):
            cut = y[one * s : (one + 1) * s]
            z = times((cut[:, :s], cut[:, s:]), h)
            x.append(jnp.concatenate([bf16(z[0]), bf16(z[1])], axis=1))
        y = dot(jnp.concatenate(x, axis=0), t3_ref[...])
        x = []
        for one in range(BATCH):
            cut = y[one * s : (one + 1) * s]
            z = times((cut[:, :s], cut[:, s:]), wc)
            x.append(jnp.concatenate([bf16(z[0]), bf16(z[1])], axis=0))
        y = dot(t4_ref[...], jnp.concatenate(x, axis=1))
        for one in range(BATCH):
            for part in (0, 1):
                row = (part * GROUP + line + one) * LONG
                ys[row : row + s, :] = y[
                    part * s : (part + 1) * s, one * s : (one + 1) * s
                ]
    for dest in range(N_RNG):
        for part in (0, 1):
            for slot in range(SLOTS):
                row = part * GROUP * LONG + dest * SLOTS + slot
                out_ref[dest, part, :, slot * s : (slot + 1) * s] = bf16(
                    ys[pl.ds(row, GROUP, stride=LONG), :]
                )


def whole(shape):
    return pl.BlockSpec(shape, lambda *_: (0,) * len(shape))


def compress_range(raw_echoes, range_filter, first, lines):
    forward = dft(SIDE, -1)
    backward = dft(SIDE, 1)
    tables = [
        as_bf16(from_left(forward)),
        as_bf16(from_right(forward)),
        as_bf16(from_right(backward)),
        as_bf16(from_left(backward)),
    ]
    turn = parts_of(twiddles(SIDE, SIDE, -1))
    table = whole((2 * SIDE, 2 * SIDE))
    out = pl.pallas_call(
        range_kernel,
        grid=(lines // GROUP,),
        in_specs=[
            pl.BlockSpec((1, 2, GROUP, BINS), lambda i: (0, 0, i + first // GROUP, 0)),
            whole((2, BINS)),
            whole((2, SIDE, SIDE)),
            table,
            table,
            table,
            table,
        ],
        out_specs=pl.BlockSpec((N_RNG, 2, GROUP, BLOCK), lambda i: (0, 0, i, 0)),
        out_shape=jax.ShapeDtypeStruct((N_RNG, 2, lines, BLOCK), jnp.bfloat16),
        scratch_shapes=[
            pltpu.VMEM((2 * SIDE * WIDE, SIDE), jnp.float32),
            pltpu.VMEM((2 * LONG * GROUP, SIDE), jnp.float32),
            pltpu.VMEM((2, SIDE, SIDE), jnp.float32),
        ],
        compiler_params=pltpu.CompilerParams(vmem_limit_bytes=VMEM),
        cost_estimate=pl.CostEstimate(flops=4 * 10**9, bytes_accessed=2**22, transcendentals=0),
        name="compress_range",
    )(raw_echoes, range_filter, turn, *tables)
    return out.reshape(N_RNG, 2 * lines, BLOCK)


def to_blocks(x):
    return lax.all_to_all(x, "rng", split_axis=0, concat_axis=0, tiled=True)


def add(a, b):
    return (a[0] + b[0], a[1] + b[1])


def sub(a, b):
    return (a[0] - b[0], a[1] - b[1])


def fan_dft(x, sign):
    root = math.sqrt(0.5)

    def quarter(a):
        return (-sign * a[1], sign * a[0]) if sign > 0 else (a[1], -a[0])

    def eighth(a):
        if sign > 0:
            return ((a[0] - a[1]) * root, (a[0] + a[1]) * root)
        return ((a[0] + a[1]) * root, (a[1] - a[0]) * root)

    def four(a, b, c, d):
        e, f, g, h = add(a, c), sub(a, c), add(b, d), quarter(sub(b, d))
        return add(e, g), add(f, h), sub(e, g), sub(f, h)

    even = four(x[0], x[2], x[4], x[6])
    odd = four(x[1], x[3], x[5], x[7])
    odd = (odd[0], eighth(odd[1]), quarter(odd[2]), quarter(eighth(odd[3])))
    return [add(p, q) for p, q in zip(even, odd)] + [sub(p, q) for p, q in zip(even, odd)]


def azimuth_step(first, early_ref, late_ref, f_ref, w_ref, t5_ref, t6_ref, spread, mixed, out_ref):
    m = LINES // FAN
    tiles = [(t * 16, lane * 128) for t in range(m // 16) for lane in range(SPAN // 128)]
    for tile, lane in tiles:
        lanes = pl.ds(pl.multiple_of(first + lane, 128), 128)
        half, line = divmod(tile, OWN)
        ref, row, lines = (
            (early_ref, line, EARLY) if line < EARLY else (late_ref, line - EARLY, LATE)
        )
        rows = [slice(part * lines + row, part * lines + row + 16) for part in (0, 1)]
        points = []
        for n in range(FAN):
            points.append(
                tuple(ref[2 * n + half, row, lanes].astype(jnp.float32) for row in rows)
            )
        for k, value in enumerate(fan_dft(points, -1)):
            if k:
                row = k * m + tile
                value = times(value, (w_ref[0, row : row + 16], w_ref[1, row : row + 16]))
            for part in (0, 1):
                row = (half * 2 + part) * OWN + line
                at = k * SPAN + lane
                spread[row : row + 16, at : at + 128] = bf16(value[part])
    y = dot(t5_ref[...], spread[...])
    x = []
    lanes = pl.ds(pl.multiple_of(first, 128), SPAN)
    for k in range(FAN):
        cut = y[:, k * SPAN : (k + 1) * SPAN]
        f = tuple(f_ref[k, part, :, lanes].astype(jnp.float32) for part in (0, 1))
        z = times((cut[:m], cut[m:]), f)
        x.append(jnp.concatenate([bf16(z[0]), bf16(z[1])], axis=0))
    mixed[...] = dot(t6_ref[...], jnp.concatenate(x, axis=1))
    for tile, lane in tiles:
        lanes = pl.ds(pl.multiple_of(first + lane, 128), 128)
        points = []
        for k in range(FAN):
            at = k * SPAN + lane
            row = tile
            value = tuple(mixed[part * m + row : part * m + row + 16, at : at + 128] for part in (0, 1))
            if k:
                row += k * m
                value = times(value, (w_ref[0, row : row + 16], -w_ref[1, row : row + 16]))
            points.append(value)
        for p, value in enumerate(fan_dft(points, 1)):
            row = p * m + tile
            for part in (0, 1):
                out_ref[part, row : row + 16, lanes] = bf16(value[part])


def azimuth_tables():
    m = LINES // FAN
    forward = np.exp(-2j * math.pi * np.outer(np.arange(m), np.arange(m)) / m) / math.sqrt(LINES)
    backward = forward.conj()
    first = from_left(forward).reshape(2 * m, 2, 2, OWN).transpose(0, 2, 1, 3).reshape(2 * m, 2 * m)
    turn = twiddles(FAN, m, -1).reshape(LINES, 1) * np.ones((1, 128))
    return parts_of(turn), as_bf16(first), as_bf16(from_left(backward))


ROWS = WIN + 16
COLS = 2 * WIN
SPANS = BLOCK // SPAN


def azimuth_kernel(
    date_ref, lines_ref, bins_ref, w_ref, t5_ref, t6_ref, f_ref, early_ref, late_ref, *refs
):
    image_ref, *outs, slices, early, late, response, image, spread, mixed, sems = refs
    date = date_ref[0]

    def span_of(ref, i):
        return ref.at[..., pl.ds(pl.multiple_of(i * SPAN, SPAN), SPAN)]

    def fetches(i):
        return [
            pltpu.make_async_copy(span_of(source, i), span_of(target, i), sems.at[at, i])
            for at, (source, target) in enumerate(
                ((early_ref, early), (late_ref, late), (f_ref, response))
            )
        ]

    def store(i):
        return pltpu.make_async_copy(span_of(image, i), span_of(image_ref.at[0], i), sems.at[3, i])

    for i in range(SPANS):
        for copy in fetches(i):
            copy.start()

    def body(i, _):
        for copy in fetches(i):
            copy.wait()
        azimuth_step(
            i * SPAN, early, late, response, w_ref, t5_ref, t6_ref, spread, mixed, image
        )
        store(i).start()
        return 0

    lax.fori_loop(0, SPANS, body, 0)

    for chip in range(CHIPS):
        line, at_bin = lines_ref[chip], bins_ref[chip]
        row = jnp.minimum(line // 16 * 16, LINES - ROWS)
        col = jnp.minimum(at_bin // WIN * WIN, BLOCK - COLS)
        for part in (0, 1):
            cut = image[part, pl.ds(pl.multiple_of(row, 16), ROWS), pl.ds(pl.multiple_of(col, WIN), COLS)]
            cut = pltpu.roll(cut.astype(jnp.float32), lax.rem(ROWS - (line - row), ROWS), 0)[:WIN]
            cut = pltpu.roll(cut, lax.rem(COLS - (at_bin - col), COLS), 1)
            slices[chip * 2 + part] = bf16(cut[:, :WIN])
    for way in range(CHIPS):
        for part in (0, 1):
            outs[way][part] = slices[2 * (way ^ (date // 2)) + part]
    for i in range(SPANS):
        store(i).wait()


def focus_azimuth(date, chip_lines, chip_bins, early, late, response):
    m = LINES // FAN
    smem, vmem = pl.BlockSpec(memory_space=pltpu.SMEM), pl.BlockSpec(memory_space=pltpu.VMEM)
    anywhere = pl.BlockSpec(memory_space=pl.ANY)
    return pl.pallas_call(
        azimuth_kernel,
        in_specs=[smem] * 3 + [vmem] * 3 + [anywhere] * 3,
        out_specs=[anywhere] + [vmem] * (CHIPS + 1),
        out_shape=[jax.ShapeDtypeStruct((1, 2, LINES, BLOCK), jnp.bfloat16)]
        + [jax.ShapeDtypeStruct((count, WIN, WIN), jnp.bfloat16) for count in (2, 2, 2, 2, 8)],
        scratch_shapes=[
            pltpu.VMEM((N_RNG, 2 * EARLY, BLOCK), jnp.bfloat16),
            pltpu.VMEM((N_RNG, 2 * LATE, BLOCK), jnp.bfloat16),
            pltpu.VMEM((FAN, 2, m, BLOCK), jnp.bfloat16),
            pltpu.VMEM((2, LINES, BLOCK), jnp.bfloat16),
            pltpu.VMEM((2 * m, FAN * SPAN), jnp.bfloat16),
            pltpu.VMEM((2 * m, FAN * SPAN), jnp.float32),
            pltpu.SemaphoreType.DMA((4, SPANS)),
        ],
        compiler_params=pltpu.CompilerParams(vmem_limit_bytes=VMEM),
        name="focus_azimuth",
    )(date, chip_lines, chip_bins, *azimuth_tables(), response, early, late)


def regroup_kernel(f_ref, out_ref, wide):
    m = LINES // FAN
    for part in (0, 1):
        wide[...] = f_ref[part].astype(jnp.float32)
        for k in range(FAN):
            out_ref[k, part] = bf16(wide[pl.ds(k, m, stride=FAN), :])


def regroup_filter(azimuth_filter):
    m = LINES // FAN
    return pl.pallas_call(
        regroup_kernel,
        grid=(BLOCK // 128,),
        in_specs=[pl.BlockSpec((2, LINES, 128), lambda i: (0, 0, i))],
        out_specs=pl.BlockSpec((FAN, 2, m, 128), lambda i: (0, 0, 0, i)),
        out_shape=jax.ShapeDtypeStruct((FAN, 2, m, BLOCK), jnp.bfloat16),
        scratch_shapes=[pltpu.VMEM((LINES, 128), jnp.float32)],
        compiler_params=pltpu.CompilerParams(vmem_limit_bytes=VMEM),
        cost_estimate=pl.CostEstimate(flops=10**7, bytes_accessed=2**23, transcendentals=0),
        name="regroup_filter",
    )(azimuth_filter)


def pass_kernel(date_ref, mate_ref, *refs):
    ins, outs, (held,) = refs[:DATES], refs[DATES : DATES + CHIPS], refs[DATES + CHIPS :]
    date = date_ref[0]
    for way in range(CHIPS):
        for other in (0, 1):
            held[2 * way + other] = ins[CHIPS * other + way][...]
    for way in range(CHIPS):
        outs[way][...] = held[mate_ref[(2 * way) ^ date] ^ date]


def pass_on(date, partner_date, held):
    smem, vmem = pl.BlockSpec(memory_space=pltpu.SMEM), pl.BlockSpec(memory_space=pltpu.VMEM)
    return pl.pallas_call(
        pass_kernel,
        in_specs=[smem] * 2 + [vmem] * DATES,
        out_specs=[vmem] * CHIPS,
        out_shape=[jax.ShapeDtypeStruct((2, WIN, WIN), jnp.bfloat16)] * CHIPS,
        scratch_shapes=[pltpu.VMEM((DATES, 2, WIN, WIN), jnp.bfloat16)],
        name="pass_on",
    )(date, partner_date, *held)


def along_y(chips):
    return [chips[0]] + [from_ways(chips[way], "date", DATES, (2 * way,))[0] for way in (1, 2, 3)]


def exchange(date, partner_date, chips):
    held = along_y(chips)
    held += [from_ways(chip, "date", DATES, (1,))[0] for chip in held]
    return along_y(pass_on(date, partner_date, held))


def transform(stacked, left, right):
    y = dot(left, jnp.concatenate(stacked, axis=1))
    half = y.shape[0] // 2
    rows = []
    for chip in range(CHIPS):
        cut = y[:, chip * WIN : (chip + 1) * WIN]
        rows.append(jnp.concatenate([bf16(cut[:half]), bf16(cut[half:])], axis=1))
    return dot(jnp.concatenate(rows, axis=0), right)


def correlate_kernel(
    date_ref, offsets_ref, own_ref, left_ref, right_ref, left3_ref, right3_ref, *refs
):
    ins, (out_ref, their_ref) = refs[:CHIPS], refs[CHIPS:]
    for way in range(CHIPS):
        their_ref[way ^ (date_ref[0] // 2)] = ins[way][...]
    left, right = left_ref[...], right_ref[...]
    inside = lax.broadcasted_iota(jnp.int32, (CHIP, WIN), 1) < CHIP
    empty = jnp.zeros((WIN - CHIP, WIN), jnp.bfloat16)
    primary = []
    for chip in range(CHIPS):
        row, col = offsets_ref[chip, 0], offsets_ref[chip, 1]
        pieces = []
        for part in (0, 1):
            cut = own_ref[chip * 2 + part].astype(jnp.float32)
            cut = pltpu.roll(cut, lax.rem(WIN - row, WIN), 0)[:CHIP]
            cut = pltpu.roll(cut, lax.rem(WIN - col, WIN), 1)
            pieces += [bf16(jnp.where(inside, cut, 0.0)), empty]
        primary.append(jnp.concatenate(pieces, axis=0))
    first = transform(primary, left, right)
    second = transform(
        [jnp.concatenate([their_ref[chip, 0], their_ref[chip, 1]], axis=0) for chip in range(CHIPS)],
        left,
        right,
    )
    a = (first[:, :WIN], first[:, WIN:])
    b = (second[:, :WIN], second[:, WIN:])
    product = (a[0] * b[0] + a[1] * b[1], a[1] * b[0] - a[0] * b[1])
    product = [bf16(part) for part in product]
    surface = transform(
        [
            jnp.concatenate([part[chip * WIN : (chip + 1) * WIN] for part in product], axis=0)
            for chip in range(CHIPS)
        ],
        left3_ref[...],
        right3_ref[...],
    )
    for chip in range(CHIPS):
        out_ref[0, chip] = surface[chip * CHIP : (chip + 1) * CHIP]


def correlate(date, offsets, own, theirs):
    table = dft(WIN, -1)
    left, right = from_left(table), from_right(table)
    factor = WIN // CHIP
    keep = np.concatenate([np.arange(CHIP), WIN + np.arange(CHIP)])
    vmem = pl.BlockSpec(memory_space=pltpu.VMEM)
    return pl.pallas_call(
        correlate_kernel,
        in_specs=[pl.BlockSpec(memory_space=pltpu.SMEM)] * 2 + [vmem] * (5 + CHIPS),
        out_specs=vmem,
        out_shape=jax.ShapeDtypeStruct((1, CHIPS, CHIP, 2 * CHIP), jnp.float32),
        scratch_shapes=[pltpu.VMEM((CHIPS, 2, WIN, WIN), jnp.bfloat16)],
        compiler_params=pltpu.CompilerParams(vmem_limit_bytes=VMEM),
        name="correlate",
    )(
        date,
        offsets,
        own,
        as_bf16(left),
        as_bf16(right),
        as_bf16(left[keep]),
        as_bf16(right[:, keep] * factor),
        *theirs,
    )


def local(
    raw_echoes, range_filter, azimuth_filter, partner_date, chip_lines, chip_bins, chip_offsets
):
    date = lax.axis_index("date").astype(jnp.int32).reshape(1)
    early = to_blocks(compress_range(raw_echoes, range_filter, 0, EARLY))
    late = compress_range(raw_echoes, range_filter, EARLY, LATE)
    late, response = lax.optimization_barrier((late, regroup_filter(azimuth_filter)))
    image, *chips, windows = focus_azimuth(
        date, chip_lines, chip_bins, early, to_blocks(late), response
    )
    theirs = exchange(date, partner_date, chips)
    correlation = correlate(date, chip_offsets, windows, theirs)
    return (image, correlation)


def solution(mesh):
    in_specs = (
        P("date", None, "rng", None),
        P(),
        P(None, None, "rng"),
        P(),
        P("rng"),
        P("rng"),
        P("rng", None),
    )
    out_specs = (P("date", None, None, "rng"), P("date", "rng", None, None))
    return jax.shard_map(local, mesh=mesh, in_specs=in_specs, out_specs=out_specs, check_vma=False)
```

```python
import functools
import math

import jax
import jax.numpy as jnp
import ml_dtypes
import numpy as np
from jax import lax
from jax.experimental import pallas as pl
from jax.experimental.pallas import tpu as pltpu
from jax.sharding import PartitionSpec as P

LINES = 1024
BINS = 16384
CHIP = 64
CHIPS = 4
WIN = 128
DATES = 8
N_RNG = 16
SIDE = 128
FAN = 8
BLOCK = BINS // N_RNG
OWN = LINES // N_RNG
SLOTS = 8
HALF = 4
PART = HALF * 128
SORT = ((0, 1), (2, 3), (0, 2), (1, 3), (1, 2))
NETWORK = SORT + tuple((i + 4, j + 4) for i, j in SORT) + ((0, 7), (1, 6), (2, 5), (3, 4))
EARLY = 16
LATE = OWN - EARLY
ORDER = 4
GROUP = 16
BATCH = 16
SPAN = 256
WIDE = GROUP + 8
LONG = SIDE + 8
VMEM = 56 * 1024 * 1024


def dft(length, sign):
    phase = np.outer(np.arange(length), np.arange(length)) % length
    return np.exp(sign * 2j * math.pi * phase / length) / math.sqrt(length)


def twiddles(count, other, sign):
    phase = np.outer(np.arange(count), np.arange(other))
    return np.exp(sign * 2j * math.pi * phase / (count * other))


def from_left(table):
    return np.block([[table.real, -table.imag], [table.imag, table.real]])


def from_right(table):
    return np.block([[table.real, table.imag], [-table.imag, table.real]])


def as_bf16(table):
    return jnp.asarray(np.asarray(table, np.float32).astype(ml_dtypes.bfloat16))


def parts_of(table):
    return jnp.asarray(np.stack([table.real, table.imag]).astype(np.float32))


def times(a, b):
    return (a[0] * b[0] - a[1] * b[1], a[0] * b[1] + a[1] * b[0])


def dot(a, b):
    return jnp.dot(a, b, preferred_element_type=jnp.float32)


def bf16(x):
    return x.astype(jnp.bfloat16)


def swapped(slots, swaps, pairs):
    slots = list(slots)
    for swap, (i, j) in zip(swaps, pairs):
        slots[i], slots[j] = (
            jnp.where(swap, slots[j], slots[i]),
            jnp.where(swap, slots[i], slots[j]),
        )
    return slots


def masks(ref):
    return [jnp.broadcast_to(ref[at : at + 1, :], (16, SIDE)) > 0.5 for at in range(len(NETWORK))]


def plan_kernel(me_ref, near_ref, *refs):
    far_refs, (swap_ref, own_ref, pick_ref) = refs[:3], refs[3:]
    me = me_ref[0]
    lane = lax.broadcasted_iota(jnp.int32, (N_RNG, SIDE), 1)
    device = lax.broadcasted_iota(jnp.int32, (N_RNG, SIDE), 0)
    runs = []
    for chip in range(CHIPS):
        first = jnp.zeros((N_RNG, SIDE), jnp.int32)
        for far, ref in zip((0, *FAR), (near_ref, *far_refs)):
            for at, near in enumerate((0, *NEAR)):
                first = jnp.where(device == (me ^ far ^ near), ref[at * CHIPS + chip], first)
        runs.append(first // SIDE + jnp.where(lane < first % SIDE, 1, 0))
    holds = [[jnp.where(run == slot, 1.0, 0.0) for slot in range(SLOTS)] for run in runs]
    wanted = [functools.reduce(jnp.maximum, [hold[slot] for hold in holds]) for slot in range(SLOTS)]
    for at, (i, j) in enumerate(NETWORK):
        swap = wanted[j] > wanted[i]
        swap_ref[at] = jnp.where(swap, 1.0, 0.0)
        wanted = swapped(wanted, [swap], [(i, j)])
        holds = [swapped(hold, [swap], [(i, j)]) for hold in holds]
    for at in range(len(NETWORK)):
        own_ref[at : at + 1, :] = swap_ref[at, pl.ds(me, 1), :]
    for chip in range(CHIPS):
        for slot in range(HALF):
            at = chip * HALF + slot
            pick_ref[at] = holds[chip][slot]


NEAR = (1, 8, 9)
FAR = (2, 4, 6)


def from_ways(x, axis, size, ways):
    return [lax.ppermute(x, axis, [(i, i ^ way) for i in range(size)]) for way in ways]


def all_bins(chip_bins):
    near = jnp.concatenate([chip_bins] + from_ways(chip_bins, "rng", N_RNG, NEAR))
    return [near] + from_ways(near, "rng", N_RNG, FAR)


def plan(me, bins):
    smem, vmem = pl.BlockSpec(memory_space=pltpu.SMEM), pl.BlockSpec(memory_space=pltpu.VMEM)
    return pl.pallas_call(
        plan_kernel,
        in_specs=[smem] * 5,
        out_specs=[vmem] * 3,
        out_shape=[
            jax.ShapeDtypeStruct((len(NETWORK), N_RNG, SIDE), jnp.float32),
            jax.ShapeDtypeStruct((len(NETWORK) + 2, SIDE), jnp.float32),
            jax.ShapeDtypeStruct((CHIPS * HALF, N_RNG, SIDE), jnp.float32),
        ],
        name="plan",
    )(me, *bins)


def range_kernel(x_ref, h_ref, w_ref, t1_ref, t2_ref, t3_ref, t4_ref, *refs, ordered):
    s = SIDE
    *refs, xs, ys, hs = refs

    @pl.when(pl.program_id(0) == 0)
    def _():
        for part in range(2):
            for j in range(s):
                ys[j : j + 1, :] = h_ref[part : part + 1, j * s : (j + 1) * s]
            hs[part] = ys[:s, :].T

    for part in range(2):
        for n in range(s):
            row = (part * s + n) * WIDE
            xs[row : row + GROUP, :] = x_ref[0, part, :, n * s : (n + 1) * s].astype(jnp.float32)
    w = (w_ref[0], w_ref[1])
    wc = (w[0], -w[1])
    h = (hs[0], hs[1])
    for line in range(0, GROUP, BATCH):
        batch = range(line, line + BATCH)
        x = [
            jnp.concatenate(
                [bf16(xs[pl.ds(part * s * WIDE + one, s, stride=WIDE), :]) for part in (0, 1)],
                axis=0,
            )
            for one in batch
        ]
        y = dot(t1_ref[...], jnp.concatenate(x, axis=1))
        x = []
        for one in range(BATCH):
            cut = y[:, one * s : (one + 1) * s]
            z = times((cut[:s], cut[s:]), w)
            x.append(jnp.concatenate([bf16(z[0]), bf16(z[1])], axis=1))
        y = dot(jnp.concatenate(x, axis=0), t2_ref[...])
        x = []
        for one in range(BATCH):
            cut = y[one * s : (one + 1) * s]
            z = times((cut[:, :s], cut[:, s:]), h)
            x.append(jnp.concatenate([bf16(z[0]), bf16(z[1])], axis=1))
        y = dot(jnp.concatenate(x, axis=0), t3_ref[...])
        x = []
        for one in range(BATCH):
            cut = y[one * s : (one + 1) * s]
            z = times((cut[:, :s], cut[:, s:]), wc)
            x.append(jnp.concatenate([bf16(z[0]), bf16(z[1])], axis=0))
        y = dot(t4_ref[...], jnp.concatenate(x, axis=1))
        for one in range(BATCH):
            for part in (0, 1):
                row = (part * GROUP + line + one) * LONG
                ys[row : row + s, :] = y[
                    part * s : (part + 1) * s, one * s : (one + 1) * s
                ]
    for dest in range(N_RNG):
        if ordered:
            swap_ref, out1_ref, out2_ref = refs
            swaps = masks(swap_ref.at[:, dest])
        else:
            (out_ref,) = refs
        for part in (0, 1):
            slots = []
            for slot in range(SLOTS):
                row = part * GROUP * LONG + dest * SLOTS + slot
                slots.append(ys[pl.ds(row, GROUP, stride=LONG), :])
            if not ordered:
                for slot in range(SLOTS):
                    out_ref[dest, part, :, slot * s : (slot + 1) * s] = bf16(slots[slot])
                continue
            slots = swapped(slots, swaps, NETWORK)
            for slot in range(HALF):
                lanes = slice(slot * s, (slot + 1) * s)
                out1_ref[dest, part, :, lanes] = bf16(slots[slot])
                out2_ref[dest, part, :, lanes] = bf16(slots[slot + HALF])


def whole(shape):
    return pl.BlockSpec(shape, lambda *_: (0,) * len(shape))


def compress_range(raw_echoes, range_filter, first, lines, swaps=None):
    forward = dft(SIDE, -1)
    backward = dft(SIDE, 1)
    tables = [
        as_bf16(from_left(forward)),
        as_bf16(from_right(forward)),
        as_bf16(from_right(backward)),
        as_bf16(from_left(backward)),
    ]
    turn = parts_of(twiddles(SIDE, SIDE, -1))
    table = whole((2 * SIDE, 2 * SIDE))
    ordered = swaps is not None
    width, count = (PART, 2) if ordered else (BLOCK, 1)
    outs = pl.pallas_call(
        functools.partial(range_kernel, ordered=ordered),
        grid=(lines // GROUP,),
        in_specs=[
            pl.BlockSpec((1, 2, GROUP, BINS), lambda i: (0, 0, i + first // GROUP, 0)),
            whole((2, BINS)),
            whole((2, SIDE, SIDE)),
            table,
            table,
            table,
            table,
        ]
        + [whole((len(NETWORK), N_RNG, SIDE))] * ordered,
        out_specs=[pl.BlockSpec((N_RNG, 2, GROUP, width), lambda i: (0, 0, i, 0))] * count,
        out_shape=[jax.ShapeDtypeStruct((N_RNG, 2, lines, width), jnp.bfloat16)] * count,
        scratch_shapes=[
            pltpu.VMEM((2 * SIDE * WIDE, SIDE), jnp.float32),
            pltpu.VMEM((2 * LONG * GROUP, SIDE), jnp.float32),
            pltpu.VMEM((2, SIDE, SIDE), jnp.float32),
        ],
        compiler_params=pltpu.CompilerParams(vmem_limit_bytes=VMEM),
        cost_estimate=pl.CostEstimate(flops=4 * 10**9, bytes_accessed=2**22, transcendentals=0),
        name="compress_range",
    )(raw_echoes, range_filter, turn, *tables, *([swaps] * ordered))
    return [out.reshape(N_RNG, 2 * lines, width) for out in outs]


def order_kernel(own_ref, x_ref, out1_ref, out2_ref):
    swaps = masks(own_ref)
    for device in range(ORDER):
        for row in range(0, 2 * EARLY, 16):
            rows = slice(row, row + 16)
            slots = [
                x_ref[device, rows, slot * SIDE : (slot + 1) * SIDE].astype(jnp.float32)
                for slot in range(SLOTS)
            ]
            slots = swapped(slots, swaps, NETWORK)
            for slot in range(HALF):
                lanes = slice(slot * SIDE, (slot + 1) * SIDE)
                out1_ref[device, rows, lanes] = bf16(slots[slot])
                out2_ref[device, rows, lanes] = bf16(slots[slot + HALF])


def order_bins(own, x):
    return pl.pallas_call(
        order_kernel,
        grid=(N_RNG // ORDER,),
        in_specs=[
            whole((len(NETWORK) + 2, SIDE)),
            pl.BlockSpec((ORDER, 2 * EARLY, BLOCK), lambda i: (i, 0, 0)),
        ],
        out_specs=[pl.BlockSpec((ORDER, 2 * EARLY, PART), lambda i: (i, 0, 0))] * 2,
        out_shape=[jax.ShapeDtypeStruct((N_RNG, 2 * EARLY, PART), jnp.bfloat16)] * 2,
        compiler_params=pltpu.CompilerParams(vmem_limit_bytes=VMEM),
        cost_estimate=pl.CostEstimate(flops=10**7, bytes_accessed=2**22, transcendentals=0),
        name="order_bins",
    )(own, x)


def add(a, b):
    return (a[0] + b[0], a[1] + b[1])


def sub(a, b):
    return (a[0] - b[0], a[1] - b[1])


def fan_dft(x, sign):
    root = math.sqrt(0.5)

    def quarter(a):
        return (-sign * a[1], sign * a[0]) if sign > 0 else (a[1], -a[0])

    def eighth(a):
        if sign > 0:
            return ((a[0] - a[1]) * root, (a[0] + a[1]) * root)
        return ((a[0] + a[1]) * root, (a[1] - a[0]) * root)

    def four(a, b, c, d):
        e, f, g, h = add(a, c), sub(a, c), add(b, d), quarter(sub(b, d))
        return add(e, g), add(f, h), sub(e, g), sub(f, h)

    even = four(x[0], x[2], x[4], x[6])
    odd = four(x[1], x[3], x[5], x[7])
    odd = (odd[0], eighth(odd[1]), quarter(odd[2]), quarter(eighth(odd[3])))
    return [add(p, q) for p, q in zip(even, odd)] + [sub(p, q) for p, q in zip(even, odd)]


def azimuth_step(a_ref, b_ref, f_ref, w_ref, t5_ref, t6_ref, spread, mixed, put):
    m = LINES // FAN
    tiles = [(t, slice(lane * 128, (lane + 1) * 128)) for t in range(m // 16) for lane in range(SPAN // 128)]
    for tile, lanes in tiles:
        half, line = divmod(tile * 16, OWN)
        points = []
        for n in range(FAN):
            ref, row, lines = (a_ref, line, EARLY) if line < EARLY else (b_ref, line - EARLY, LATE)
            rows = [slice(part * lines + row, part * lines + row + 16) for part in (0, 1)]
            points.append(tuple(ref[2 * n + half, row, lanes].astype(jnp.float32) for row in rows))
        for k, value in enumerate(fan_dft(points, -1)):
            if k:
                row = k * m + tile * 16
                value = times(value, (w_ref[0, row : row + 16], w_ref[1, row : row + 16]))
            for part in (0, 1):
                row = (half * 2 + part) * OWN + line
                at = k * SPAN + lanes.start
                spread[row : row + 16, at : at + 128] = bf16(value[part])
    y = dot(t5_ref[...], spread[...])
    x = []
    for k in range(FAN):
        cut = y[:, k * SPAN : (k + 1) * SPAN]
        f = (f_ref[k, 0].astype(jnp.float32), f_ref[k, 1].astype(jnp.float32))
        z = times((cut[:m], cut[m:]), f)
        x.append(jnp.concatenate([bf16(z[0]), bf16(z[1])], axis=0))
    mixed[...] = dot(t6_ref[...], jnp.concatenate(x, axis=1))
    for tile, lanes in tiles:
        points = []
        for k in range(FAN):
            at = k * SPAN + lanes.start
            row = tile * 16
            value = tuple(mixed[part * m + row : part * m + row + 16, at : at + 128] for part in (0, 1))
            if k:
                row += k * m
                value = times(value, (w_ref[0, row : row + 16], -w_ref[1, row : row + 16]))
            points.append(value)
        for p, value in enumerate(fan_dft(points, 1)):
            row = p * m + tile * 16
            for part in (0, 1):
                put(part, row, lanes, bf16(value[part]))


def azimuth_kernel(a_ref, b_ref, f_ref, w_ref, t5_ref, t6_ref, out_ref, spread, mixed):
    def put(part, row, lanes, value):
        out_ref[part, row : row + 16, lanes] = value

    azimuth_step(a_ref, b_ref, f_ref, w_ref, t5_ref, t6_ref, spread, mixed, put)


def azimuth_tables():
    m = LINES // FAN
    forward = np.exp(-2j * math.pi * np.outer(np.arange(m), np.arange(m)) / m) / math.sqrt(LINES)
    backward = forward.conj()
    first = from_left(forward).reshape(2 * m, 2, 2, OWN).transpose(0, 2, 1, 3).reshape(2 * m, 2 * m)
    turn = twiddles(FAN, m, -1).reshape(LINES, 1) * np.ones((1, 128))
    return parts_of(turn), as_bf16(first), as_bf16(from_left(backward))


AZIMUTH_SCRATCH = [
    pltpu.VMEM((2 * LINES // FAN, FAN * SPAN), jnp.bfloat16),
    pltpu.VMEM((2 * LINES // FAN, FAN * SPAN), jnp.float32),
]


def focus_azimuth(early, late, response):
    m = LINES // FAN
    table = whole((2 * m, 2 * m))
    return pl.pallas_call(
        azimuth_kernel,
        grid=(PART // SPAN,),
        in_specs=[
            pl.BlockSpec((N_RNG, 2 * EARLY, SPAN), lambda i: (0, 0, i)),
            pl.BlockSpec((N_RNG, 2 * LATE, SPAN), lambda i: (0, 0, i)),
            pl.BlockSpec((FAN, 2, m, SPAN), lambda i: (0, 0, 0, i)),
            whole((2, LINES, 128)),
            table,
            table,
        ],
        out_specs=pl.BlockSpec((2, LINES, SPAN), lambda i: (0, 0, i)),
        out_shape=jax.ShapeDtypeStruct((2, LINES, PART), jnp.bfloat16),
        scratch_shapes=AZIMUTH_SCRATCH,
        compiler_params=pltpu.CompilerParams(vmem_limit_bytes=VMEM),
        name="focus_azimuth",
    )(early, late, response, *azimuth_tables())


def regroup_kernel(f_ref, own_ref, out1_ref, out2_ref, wide):
    swaps = masks(own_ref)
    for part in (0, 1):
        for slot in range(SLOTS):
            wide[slot] = f_ref[part, :, slot * SIDE : (slot + 1) * SIDE].astype(jnp.float32)
        for k in range(FAN):
            slots = [wide[slot, pl.ds(k, 16, stride=FAN), :] for slot in range(SLOTS)]
            slots = swapped(slots, swaps, NETWORK)
            for slot in range(HALF):
                lanes = slice(slot * SIDE, (slot + 1) * SIDE)
                out1_ref[k, part, :, lanes] = bf16(slots[slot])
                out2_ref[k, part, :, lanes] = bf16(slots[slot + HALF])


def regroup_filter(azimuth_filter, own):
    m = LINES // FAN
    return pl.pallas_call(
        regroup_kernel,
        grid=(FAN,),
        in_specs=[
            pl.BlockSpec((2, 16 * FAN, BLOCK), lambda i: (0, i, 0)),
            whole((len(NETWORK) + 2, SIDE)),
        ],
        out_specs=[pl.BlockSpec((FAN, 2, 16, PART), lambda i: (0, 0, i, 0))] * 2,
        out_shape=[jax.ShapeDtypeStruct((FAN, 2, m, PART), jnp.bfloat16)] * 2,
        scratch_shapes=[pltpu.VMEM((SLOTS, 16 * FAN, SIDE), jnp.float32)],
        compiler_params=pltpu.CompilerParams(vmem_limit_bytes=VMEM),
        cost_estimate=pl.CostEstimate(flops=10**7, bytes_accessed=2**23, transcendentals=0),
        name="regroup_filter",
    )(azimuth_filter, own)


MERGE = 256
STEPS = PART // SPAN


def finish_kernel(
    own_ref, a_ref, b_ref, f_ref, w_ref, t5_ref, t6_ref, first_ref, out_ref, spread, mixed, held
):
    step = pl.program_id(0)

    @pl.when(step < STEPS)
    def _():
        def put(part, row, lanes, value):
            held[step, part, row : row + 16, lanes] = value

        azimuth_step(a_ref, b_ref, f_ref, w_ref, t5_ref, t6_ref, spread, mixed, put)

    @pl.when(step >= STEPS)
    def _():
        swaps = masks(own_ref)
        first = (step - STEPS) * MERGE
        for part in (0, 1):
            for row in range(0, MERGE, 16):
                rows = slice(row, row + 16)
                slots = [
                    first_ref[part, rows, slot * SIDE : (slot + 1) * SIDE] for slot in range(HALF)
                ]
                for slot in range(HALF):
                    at, lane = divmod(slot * SIDE, SPAN)
                    from_row = pl.ds(pl.multiple_of(first + row, 16), 16)
                    slots.append(held[at, part, from_row, lane : lane + SIDE])
                slots = [slot.astype(jnp.float32) for slot in slots]
                slots = swapped(slots, swaps[::-1], NETWORK[::-1])
                for slot in range(SLOTS):
                    out_ref[0, part, rows, slot * SIDE : (slot + 1) * SIDE] = bf16(slots[slot])


def finish(own, early, late, response, image):
    m = LINES // FAN
    table = whole((2 * m, 2 * m))
    return pl.pallas_call(
        finish_kernel,
        grid=(STEPS + LINES // MERGE,),
        in_specs=[
            whole((len(NETWORK) + 2, SIDE)),
            pl.BlockSpec((N_RNG, 2 * EARLY, SPAN), lambda i: (0, 0, jnp.minimum(i, STEPS - 1))),
            pl.BlockSpec((N_RNG, 2 * LATE, SPAN), lambda i: (0, 0, jnp.minimum(i, STEPS - 1))),
            pl.BlockSpec((FAN, 2, m, SPAN), lambda i: (0, 0, 0, jnp.minimum(i, STEPS - 1))),
            whole((2, LINES, 128)),
            table,
            table,
            pl.BlockSpec((2, MERGE, PART), lambda i: (0, jnp.maximum(i - STEPS, 0), 0)),
        ],
        out_specs=pl.BlockSpec(
            (1, 2, MERGE, BLOCK), lambda i: (0, 0, jnp.maximum(i - STEPS, 0), 0)
        ),
        out_shape=jax.ShapeDtypeStruct((1, 2, LINES, BLOCK), jnp.bfloat16),
        scratch_shapes=AZIMUTH_SCRATCH + [pltpu.VMEM((STEPS, 2, LINES, SPAN), jnp.bfloat16)],
        compiler_params=pltpu.CompilerParams(vmem_limit_bytes=VMEM),
        name="finish",
    )(own, early, late, response, *azimuth_tables(), image)


ROWS = WIN + 16


def window_kernel(me_ref, date_ref, lines_ref, bins_ref, pick_ref, image_ref, *refs):
    *outs, slices, held, sems = refs
    me, date = me_ref[0], date_ref[0]
    copies = []
    shifts = []
    for chip in range(CHIPS):
        line = lines_ref[chip]
        row = jnp.minimum(line // 16 * 16, LINES - ROWS)
        copy = pltpu.make_async_copy(
            image_ref.at[:, pl.ds(pl.multiple_of(row, 16), ROWS), :], held.at[chip], sems.at[chip]
        )
        copy.start()
        copies.append(copy)
        shifts.append(lax.rem(ROWS - (line - row), ROWS))
    for chip in range(CHIPS):
        copies[chip].wait()
        picks = [pick_ref[chip * HALF + slot, pl.ds(me, 1), :] > 0.5 for slot in range(HALF)]
        for part in (0, 1):
            cut = held[chip, part, :, :SIDE].astype(jnp.float32)
            for slot in range(1, HALF):
                other = held[chip, part, :, slot * SIDE : (slot + 1) * SIDE].astype(jnp.float32)
                cut = jnp.where(picks[slot], other, cut)
            cut = pltpu.roll(cut, shifts[chip], 0)[:WIN]
            cut = pltpu.roll(cut, lax.rem(WIN - lax.rem(bins_ref[chip], WIN), WIN), 1)
            slices[chip * 2 + part] = bf16(cut)
    for way in range(CHIPS):
        for part in (0, 1):
            outs[way][part] = slices[2 * (way ^ (date // 2)) + part]


def cut_windows(me, date, chip_lines, chip_bins, picks, image):
    smem, vmem = pl.BlockSpec(memory_space=pltpu.SMEM), pl.BlockSpec(memory_space=pltpu.VMEM)
    return pl.pallas_call(
        window_kernel,
        in_specs=[smem] * 4 + [vmem, pl.BlockSpec(memory_space=pl.ANY)],
        out_specs=[vmem] * (CHIPS + 1),
        out_shape=[jax.ShapeDtypeStruct((count, WIN, WIN), jnp.bfloat16) for count in (2, 2, 2, 2, 8)],
        scratch_shapes=[
            pltpu.VMEM((CHIPS, 2, ROWS, PART), jnp.bfloat16),
            pltpu.SemaphoreType.DMA((CHIPS,)),
        ],
        compiler_params=pltpu.CompilerParams(vmem_limit_bytes=VMEM),
        name="cut_windows",
    )(me, date, chip_lines, chip_bins, picks, image)


def pass_kernel(date_ref, mate_ref, *refs):
    ins, outs, (held,) = refs[:DATES], refs[DATES : DATES + CHIPS], refs[DATES + CHIPS :]
    date = date_ref[0]
    for way in range(CHIPS):
        for other in (0, 1):
            held[2 * way + other] = ins[CHIPS * other + way][...]
    for way in range(CHIPS):
        outs[way][...] = held[mate_ref[(2 * way) ^ date] ^ date]


def pass_on(date, partner_date, held):
    smem, vmem = pl.BlockSpec(memory_space=pltpu.SMEM), pl.BlockSpec(memory_space=pltpu.VMEM)
    return pl.pallas_call(
        pass_kernel,
        in_specs=[smem] * 2 + [vmem] * DATES,
        out_specs=[vmem] * CHIPS,
        out_shape=[jax.ShapeDtypeStruct((2, WIN, WIN), jnp.bfloat16)] * CHIPS,
        scratch_shapes=[pltpu.VMEM((DATES, 2, WIN, WIN), jnp.bfloat16)],
        name="pass_on",
    )(date, partner_date, *held)


def along_y(chips):
    return [chips[0]] + [from_ways(chips[way], "date", DATES, (2 * way,))[0] for way in (1, 2, 3)]


def exchange(date, partner_date, chips):
    held = along_y(chips)
    held += [from_ways(chip, "date", DATES, (1,))[0] for chip in held]
    return along_y(pass_on(date, partner_date, held))


def transform(stacked, left, right):
    y = dot(left, jnp.concatenate(stacked, axis=1))
    half = y.shape[0] // 2
    rows = []
    for chip in range(CHIPS):
        cut = y[:, chip * WIN : (chip + 1) * WIN]
        rows.append(jnp.concatenate([bf16(cut[:half]), bf16(cut[half:])], axis=1))
    return dot(jnp.concatenate(rows, axis=0), right)


def correlate_kernel(
    date_ref, offsets_ref, own_ref, left_ref, right_ref, left3_ref, right3_ref, *refs
):
    ins, (out_ref, their_ref) = refs[:CHIPS], refs[CHIPS:]
    for way in range(CHIPS):
        their_ref[way ^ (date_ref[0] // 2)] = ins[way][...]
    left, right = left_ref[...], right_ref[...]
    inside = lax.broadcasted_iota(jnp.int32, (CHIP, WIN), 1) < CHIP
    empty = jnp.zeros((WIN - CHIP, WIN), jnp.bfloat16)
    primary = []
    for chip in range(CHIPS):
        row, col = offsets_ref[chip, 0], offsets_ref[chip, 1]
        pieces = []
        for part in (0, 1):
            cut = own_ref[chip * 2 + part].astype(jnp.float32)
            cut = pltpu.roll(cut, lax.rem(WIN - row, WIN), 0)[:CHIP]
            cut = pltpu.roll(cut, lax.rem(WIN - col, WIN), 1)
            pieces += [bf16(jnp.where(inside, cut, 0.0)), empty]
        primary.append(jnp.concatenate(pieces, axis=0))
    first = transform(primary, left, right)
    second = transform(
        [jnp.concatenate([their_ref[chip, 0], their_ref[chip, 1]], axis=0) for chip in range(CHIPS)],
        left,
        right,
    )
    a = (first[:, :WIN], first[:, WIN:])
    b = (second[:, :WIN], second[:, WIN:])
    product = (a[0] * b[0] + a[1] * b[1], a[1] * b[0] - a[0] * b[1])
    product = [bf16(part) for part in product]
    surface = transform(
        [
            jnp.concatenate([part[chip * WIN : (chip + 1) * WIN] for part in product], axis=0)
            for chip in range(CHIPS)
        ],
        left3_ref[...],
        right3_ref[...],
    )
    for chip in range(CHIPS):
        out_ref[0, chip] = surface[chip * CHIP : (chip + 1) * CHIP]


def correlate(date, offsets, own, theirs):
    table = dft(WIN, -1)
    left, right = from_left(table), from_right(table)
    factor = WIN // CHIP
    keep = np.concatenate([np.arange(CHIP), WIN + np.arange(CHIP)])
    vmem = pl.BlockSpec(memory_space=pltpu.VMEM)
    return pl.pallas_call(
        correlate_kernel,
        in_specs=[pl.BlockSpec(memory_space=pltpu.SMEM)] * 2 + [vmem] * (5 + CHIPS),
        out_specs=vmem,
        out_shape=jax.ShapeDtypeStruct((1, CHIPS, CHIP, 2 * CHIP), jnp.float32),
        scratch_shapes=[pltpu.VMEM((CHIPS, 2, WIN, WIN), jnp.bfloat16)],
        compiler_params=pltpu.CompilerParams(vmem_limit_bytes=VMEM),
        name="correlate",
    )(
        date,
        offsets,
        own,
        as_bf16(left),
        as_bf16(right),
        as_bf16(left[keep]),
        as_bf16(right[:, keep] * factor),
        *theirs,
    )


def to_blocks(x):
    return lax.all_to_all(x, "rng", split_axis=0, concat_axis=0, tiled=True)


def local(
    raw_echoes, range_filter, azimuth_filter, partner_date, chip_lines, chip_bins, chip_offsets
):
    me = lax.axis_index("rng").astype(jnp.int32).reshape(1)
    date = lax.axis_index("date").astype(jnp.int32).reshape(1)
    bins = all_bins(chip_bins)
    (early,) = compress_range(raw_echoes, range_filter, 0, EARLY)
    early, bins = lax.optimization_barrier((early, bins))
    early = to_blocks(early)
    swaps, own, picks = plan(me, bins)
    late, late_two = compress_range(raw_echoes, range_filter, EARLY, LATE, swaps)
    response, response_two = regroup_filter(azimuth_filter, own)
    late, early, response, response_two = lax.optimization_barrier(
        (late, early, response, response_two)
    )
    late = to_blocks(late)
    early, early_two = order_bins(own, early)
    late_two, early, early_two = lax.optimization_barrier((late_two, early, early_two))
    late_two = to_blocks(late_two)
    first = focus_azimuth(early, late, response)
    *chips, windows = cut_windows(me, date, chip_lines, chip_bins, picks, first)
    theirs = exchange(date, partner_date, chips)
    correlation = correlate(date, chip_offsets, windows, theirs)
    return (finish(own, early_two, late_two, response_two, first), correlation)


def solution(mesh):
    in_specs = (
        P("date", None, "rng", None),
        P(),
        P(None, None, "rng"),
        P(),
        P("rng"),
        P("rng"),
        P("rng", None),
    )
    out_specs = (P("date", None, None, "rng"), P("date", "rng", None, None))
    return jax.shard_map(local, mesh=mesh, in_specs=in_specs, out_specs=out_specs, check_vma=False)
```

```python
import functools
import math

import jax
import jax.numpy as jnp
import ml_dtypes
import numpy as np
from jax import lax
from jax.experimental import pallas as pl
from jax.experimental.pallas import tpu as pltpu
from jax.sharding import PartitionSpec as P

LINES = 1024
BINS = 16384
CHIP = 64
CHIPS = 4
WIN = 128
DATES = 8
N_RNG = 16
SIDE = 128
FAN = 8
BLOCK = BINS // N_RNG
OWN = LINES // N_RNG
SLOTS = 8
HALF = 4
PART = HALF * 128
SORT = ((0, 1), (2, 3), (0, 2), (1, 3), (1, 2))
NETWORK = SORT + tuple((i + 4, j + 4) for i, j in SORT) + ((0, 7), (1, 6), (2, 5), (3, 4))
EARLY = 16
LATE = OWN - EARLY
ORDER = 4
GROUP = 16
BATCH = 16
SPAN = 256
WIDE = GROUP + 8
LONG = SIDE + 8
VMEM = 56 * 1024 * 1024


def dft(length, sign):
    phase = np.outer(np.arange(length), np.arange(length)) % length
    return np.exp(sign * 2j * math.pi * phase / length) / math.sqrt(length)


def twiddles(count, other, sign):
    phase = np.outer(np.arange(count), np.arange(other))
    return np.exp(sign * 2j * math.pi * phase / (count * other))


def from_left(table):
    return np.block([[table.real, -table.imag], [table.imag, table.real]])


def from_right(table):
    return np.block([[table.real, table.imag], [-table.imag, table.real]])


def as_bf16(table):
    return jnp.asarray(np.asarray(table, np.float32).astype(ml_dtypes.bfloat16))


def parts_of(table):
    return jnp.asarray(np.stack([table.real, table.imag]).astype(np.float32))


def times(a, b):
    return (a[0] * b[0] - a[1] * b[1], a[0] * b[1] + a[1] * b[0])


def dot(a, b):
    return jnp.dot(a, b, preferred_element_type=jnp.float32)


def bf16(x):
    return x.astype(jnp.bfloat16)


def swapped(slots, swaps, pairs):
    slots = list(slots)
    for swap, (i, j) in zip(swaps, pairs):
        slots[i], slots[j] = (
            jnp.where(swap, slots[j], slots[i]),
            jnp.where(swap, slots[i], slots[j]),
        )
    return slots


def masks(ref):
    return [jnp.broadcast_to(ref[at : at + 1, :], (16, SIDE)) > 0.5 for at in range(len(NETWORK))]


def plan_kernel(me_ref, near_ref, *refs):
    far_refs, (swap_ref, own_ref, pick_ref) = refs[:3], refs[3:]
    me = me_ref[0]
    lane = lax.broadcasted_iota(jnp.int32, (N_RNG, SIDE), 1)
    device = lax.broadcasted_iota(jnp.int32, (N_RNG, SIDE), 0)
    runs = []
    for chip in range(CHIPS):
        first = jnp.zeros((N_RNG, SIDE), jnp.int32)
        for far, ref in zip((0, *FAR), (near_ref, *far_refs)):
            for at, near in enumerate((0, *NEAR)):
                first = jnp.where(device == (me ^ far ^ near), ref[at * CHIPS + chip], first)
        runs.append(first // SIDE + jnp.where(lane < first % SIDE, 1, 0))
    holds = [[jnp.where(run == slot, 1.0, 0.0) for slot in range(SLOTS)] for run in runs]
    wanted = [functools.reduce(jnp.maximum, [hold[slot] for hold in holds]) for slot in range(SLOTS)]
    for at, (i, j) in enumerate(NETWORK):
        swap = wanted[j] > wanted[i]
        swap_ref[at] = jnp.where(swap, 1.0, 0.0)
        wanted = swapped(wanted, [swap], [(i, j)])
        holds = [swapped(hold, [swap], [(i, j)]) for hold in holds]
    for at in range(len(NETWORK)):
        own_ref[at : at + 1, :] = swap_ref[at, pl.ds(me, 1), :]
    for chip in range(CHIPS):
        for slot in range(HALF):
            at = chip * HALF + slot
            pick_ref[at] = holds[chip][slot]


NEAR = (1, 8, 9)
FAR = (2, 4, 6)


def from_ways(x, axis, size, ways):
    return [lax.ppermute(x, axis, [(i, i ^ way) for i in range(size)]) for way in ways]


def all_bins(chip_bins):
    near = jnp.concatenate([chip_bins] + from_ways(chip_bins, "rng", N_RNG, NEAR))
    return [near] + from_ways(near, "rng", N_RNG, FAR)


def plan(me, bins):
    smem, vmem = pl.BlockSpec(memory_space=pltpu.SMEM), pl.BlockSpec(memory_space=pltpu.VMEM)
    return pl.pallas_call(
        plan_kernel,
        in_specs=[smem] * 5,
        out_specs=[vmem] * 3,
        out_shape=[
            jax.ShapeDtypeStruct((len(NETWORK), N_RNG, SIDE), jnp.float32),
            jax.ShapeDtypeStruct((len(NETWORK) + 2, SIDE), jnp.float32),
            jax.ShapeDtypeStruct((CHIPS * HALF, N_RNG, SIDE), jnp.float32),
        ],
        name="plan",
    )(me, *bins)


def range_kernel(x_ref, h_ref, w_ref, t1_ref, t2_ref, t3_ref, t4_ref, *refs, ordered):
    s = SIDE
    *refs, xs, ys, hs = refs

    @pl.when(pl.program_id(0) == 0)
    def _():
        for part in range(2):
            for j in range(s):
                ys[j : j + 1, :] = h_ref[part : part + 1, j * s : (j + 1) * s]
            hs[part] = ys[:s, :].T

    for part in range(2):
        for n in range(s):
            row = (part * s + n) * WIDE
            xs[row : row + GROUP, :] = x_ref[0, part, :, n * s : (n + 1) * s].astype(jnp.float32)
    w = (w_ref[0], w_ref[1])
    wc = (w[0], -w[1])
    h = (hs[0], hs[1])
    for line in range(0, GROUP, BATCH):
        batch = range(line, line + BATCH)
        x = [
            jnp.concatenate(
                [bf16(xs[pl.ds(part * s * WIDE + one, s, stride=WIDE), :]) for part in (0, 1)],
                axis=0,
            )
            for one in batch
        ]
        y = dot(t1_ref[...], jnp.concatenate(x, axis=1))
        x = []
        for one in range(BATCH):
            cut = y[:, one * s : (one + 1) * s]
            z = times((cut[:s], cut[s:]), w)
            x.append(jnp.concatenate([bf16(z[0]), bf16(z[1])], axis=1))
        y = dot(jnp.concatenate(x, axis=0), t2_ref[...])
        x = []
        for one in range(BATCH):
            cut = y[one * s : (one + 1) * s]
            z = times((cut[:, :s], cut[:, s:]), h)
            x.append(jnp.concatenate([bf16(z[0]), bf16(z[1])], axis=1))
        y = dot(jnp.concatenate(x, axis=0), t3_ref[...])
        x = []
        for one in range(BATCH):
            cut = y[one * s : (one + 1) * s]
            z = times((cut[:, :s], cut[:, s:]), wc)
            x.append(jnp.concatenate([bf16(z[0]), bf16(z[1])], axis=0))
        y = dot(t4_ref[...], jnp.concatenate(x, axis=1))
        for one in range(BATCH):
            for part in (0, 1):
                row = (part * GROUP + line + one) * LONG
                ys[row : row + s, :] = y[
                    part * s : (part + 1) * s, one * s : (one + 1) * s
                ]
    for dest in range(N_RNG):
        if ordered:
            swap_ref, out1_ref, out2_ref = refs
            swaps = masks(swap_ref.at[:, dest])
        else:
            (out_ref,) = refs
        for part in (0, 1):
            slots = []
            for slot in range(SLOTS):
                row = part * GROUP * LONG + dest * SLOTS + slot
                slots.append(ys[pl.ds(row, GROUP, stride=LONG), :])
            if not ordered:
                for slot in range(SLOTS):
                    out_ref[dest, part, :, slot * s : (slot + 1) * s] = bf16(slots[slot])
                continue
            slots = swapped(slots, swaps, NETWORK)
            for slot in range(HALF):
                lanes = slice(slot * s, (slot + 1) * s)
                out1_ref[dest, part, :, lanes] = bf16(slots[slot])
                out2_ref[dest, part, :, lanes] = bf16(slots[slot + HALF])


def whole(shape):
    return pl.BlockSpec(shape, lambda *_: (0,) * len(shape))


def compress_range(raw_echoes, range_filter, first, lines, swaps=None):
    forward = dft(SIDE, -1)
    backward = dft(SIDE, 1)
    tables = [
        as_bf16(from_left(forward)),
        as_bf16(from_right(forward)),
        as_bf16(from_right(backward)),
        as_bf16(from_left(backward)),
    ]
    turn = parts_of(twiddles(SIDE, SIDE, -1))
    table = whole((2 * SIDE, 2 * SIDE))
    ordered = swaps is not None
    width, count = (PART, 2) if ordered else (BLOCK, 1)
    outs = pl.pallas_call(
        functools.partial(range_kernel, ordered=ordered),
        grid=(lines // GROUP,),
        in_specs=[
            pl.BlockSpec((1, 2, GROUP, BINS), lambda i: (0, 0, i + first // GROUP, 0)),
            whole((2, BINS)),
            whole((2, SIDE, SIDE)),
            table,
            table,
            table,
            table,
        ]
        + [whole((len(NETWORK), N_RNG, SIDE))] * ordered,
        out_specs=[pl.BlockSpec((N_RNG, 2, GROUP, width), lambda i: (0, 0, i, 0))] * count,
        out_shape=[jax.ShapeDtypeStruct((N_RNG, 2, lines, width), jnp.bfloat16)] * count,
        scratch_shapes=[
            pltpu.VMEM((2 * SIDE * WIDE, SIDE), jnp.float32),
            pltpu.VMEM((2 * LONG * GROUP, SIDE), jnp.float32),
            pltpu.VMEM((2, SIDE, SIDE), jnp.float32),
        ],
        compiler_params=pltpu.CompilerParams(vmem_limit_bytes=VMEM),
        cost_estimate=pl.CostEstimate(flops=4 * 10**9, bytes_accessed=2**22, transcendentals=0),
        name="compress_range",
    )(raw_echoes, range_filter, turn, *tables, *([swaps] * ordered))
    return [out.reshape(N_RNG, 2 * lines, width) for out in outs]


def order_kernel(own_ref, x_ref, out1_ref, out2_ref):
    swaps = masks(own_ref)
    for device in range(ORDER):
        for row in range(0, 2 * EARLY, 16):
            rows = slice(row, row + 16)
            slots = [
                x_ref[device, rows, slot * SIDE : (slot + 1) * SIDE].astype(jnp.float32)
                for slot in range(SLOTS)
            ]
            slots = swapped(slots, swaps, NETWORK)
            for slot in range(HALF):
                lanes = slice(slot * SIDE, (slot + 1) * SIDE)
                out1_ref[device, rows, lanes] = bf16(slots[slot])
                out2_ref[device, rows, lanes] = bf16(slots[slot + HALF])


def order_bins(own, x):
    return pl.pallas_call(
        order_kernel,
        grid=(N_RNG // ORDER,),
        in_specs=[
            whole((len(NETWORK) + 2, SIDE)),
            pl.BlockSpec((ORDER, 2 * EARLY, BLOCK), lambda i: (i, 0, 0)),
        ],
        out_specs=[pl.BlockSpec((ORDER, 2 * EARLY, PART), lambda i: (i, 0, 0))] * 2,
        out_shape=[jax.ShapeDtypeStruct((N_RNG, 2 * EARLY, PART), jnp.bfloat16)] * 2,
        compiler_params=pltpu.CompilerParams(vmem_limit_bytes=VMEM),
        cost_estimate=pl.CostEstimate(flops=10**7, bytes_accessed=2**22, transcendentals=0),
        name="order_bins",
    )(own, x)


def add(a, b):
    return (a[0] + b[0], a[1] + b[1])


def sub(a, b):
    return (a[0] - b[0], a[1] - b[1])


def fan_dft(x, sign):
    root = math.sqrt(0.5)

    def quarter(a):
        return (-sign * a[1], sign * a[0]) if sign > 0 else (a[1], -a[0])

    def eighth(a):
        if sign > 0:
            return ((a[0] - a[1]) * root, (a[0] + a[1]) * root)
        return ((a[0] + a[1]) * root, (a[1] - a[0]) * root)

    def four(a, b, c, d):
        e, f, g, h = add(a, c), sub(a, c), add(b, d), quarter(sub(b, d))
        return add(e, g), add(f, h), sub(e, g), sub(f, h)

    even = four(x[0], x[2], x[4], x[6])
    odd = four(x[1], x[3], x[5], x[7])
    odd = (odd[0], eighth(odd[1]), quarter(odd[2]), quarter(eighth(odd[3])))
    return [add(p, q) for p, q in zip(even, odd)] + [sub(p, q) for p, q in zip(even, odd)]


def azimuth_step(a_ref, b_ref, f_ref, w_ref, t5_ref, t6_ref, spread, mixed, put):
    m = LINES // FAN
    tiles = [(t, slice(lane * 128, (lane + 1) * 128)) for t in range(m // 16) for lane in range(SPAN // 128)]
    for tile, lanes in tiles:
        half, line = divmod(tile * 16, OWN)
        points = []
        for n in range(FAN):
            ref, row, lines = (a_ref, line, EARLY) if line < EARLY else (b_ref, line - EARLY, LATE)
            rows = [slice(part * lines + row, part * lines + row + 16) for part in (0, 1)]
            points.append(tuple(ref[2 * n + half, row, lanes].astype(jnp.float32) for row in rows))
        for k, value in enumerate(fan_dft(points, -1)):
            if k:
                row = k * m + tile * 16
                value = times(value, (w_ref[0, row : row + 16], w_ref[1, row : row + 16]))
            for part in (0, 1):
                row = (half * 2 + part) * OWN + line
                at = k * SPAN + lanes.start
                spread[row : row + 16, at : at + 128] = bf16(value[part])
    y = dot(t5_ref[...], spread[...])
    x = []
    for k in range(FAN):
        cut = y[:, k * SPAN : (k + 1) * SPAN]
        f = (f_ref[k, 0].astype(jnp.float32), f_ref[k, 1].astype(jnp.float32))
        z = times((cut[:m], cut[m:]), f)
        x.append(jnp.concatenate([bf16(z[0]), bf16(z[1])], axis=0))
    mixed[...] = dot(t6_ref[...], jnp.concatenate(x, axis=1))
    for tile, lanes in tiles:
        points = []
        for k in range(FAN):
            at = k * SPAN + lanes.start
            row = tile * 16
            value = tuple(mixed[part * m + row : part * m + row + 16, at : at + 128] for part in (0, 1))
            if k:
                row += k * m
                value = times(value, (w_ref[0, row : row + 16], -w_ref[1, row : row + 16]))
            points.append(value)
        for p, value in enumerate(fan_dft(points, 1)):
            row = p * m + tile * 16
            for part in (0, 1):
                put(part, row, lanes, bf16(value[part]))


def azimuth_kernel(a_ref, b_ref, f_ref, w_ref, t5_ref, t6_ref, out_ref, spread, mixed):
    def put(part, row, lanes, value):
        out_ref[part, row : row + 16, lanes] = value

    azimuth_step(a_ref, b_ref, f_ref, w_ref, t5_ref, t6_ref, spread, mixed, put)


def azimuth_tables():
    m = LINES // FAN
    forward = np.exp(-2j * math.pi * np.outer(np.arange(m), np.arange(m)) / m) / math.sqrt(LINES)
    backward = forward.conj()
    first = from_left(forward).reshape(2 * m, 2, 2, OWN).transpose(0, 2, 1, 3).reshape(2 * m, 2 * m)
    turn = twiddles(FAN, m, -1).reshape(LINES, 1) * np.ones((1, 128))
    return parts_of(turn), as_bf16(first), as_bf16(from_left(backward))


AZIMUTH_SCRATCH = [
    pltpu.VMEM((2 * LINES // FAN, FAN * SPAN), jnp.bfloat16),
    pltpu.VMEM((2 * LINES // FAN, FAN * SPAN), jnp.float32),
]


def focus_azimuth(early, late, response):
    m = LINES // FAN
    table = whole((2 * m, 2 * m))
    return pl.pallas_call(
        azimuth_kernel,
        grid=(PART // SPAN,),
        in_specs=[
            pl.BlockSpec((N_RNG, 2 * EARLY, SPAN), lambda i: (0, 0, i)),
            pl.BlockSpec((N_RNG, 2 * LATE, SPAN), lambda i: (0, 0, i)),
            pl.BlockSpec((FAN, 2, m, SPAN), lambda i: (0, 0, 0, i)),
            whole((2, LINES, 128)),
            table,
            table,
        ],
        out_specs=pl.BlockSpec((2, LINES, SPAN), lambda i: (0, 0, i)),
        out_shape=jax.ShapeDtypeStruct((2, LINES, PART), jnp.bfloat16),
        scratch_shapes=AZIMUTH_SCRATCH,
        compiler_params=pltpu.CompilerParams(vmem_limit_bytes=VMEM),
        name="focus_azimuth",
    )(early, late, response, *azimuth_tables())


def regroup_kernel(f_ref, own_ref, out1_ref, out2_ref, wide):
    swaps = masks(own_ref)
    for part in (0, 1):
        for slot in range(SLOTS):
            wide[slot] = f_ref[part, :, slot * SIDE : (slot + 1) * SIDE].astype(jnp.float32)
        for k in range(FAN):
            slots = [wide[slot, pl.ds(k, 16, stride=FAN), :] for slot in range(SLOTS)]
            slots = swapped(slots, swaps, NETWORK)
            for slot in range(HALF):
                lanes = slice(slot * SIDE, (slot + 1) * SIDE)
                out1_ref[k, part, :, lanes] = bf16(slots[slot])
                out2_ref[k, part, :, lanes] = bf16(slots[slot + HALF])


def regroup_filter(azimuth_filter, own):
    m = LINES // FAN
    return pl.pallas_call(
        regroup_kernel,
        grid=(FAN,),
        in_specs=[
            pl.BlockSpec((2, 16 * FAN, BLOCK), lambda i: (0, i, 0)),
            whole((len(NETWORK) + 2, SIDE)),
        ],
        out_specs=[pl.BlockSpec((FAN, 2, 16, PART), lambda i: (0, 0, i, 0))] * 2,
        out_shape=[jax.ShapeDtypeStruct((FAN, 2, m, PART), jnp.bfloat16)] * 2,
        scratch_shapes=[pltpu.VMEM((SLOTS, 16 * FAN, SIDE), jnp.float32)],
        compiler_params=pltpu.CompilerParams(vmem_limit_bytes=VMEM),
        cost_estimate=pl.CostEstimate(flops=10**7, bytes_accessed=2**23, transcendentals=0),
        name="regroup_filter",
    )(azimuth_filter, own)


MERGE = 256
STEPS = PART // SPAN


def finish_kernel(
    own_ref, a_ref, b_ref, f_ref, w_ref, t5_ref, t6_ref, first_ref, out_ref, spread, mixed, held
):
    step = pl.program_id(0)

    @pl.when(step < STEPS)
    def _():
        def put(part, row, lanes, value):
            held[step, part, row : row + 16, lanes] = value

        azimuth_step(a_ref, b_ref, f_ref, w_ref, t5_ref, t6_ref, spread, mixed, put)

    @pl.when(step >= STEPS)
    def _():
        swaps = masks(own_ref)
        first = (step - STEPS) * MERGE
        for part in (0, 1):
            for row in range(0, MERGE, 16):
                rows = slice(row, row + 16)
                slots = [
                    first_ref[part, rows, slot * SIDE : (slot + 1) * SIDE] for slot in range(HALF)
                ]
                for slot in range(HALF):
                    at, lane = divmod(slot * SIDE, SPAN)
                    from_row = pl.ds(pl.multiple_of(first + row, 16), 16)
                    slots.append(held[at, part, from_row, lane : lane + SIDE])
                slots = [slot.astype(jnp.float32) for slot in slots]
                slots = swapped(slots, swaps[::-1], NETWORK[::-1])
                for slot in range(SLOTS):
                    out_ref[0, part, rows, slot * SIDE : (slot + 1) * SIDE] = bf16(slots[slot])


def finish(own, early, late, response, image):
    m = LINES // FAN
    table = whole((2 * m, 2 * m))
    return pl.pallas_call(
        finish_kernel,
        grid=(STEPS + LINES // MERGE,),
        in_specs=[
            whole((len(NETWORK) + 2, SIDE)),
            pl.BlockSpec((N_RNG, 2 * EARLY, SPAN), lambda i: (0, 0, jnp.minimum(i, STEPS - 1))),
            pl.BlockSpec((N_RNG, 2 * LATE, SPAN), lambda i: (0, 0, jnp.minimum(i, STEPS - 1))),
            pl.BlockSpec((FAN, 2, m, SPAN), lambda i: (0, 0, 0, jnp.minimum(i, STEPS - 1))),
            whole((2, LINES, 128)),
            table,
            table,
            pl.BlockSpec((2, MERGE, PART), lambda i: (0, jnp.maximum(i - STEPS, 0), 0)),
        ],
        out_specs=pl.BlockSpec(
            (1, 2, MERGE, BLOCK), lambda i: (0, 0, jnp.maximum(i - STEPS, 0), 0)
        ),
        out_shape=jax.ShapeDtypeStruct((1, 2, LINES, BLOCK), jnp.bfloat16),
        scratch_shapes=AZIMUTH_SCRATCH + [pltpu.VMEM((STEPS, 2, LINES, SPAN), jnp.bfloat16)],
        compiler_params=pltpu.CompilerParams(vmem_limit_bytes=VMEM),
        name="finish",
    )(own, early, late, response, *azimuth_tables(), image)


ROWS = WIN + 16


def window_kernel(me_ref, date_ref, lines_ref, bins_ref, pick_ref, image_ref, *refs):
    *outs, slices, held, sems = refs
    me, date = me_ref[0], date_ref[0]
    copies = []
    shifts = []
    for chip in range(CHIPS):
        line = lines_ref[chip]
        row = jnp.minimum(line // 16 * 16, LINES - ROWS)
        copy = pltpu.make_async_copy(
            image_ref.at[:, pl.ds(pl.multiple_of(row, 16), ROWS), :], held.at[chip], sems.at[chip]
        )
        copy.start()
        copies.append(copy)
        shifts.append(lax.rem(ROWS - (line - row), ROWS))
    for chip in range(CHIPS):
        copies[chip].wait()
        picks = [pick_ref[chip * HALF + slot, pl.ds(me, 1), :] > 0.5 for slot in range(HALF)]
        for part in (0, 1):
            cut = held[chip, part, :, :SIDE].astype(jnp.float32)
            for slot in range(1, HALF):
                other = held[chip, part, :, slot * SIDE : (slot + 1) * SIDE].astype(jnp.float32)
                cut = jnp.where(picks[slot], other, cut)
            cut = pltpu.roll(cut, shifts[chip], 0)[:WIN]
            cut = pltpu.roll(cut, lax.rem(WIN - lax.rem(bins_ref[chip], WIN), WIN), 1)
            slices[chip * 2 + part] = bf16(cut)
    for way in range(CHIPS):
        for part in (0, 1):
            outs[way][part] = slices[2 * (way ^ (date // 2)) + part]


def cut_windows(me, date, chip_lines, chip_bins, picks, image):
    smem, vmem = pl.BlockSpec(memory_space=pltpu.SMEM), pl.BlockSpec(memory_space=pltpu.VMEM)
    return pl.pallas_call(
        window_kernel,
        in_specs=[smem] * 4 + [vmem, pl.BlockSpec(memory_space=pl.ANY)],
        out_specs=[vmem] * (CHIPS + 1),
        out_shape=[jax.ShapeDtypeStruct((count, WIN, WIN), jnp.bfloat16) for count in (2, 2, 2, 2, 8)],
        scratch_shapes=[
            pltpu.VMEM((CHIPS, 2, ROWS, PART), jnp.bfloat16),
            pltpu.SemaphoreType.DMA((CHIPS,)),
        ],
        compiler_params=pltpu.CompilerParams(vmem_limit_bytes=VMEM),
        name="cut_windows",
    )(me, date, chip_lines, chip_bins, picks, image)


def pass_kernel(date_ref, mate_ref, *refs):
    ins, outs, (held,) = refs[:DATES], refs[DATES : DATES + CHIPS], refs[DATES + CHIPS :]
    date = date_ref[0]
    for way in range(CHIPS):
        for other in (0, 1):
            held[2 * way + other] = ins[CHIPS * other + way][...]
    for way in range(CHIPS):
        outs[way][...] = held[mate_ref[(2 * way) ^ date] ^ date]


def pass_on(date, partner_date, held):
    smem, vmem = pl.BlockSpec(memory_space=pltpu.SMEM), pl.BlockSpec(memory_space=pltpu.VMEM)
    return pl.pallas_call(
        pass_kernel,
        in_specs=[smem] * 2 + [vmem] * DATES,
        out_specs=[vmem] * CHIPS,
        out_shape=[jax.ShapeDtypeStruct((2, WIN, WIN), jnp.bfloat16)] * CHIPS,
        scratch_shapes=[pltpu.VMEM((DATES, 2, WIN, WIN), jnp.bfloat16)],
        name="pass_on",
    )(date, partner_date, *held)


def along_y(chips):
    return [chips[0]] + [from_ways(chips[way], "date", DATES, (2 * way,))[0] for way in (1, 2, 3)]


def exchange(date, partner_date, chips):
    held = along_y(chips)
    held += [from_ways(chip, "date", DATES, (1,))[0] for chip in held]
    return along_y(pass_on(date, partner_date, held))


def transform(stacked, left, right):
    y = dot(left, jnp.concatenate(stacked, axis=1))
    half = y.shape[0] // 2
    rows = []
    for chip in range(CHIPS):
        cut = y[:, chip * WIN : (chip + 1) * WIN]
        rows.append(jnp.concatenate([bf16(cut[:half]), bf16(cut[half:])], axis=1))
    return dot(jnp.concatenate(rows, axis=0), right)


def correlate_kernel(
    date_ref, offsets_ref, own_ref, left_ref, right_ref, left3_ref, right3_ref, *refs
):
    ins, (out_ref, their_ref) = refs[:CHIPS], refs[CHIPS:]
    for way in range(CHIPS):
        their_ref[way ^ (date_ref[0] // 2)] = ins[way][...]
    left, right = left_ref[...], right_ref[...]
    inside = lax.broadcasted_iota(jnp.int32, (CHIP, WIN), 1) < CHIP
    empty = jnp.zeros((WIN - CHIP, WIN), jnp.bfloat16)
    primary = []
    for chip in range(CHIPS):
        row, col = offsets_ref[2 * chip], offsets_ref[2 * chip + 1]
        pieces = []
        for part in (0, 1):
            cut = own_ref[chip * 2 + part].astype(jnp.float32)
            cut = pltpu.roll(cut, lax.rem(WIN - row, WIN), 0)[:CHIP]
            cut = pltpu.roll(cut, lax.rem(WIN - col, WIN), 1)
            pieces += [bf16(jnp.where(inside, cut, 0.0)), empty]
        primary.append(jnp.concatenate(pieces, axis=0))
    first = transform(primary, left, right)
    second = transform(
        [jnp.concatenate([their_ref[chip, 0], their_ref[chip, 1]], axis=0) for chip in range(CHIPS)],
        left,
        right,
    )
    a = (first[:, :WIN], first[:, WIN:])
    b = (second[:, :WIN], second[:, WIN:])
    product = (a[0] * b[0] + a[1] * b[1], a[1] * b[0] - a[0] * b[1])
    product = [bf16(part) for part in product]
    surface = transform(
        [
            jnp.concatenate([part[chip * WIN : (chip + 1) * WIN] for part in product], axis=0)
            for chip in range(CHIPS)
        ],
        left3_ref[...],
        right3_ref[...],
    )
    for chip in range(CHIPS):
        out_ref[0, chip] = surface[chip * CHIP : (chip + 1) * CHIP]


def correlate(date, offsets, own, theirs):
    table = dft(WIN, -1)
    left, right = from_left(table), from_right(table)
    factor = WIN // CHIP
    keep = np.concatenate([np.arange(CHIP), WIN + np.arange(CHIP)])
    vmem = pl.BlockSpec(memory_space=pltpu.VMEM)
    return pl.pallas_call(
        correlate_kernel,
        in_specs=[pl.BlockSpec(memory_space=pltpu.SMEM)] * 2 + [vmem] * (5 + CHIPS),
        out_specs=vmem,
        out_shape=jax.ShapeDtypeStruct((1, CHIPS, CHIP, 2 * CHIP), jnp.float32),
        scratch_shapes=[pltpu.VMEM((CHIPS, 2, WIN, WIN), jnp.bfloat16)],
        compiler_params=pltpu.CompilerParams(vmem_limit_bytes=VMEM),
        name="correlate",
    )(
        date,
        offsets,
        own,
        as_bf16(left),
        as_bf16(right),
        as_bf16(left[keep]),
        as_bf16(right[:, keep] * factor),
        *theirs,
    )


def to_blocks(x):
    return lax.all_to_all(x, "rng", split_axis=0, concat_axis=0, tiled=True)


def local(
    raw_echoes, range_filter, azimuth_filter, partner_date, chip_lines, chip_bins, chip_offsets
):
    me = lax.axis_index("rng").astype(jnp.int32).reshape(1)
    date = lax.axis_index("date").astype(jnp.int32).reshape(1)
    bins = all_bins(chip_bins)
    (early,) = compress_range(raw_echoes, range_filter, 0, EARLY)
    early, bins, offsets = lax.optimization_barrier((early, bins, chip_offsets.reshape(-1)))
    early = to_blocks(early)
    swaps, own, picks = plan(me, bins)
    late, late_two = compress_range(raw_echoes, range_filter, EARLY, LATE, swaps)
    late, own, early = lax.optimization_barrier((late, own, early))
    late = to_blocks(late)
    early, early_two = order_bins(own, early)
    response, response_two = regroup_filter(azimuth_filter, own)
    late_two, early, early_two, response, response_two = lax.optimization_barrier(
        (late_two, early, early_two, response, response_two)
    )
    late_two = to_blocks(late_two)
    first = focus_azimuth(early, late, response)
    *chips, windows = cut_windows(me, date, chip_lines, chip_bins, picks, first)
    theirs = exchange(date, partner_date, chips)
    correlation = correlate(date, offsets, windows, theirs)
    return (finish(own, early_two, late_two, response_two, first), correlation)


def solution(mesh):
    in_specs = (
        P("date", None, "rng", None),
        P(),
        P(None, None, "rng"),
        P(),
        P("rng"),
        P("rng"),
        P("rng", None),
    )
    out_specs = (P("date", None, None, "rng"), P("date", "rng", None, None))
    return jax.shard_map(local, mesh=mesh, in_specs=in_specs, out_specs=out_specs, check_vma=False)
```

```python
import functools
import math

import jax
import jax.numpy as jnp
import ml_dtypes
import numpy as np
from jax import lax
from jax.experimental import pallas as pl
from jax.experimental.pallas import tpu as pltpu
from jax.sharding import PartitionSpec as P

LINES = 1024
BINS = 16384
CHIP = 64
CHIPS = 4
WIN = 128
DATES = 8
N_RNG = 16
SIDE = 128
FAN = 8
BLOCK = BINS // N_RNG
OWN = LINES // N_RNG
SLOTS = 8
HALF = 4
PART = HALF * 128
SORT = ((0, 1), (2, 3), (0, 2), (1, 3), (1, 2))
NETWORK = SORT + tuple((i + 4, j + 4) for i, j in SORT) + ((0, 7), (1, 6), (2, 5), (3, 4))
EARLY = 16
LATE = OWN - EARLY
ORDER = 4
GROUP = 16
BATCH = 16
SPAN = 256
WIDE = GROUP + 8
LONG = SIDE + 8
VMEM = 56 * 1024 * 1024


def dft(length, sign):
    phase = np.outer(np.arange(length), np.arange(length)) % length
    return np.exp(sign * 2j * math.pi * phase / length) / math.sqrt(length)


def twiddles(count, other, sign):
    phase = np.outer(np.arange(count), np.arange(other))
    return np.exp(sign * 2j * math.pi * phase / (count * other))


def from_left(table):
    return np.block([[table.real, -table.imag], [table.imag, table.real]])


def from_right(table):
    return np.block([[table.real, table.imag], [-table.imag, table.real]])


def as_bf16(table):
    return jnp.asarray(np.asarray(table, np.float32).astype(ml_dtypes.bfloat16))


def parts_of(table):
    return jnp.asarray(np.stack([table.real, table.imag]).astype(np.float32))


def times(a, b):
    return (a[0] * b[0] - a[1] * b[1], a[0] * b[1] + a[1] * b[0])


def dot(a, b):
    return jnp.dot(a, b, preferred_element_type=jnp.float32)


def bf16(x):
    return x.astype(jnp.bfloat16)


def swapped(slots, swaps, pairs):
    slots = list(slots)
    for swap, (i, j) in zip(swaps, pairs):
        slots[i], slots[j] = (
            jnp.where(swap, slots[j], slots[i]),
            jnp.where(swap, slots[i], slots[j]),
        )
    return slots


def masks(ref):
    rows = [jnp.broadcast_to(ref[at : at + 1, :], (16, SIDE)) for at in range(len(NETWORK))]
    return [bf16(row) > jnp.bfloat16(0.5) for row in rows]


def plan_kernel(me_ref, near_ref, *refs):
    far_refs, (swap_ref, own_ref, pick_ref) = refs[:3], refs[3:]
    me = me_ref[0]
    lane = lax.broadcasted_iota(jnp.int32, (N_RNG, SIDE), 1)
    device = lax.broadcasted_iota(jnp.int32, (N_RNG, SIDE), 0)
    runs = []
    for chip in range(CHIPS):
        first = jnp.zeros((N_RNG, SIDE), jnp.int32)
        for far, ref in zip((0, *FAR), (near_ref, *far_refs)):
            for at, near in enumerate((0, *NEAR)):
                first = jnp.where(device == (me ^ far ^ near), ref[at * CHIPS + chip], first)
        runs.append(first // SIDE + jnp.where(lane < first % SIDE, 1, 0))
    holds = [[jnp.where(run == slot, 1.0, 0.0) for slot in range(SLOTS)] for run in runs]
    wanted = [functools.reduce(jnp.maximum, [hold[slot] for hold in holds]) for slot in range(SLOTS)]
    for at, (i, j) in enumerate(NETWORK):
        swap = wanted[j] > wanted[i]
        swap_ref[at] = jnp.where(swap, 1.0, 0.0)
        wanted = swapped(wanted, [swap], [(i, j)])
        holds = [swapped(hold, [swap], [(i, j)]) for hold in holds]
    for at in range(len(NETWORK)):
        own_ref[at : at + 1, :] = swap_ref[at, pl.ds(me, 1), :]
    for chip in range(CHIPS):
        for slot in range(HALF):
            at = chip * HALF + slot
            pick_ref[at] = holds[chip][slot]


NEAR = (1, 8, 9)
FAR = (2, 4, 6)


def from_ways(x, axis, size, ways):
    return [lax.ppermute(x, axis, [(i, i ^ way) for i in range(size)]) for way in ways]


def all_bins(chip_bins):
    near = jnp.concatenate([chip_bins] + from_ways(chip_bins, "rng", N_RNG, NEAR))
    return [near] + from_ways(near, "rng", N_RNG, FAR)


def plan(me, bins):
    smem, vmem = pl.BlockSpec(memory_space=pltpu.SMEM), pl.BlockSpec(memory_space=pltpu.VMEM)
    return pl.pallas_call(
        plan_kernel,
        in_specs=[smem] * 5,
        out_specs=[vmem] * 3,
        out_shape=[
            jax.ShapeDtypeStruct((len(NETWORK), N_RNG, SIDE), jnp.float32),
            jax.ShapeDtypeStruct((len(NETWORK) + 2, SIDE), jnp.float32),
            jax.ShapeDtypeStruct((CHIPS * HALF, N_RNG, SIDE), jnp.float32),
        ],
        name="plan",
    )(me, *bins)


def range_kernel(x_ref, h_ref, w_ref, t1_ref, t2_ref, t3_ref, t4_ref, *refs, ordered):
    s = SIDE
    *refs, xs, ys, hs = refs

    @pl.when(pl.program_id(0) == 0)
    def _():
        for part in range(2):
            for j in range(s):
                ys[j : j + 1, :] = h_ref[part : part + 1, j * s : (j + 1) * s]
            hs[part] = ys[:s, :].T

    for part in range(2):
        for n in range(s):
            row = (part * s + n) * WIDE
            xs[row : row + GROUP, :] = x_ref[0, part, :, n * s : (n + 1) * s].astype(jnp.float32)
    w = (w_ref[0], w_ref[1])
    wc = (w[0], -w[1])
    h = (hs[0], hs[1])
    for line in range(0, GROUP, BATCH):
        batch = range(line, line + BATCH)
        x = [
            jnp.concatenate(
                [bf16(xs[pl.ds(part * s * WIDE + one, s, stride=WIDE), :]) for part in (0, 1)],
                axis=0,
            )
            for one in batch
        ]
        y = dot(t1_ref[...], jnp.concatenate(x, axis=1))
        x = []
        for one in range(BATCH):
            cut = y[:, one * s : (one + 1) * s]
            z = times((cut[:s], cut[s:]), w)
            x.append(jnp.concatenate([bf16(z[0]), bf16(z[1])], axis=1))
        y = dot(jnp.concatenate(x, axis=0), t2_ref[...])
        x = []
        for one in range(BATCH):
            cut = y[one * s : (one + 1) * s]
            z = times((cut[:, :s], cut[:, s:]), h)
            x.append(jnp.concatenate([bf16(z[0]), bf16(z[1])], axis=1))
        y = dot(jnp.concatenate(x, axis=0), t3_ref[...])
        x = []
        for one in range(BATCH):
            cut = y[one * s : (one + 1) * s]
            z = times((cut[:, :s], cut[:, s:]), wc)
            x.append(jnp.concatenate([bf16(z[0]), bf16(z[1])], axis=0))
        y = dot(t4_ref[...], jnp.concatenate(x, axis=1))
        for one in range(BATCH):
            for part in (0, 1):
                row = (part * GROUP + line + one) * LONG
                ys[row : row + s, :] = y[
                    part * s : (part + 1) * s, one * s : (one + 1) * s
                ]
    for dest in range(N_RNG):
        if ordered:
            swap_ref, out1_ref, out2_ref = refs
            swaps = masks(swap_ref.at[:, dest])
        else:
            (out_ref,) = refs
        for part in (0, 1):
            slots = []
            for slot in range(SLOTS):
                row = part * GROUP * LONG + dest * SLOTS + slot
                slots.append(bf16(ys[pl.ds(row, GROUP, stride=LONG), :]))
            if not ordered:
                for slot in range(SLOTS):
                    out_ref[dest, part, :, slot * s : (slot + 1) * s] = slots[slot]
                continue
            slots = swapped(slots, swaps, NETWORK)
            for slot in range(HALF):
                lanes = slice(slot * s, (slot + 1) * s)
                out1_ref[dest, part, :, lanes] = slots[slot]
                out2_ref[dest, part, :, lanes] = slots[slot + HALF]


def whole(shape):
    return pl.BlockSpec(shape, lambda *_: (0,) * len(shape))


def compress_range(raw_echoes, range_filter, first, lines, swaps=None):
    forward = dft(SIDE, -1)
    backward = dft(SIDE, 1)
    tables = [
        as_bf16(from_left(forward)),
        as_bf16(from_right(forward)),
        as_bf16(from_right(backward)),
        as_bf16(from_left(backward)),
    ]
    turn = parts_of(twiddles(SIDE, SIDE, -1))
    table = whole((2 * SIDE, 2 * SIDE))
    ordered = swaps is not None
    width, count = (PART, 2) if ordered else (BLOCK, 1)
    outs = pl.pallas_call(
        functools.partial(range_kernel, ordered=ordered),
        grid=(lines // GROUP,),
        in_specs=[
            pl.BlockSpec((1, 2, GROUP, BINS), lambda i: (0, 0, i + first // GROUP, 0)),
            whole((2, BINS)),
            whole((2, SIDE, SIDE)),
            table,
            table,
            table,
            table,
        ]
        + [whole((len(NETWORK), N_RNG, SIDE))] * ordered,
        out_specs=[pl.BlockSpec((N_RNG, 2, GROUP, width), lambda i: (0, 0, i, 0))] * count,
        out_shape=[jax.ShapeDtypeStruct((N_RNG, 2, lines, width), jnp.bfloat16)] * count,
        scratch_shapes=[
            pltpu.VMEM((2 * SIDE * WIDE, SIDE), jnp.float32),
            pltpu.VMEM((2 * LONG * GROUP, SIDE), jnp.float32),
            pltpu.VMEM((2, SIDE, SIDE), jnp.float32),
        ],
        compiler_params=pltpu.CompilerParams(vmem_limit_bytes=VMEM),
        cost_estimate=pl.CostEstimate(flops=4 * 10**9, bytes_accessed=2**22, transcendentals=0),
        name="compress_range",
    )(raw_echoes, range_filter, turn, *tables, *([swaps] * ordered))
    return [out.reshape(N_RNG, 2 * lines, width) for out in outs]


def order_kernel(own_ref, x_ref, out1_ref, out2_ref):
    swaps = masks(own_ref)
    for device in range(ORDER):
        for row in range(0, 2 * EARLY, 16):
            rows = slice(row, row + 16)
            slots = [
                x_ref[device, rows, slot * SIDE : (slot + 1) * SIDE] for slot in range(SLOTS)
            ]
            slots = swapped(slots, swaps, NETWORK)
            for slot in range(HALF):
                lanes = slice(slot * SIDE, (slot + 1) * SIDE)
                out1_ref[device, rows, lanes] = slots[slot]
                out2_ref[device, rows, lanes] = slots[slot + HALF]


def order_bins(own, x):
    return pl.pallas_call(
        order_kernel,
        grid=(N_RNG // ORDER,),
        in_specs=[
            whole((len(NETWORK) + 2, SIDE)),
            pl.BlockSpec((ORDER, 2 * EARLY, BLOCK), lambda i: (i, 0, 0)),
        ],
        out_specs=[pl.BlockSpec((ORDER, 2 * EARLY, PART), lambda i: (i, 0, 0))] * 2,
        out_shape=[jax.ShapeDtypeStruct((N_RNG, 2 * EARLY, PART), jnp.bfloat16)] * 2,
        compiler_params=pltpu.CompilerParams(vmem_limit_bytes=VMEM),
        cost_estimate=pl.CostEstimate(flops=10**7, bytes_accessed=2**22, transcendentals=0),
        name="order_bins",
    )(own, x)


def add(a, b):
    return (a[0] + b[0], a[1] + b[1])


def sub(a, b):
    return (a[0] - b[0], a[1] - b[1])


def fan_dft(x, sign):
    root = math.sqrt(0.5)

    def quarter(a):
        return (-sign * a[1], sign * a[0]) if sign > 0 else (a[1], -a[0])

    def eighth(a):
        if sign > 0:
            return ((a[0] - a[1]) * root, (a[0] + a[1]) * root)
        return ((a[0] + a[1]) * root, (a[1] - a[0]) * root)

    def four(a, b, c, d):
        e, f, g, h = add(a, c), sub(a, c), add(b, d), quarter(sub(b, d))
        return add(e, g), add(f, h), sub(e, g), sub(f, h)

    even = four(x[0], x[2], x[4], x[6])
    odd = four(x[1], x[3], x[5], x[7])
    odd = (odd[0], eighth(odd[1]), quarter(odd[2]), quarter(eighth(odd[3])))
    return [add(p, q) for p, q in zip(even, odd)] + [sub(p, q) for p, q in zip(even, odd)]


def azimuth_step(a_ref, b_ref, f_ref, w_ref, t5_ref, t6_ref, spread, mixed, put):
    m = LINES // FAN
    tiles = [(t, slice(lane * 128, (lane + 1) * 128)) for t in range(m // 16) for lane in range(SPAN // 128)]
    for tile, lanes in tiles:
        half, line = divmod(tile * 16, OWN)
        points = []
        for n in range(FAN):
            ref, row, lines = (a_ref, line, EARLY) if line < EARLY else (b_ref, line - EARLY, LATE)
            rows = [slice(part * lines + row, part * lines + row + 16) for part in (0, 1)]
            points.append(tuple(ref[2 * n + half, row, lanes].astype(jnp.float32) for row in rows))
        for k, value in enumerate(fan_dft(points, -1)):
            if k:
                row = k * m + tile * 16
                value = times(value, (w_ref[0, row : row + 16], w_ref[1, row : row + 16]))
            for part in (0, 1):
                row = (half * 2 + part) * OWN + line
                at = k * SPAN + lanes.start
                spread[row : row + 16, at : at + 128] = bf16(value[part])
    y = dot(t5_ref[...], spread[...])
    x = []
    for k in range(FAN):
        cut = y[:, k * SPAN : (k + 1) * SPAN]
        f = (f_ref[k, 0].astype(jnp.float32), f_ref[k, 1].astype(jnp.float32))
        z = times((cut[:m], cut[m:]), f)
        x.append(jnp.concatenate([bf16(z[0]), bf16(z[1])], axis=0))
    mixed[...] = dot(t6_ref[...], jnp.concatenate(x, axis=1))
    for tile, lanes in tiles:
        points = []
        for k in range(FAN):
            at = k * SPAN + lanes.start
            row = tile * 16
            value = tuple(mixed[part * m + row : part * m + row + 16, at : at + 128] for part in (0, 1))
            if k:
                row += k * m
                value = times(value, (w_ref[0, row : row + 16], -w_ref[1, row : row + 16]))
            points.append(value)
        for p, value in enumerate(fan_dft(points, 1)):
            row = p * m + tile * 16
            for part in (0, 1):
                put(part, row, lanes, bf16(value[part]))


ROWS = WIN + 16
STEPS = PART // SPAN


def azimuth_kernel(
    me_ref, date_ref, lines_ref, bins_ref, pick_ref, a_ref, b_ref, f_ref, w_ref, t5_ref, t6_ref, *refs
):
    out_ref, *outs, slices, spread, mixed, held = refs
    step = pl.program_id(0)

    def put(part, row, lanes, value):
        out_ref[part, row : row + 16, lanes] = value
        held[step, part, row : row + 16, lanes] = value

    azimuth_step(a_ref, b_ref, f_ref, w_ref, t5_ref, t6_ref, spread, mixed, put)

    @pl.when(step == STEPS - 1)
    def _():
        me, date = me_ref[0], date_ref[0]
        for chip in range(CHIPS):
            line = lines_ref[chip]
            row = jnp.minimum(line // 16 * 16, LINES - ROWS)
            picks = [pick_ref[chip * HALF + slot, pl.ds(me, 1), :] > 0.5 for slot in range(HALF)]
            for part in (0, 1):
                for slot in range(HALF):
                    at, lane = divmod(slot * SIDE, SPAN)
                    other = held[at, part, pl.ds(pl.multiple_of(row, 16), ROWS), lane : lane + SIDE]
                    other = other.astype(jnp.float32)
                    cut = jnp.where(picks[slot], other, cut) if slot else other
                cut = pltpu.roll(cut, lax.rem(ROWS - (line - row), ROWS), 0)[:WIN]
                cut = pltpu.roll(cut, lax.rem(WIN - lax.rem(bins_ref[chip], WIN), WIN), 1)
                slices[chip * 2 + part] = bf16(cut)
        for way in range(CHIPS):
            for part in (0, 1):
                outs[way][part] = slices[2 * (way ^ (date // 2)) + part]


def azimuth_tables():
    m = LINES // FAN
    forward = np.exp(-2j * math.pi * np.outer(np.arange(m), np.arange(m)) / m) / math.sqrt(LINES)
    backward = forward.conj()
    first = from_left(forward).reshape(2 * m, 2, 2, OWN).transpose(0, 2, 1, 3).reshape(2 * m, 2 * m)
    turn = twiddles(FAN, m, -1).reshape(LINES, 1) * np.ones((1, 128))
    return parts_of(turn), as_bf16(first), as_bf16(from_left(backward))


AZIMUTH_SCRATCH = [
    pltpu.VMEM((2 * LINES // FAN, FAN * SPAN), jnp.bfloat16),
    pltpu.VMEM((2 * LINES // FAN, FAN * SPAN), jnp.float32),
]


def focus_azimuth(me, date, chip_lines, chip_bins, picks, early, late, response):
    m = LINES // FAN
    table = whole((2 * m, 2 * m))
    smem = pl.BlockSpec(memory_space=pltpu.SMEM)
    counts = (2, 2, 2, 2, 2 * CHIPS)
    return pl.pallas_call(
        azimuth_kernel,
        grid=(STEPS,),
        in_specs=[
            smem,
            smem,
            smem,
            smem,
            whole((CHIPS * HALF, N_RNG, SIDE)),
            pl.BlockSpec((N_RNG, 2 * EARLY, SPAN), lambda i: (0, 0, i)),
            pl.BlockSpec((N_RNG, 2 * LATE, SPAN), lambda i: (0, 0, i)),
            pl.BlockSpec((FAN, 2, m, SPAN), lambda i: (0, 0, 0, i)),
            whole((2, LINES, 128)),
            table,
            table,
        ],
        out_specs=[pl.BlockSpec((2, LINES, SPAN), lambda i: (0, 0, i))]
        + [whole((count, WIN, WIN)) for count in counts],
        out_shape=[jax.ShapeDtypeStruct((2, LINES, PART), jnp.bfloat16)]
        + [jax.ShapeDtypeStruct((count, WIN, WIN), jnp.bfloat16) for count in counts],
        scratch_shapes=AZIMUTH_SCRATCH + [pltpu.VMEM((STEPS, 2, LINES, SPAN), jnp.bfloat16)],
        compiler_params=pltpu.CompilerParams(vmem_limit_bytes=VMEM),
        name="focus_azimuth",
    )(me, date, chip_lines, chip_bins, picks, early, late, response, *azimuth_tables())


def regroup_kernel(f_ref, own_ref, out1_ref, out2_ref, wide):
    swaps = masks(own_ref)
    for part in (0, 1):
        for slot in range(SLOTS):
            wide[slot] = f_ref[part, :, slot * SIDE : (slot + 1) * SIDE].astype(jnp.float32)
        for k in range(FAN):
            slots = [bf16(wide[slot, pl.ds(k, 16, stride=FAN), :]) for slot in range(SLOTS)]
            slots = swapped(slots, swaps, NETWORK)
            for slot in range(HALF):
                lanes = slice(slot * SIDE, (slot + 1) * SIDE)
                out1_ref[k, part, :, lanes] = slots[slot]
                out2_ref[k, part, :, lanes] = slots[slot + HALF]


def regroup_filter(azimuth_filter, own):
    m = LINES // FAN
    return pl.pallas_call(
        regroup_kernel,
        grid=(FAN,),
        in_specs=[
            pl.BlockSpec((2, 16 * FAN, BLOCK), lambda i: (0, i, 0)),
            whole((len(NETWORK) + 2, SIDE)),
        ],
        out_specs=[pl.BlockSpec((FAN, 2, 16, PART), lambda i: (0, 0, i, 0))] * 2,
        out_shape=[jax.ShapeDtypeStruct((FAN, 2, m, PART), jnp.bfloat16)] * 2,
        scratch_shapes=[pltpu.VMEM((SLOTS, 16 * FAN, SIDE), jnp.float32)],
        compiler_params=pltpu.CompilerParams(vmem_limit_bytes=VMEM),
        cost_estimate=pl.CostEstimate(flops=10**7, bytes_accessed=2**23, transcendentals=0),
        name="regroup_filter",
    )(azimuth_filter, own)


MERGE = 256


def finish_kernel(
    own_ref, a_ref, b_ref, f_ref, w_ref, t5_ref, t6_ref, first_ref, out_ref, spread, mixed, held
):
    step = pl.program_id(0)

    @pl.when(step < STEPS)
    def _():
        def put(part, row, lanes, value):
            held[step, part, row : row + 16, lanes] = value

        azimuth_step(a_ref, b_ref, f_ref, w_ref, t5_ref, t6_ref, spread, mixed, put)

    @pl.when(step >= STEPS)
    def _():
        swaps = masks(own_ref)
        first = (step - STEPS) * MERGE
        for part in (0, 1):
            for row in range(0, MERGE, 16):
                rows = slice(row, row + 16)
                slots = [
                    first_ref[part, rows, slot * SIDE : (slot + 1) * SIDE] for slot in range(HALF)
                ]
                for slot in range(HALF):
                    at, lane = divmod(slot * SIDE, SPAN)
                    from_row = pl.ds(pl.multiple_of(first + row, 16), 16)
                    slots.append(held[at, part, from_row, lane : lane + SIDE])
                slots = swapped(slots, swaps[::-1], NETWORK[::-1])
                for slot in range(SLOTS):
                    out_ref[0, part, rows, slot * SIDE : (slot + 1) * SIDE] = slots[slot]


def finish(own, early, late, response, image):
    m = LINES // FAN
    table = whole((2 * m, 2 * m))
    return pl.pallas_call(
        finish_kernel,
        grid=(STEPS + LINES // MERGE,),
        in_specs=[
            whole((len(NETWORK) + 2, SIDE)),
            pl.BlockSpec((N_RNG, 2 * EARLY, SPAN), lambda i: (0, 0, jnp.minimum(i, STEPS - 1))),
            pl.BlockSpec((N_RNG, 2 * LATE, SPAN), lambda i: (0, 0, jnp.minimum(i, STEPS - 1))),
            pl.BlockSpec((FAN, 2, m, SPAN), lambda i: (0, 0, 0, jnp.minimum(i, STEPS - 1))),
            whole((2, LINES, 128)),
            table,
            table,
            pl.BlockSpec((2, MERGE, PART), lambda i: (0, jnp.maximum(i - STEPS, 0), 0)),
        ],
        out_specs=pl.BlockSpec(
            (1, 2, MERGE, BLOCK), lambda i: (0, 0, jnp.maximum(i - STEPS, 0), 0)
        ),
        out_shape=jax.ShapeDtypeStruct((1, 2, LINES, BLOCK), jnp.bfloat16),
        scratch_shapes=AZIMUTH_SCRATCH + [pltpu.VMEM((STEPS, 2, LINES, SPAN), jnp.bfloat16)],
        compiler_params=pltpu.CompilerParams(vmem_limit_bytes=VMEM),
        name="finish",
    )(own, early, late, response, *azimuth_tables(), image)


def pass_kernel(date_ref, mate_ref, *refs):
    ins, outs, (held,) = refs[:DATES], refs[DATES : DATES + CHIPS], refs[DATES + CHIPS :]
    date = date_ref[0]
    for way in range(CHIPS):
        for other in (0, 1):
            held[2 * way + other] = ins[CHIPS * other + way][...]
    for way in range(CHIPS):
        outs[way][...] = held[mate_ref[(2 * way) ^ date] ^ date]


def pass_on(date, partner_date, held):
    smem, vmem = pl.BlockSpec(memory_space=pltpu.SMEM), pl.BlockSpec(memory_space=pltpu.VMEM)
    return pl.pallas_call(
        pass_kernel,
        in_specs=[smem] * 2 + [vmem] * DATES,
        out_specs=[vmem] * CHIPS,
        out_shape=[jax.ShapeDtypeStruct((2, WIN, WIN), jnp.bfloat16)] * CHIPS,
        scratch_shapes=[pltpu.VMEM((DATES, 2, WIN, WIN), jnp.bfloat16)],
        name="pass_on",
    )(date, partner_date, *held)


def along_y(chips):
    return [chips[0]] + [from_ways(chips[way], "date", DATES, (2 * way,))[0] for way in (1, 2, 3)]


def exchange(date, partner_date, chips):
    held = along_y(chips)
    held += [from_ways(chip, "date", DATES, (1,))[0] for chip in held]
    return along_y(pass_on(date, partner_date, held))


def transform(stacked, left, right):
    y = dot(left, jnp.concatenate(stacked, axis=1))
    half = y.shape[0] // 2
    rows = []
    for chip in range(CHIPS):
        cut = y[:, chip * WIN : (chip + 1) * WIN]
        rows.append(jnp.concatenate([bf16(cut[:half]), bf16(cut[half:])], axis=1))
    return dot(jnp.concatenate(rows, axis=0), right)


def correlate_kernel(
    date_ref, offsets_ref, own_ref, left_ref, right_ref, left3_ref, right3_ref, *refs
):
    ins, (out_ref, their_ref) = refs[:CHIPS], refs[CHIPS:]
    for way in range(CHIPS):
        their_ref[way ^ (date_ref[0] // 2)] = ins[way][...]
    left, right = left_ref[...], right_ref[...]
    inside = lax.broadcasted_iota(jnp.int32, (CHIP, WIN), 1) < CHIP
    empty = jnp.zeros((WIN - CHIP, WIN), jnp.bfloat16)
    primary = []
    for chip in range(CHIPS):
        row, col = offsets_ref[2 * chip], offsets_ref[2 * chip + 1]
        pieces = []
        for part in (0, 1):
            cut = own_ref[chip * 2 + part].astype(jnp.float32)
            cut = pltpu.roll(cut, lax.rem(WIN - row, WIN), 0)[:CHIP]
            cut = pltpu.roll(cut, lax.rem(WIN - col, WIN), 1)
            pieces += [bf16(jnp.where(inside, cut, 0.0)), empty]
        primary.append(jnp.concatenate(pieces, axis=0))
    first = transform(primary, left, right)
    second = transform(
        [jnp.concatenate([their_ref[chip, 0], their_ref[chip, 1]], axis=0) for chip in range(CHIPS)],
        left,
        right,
    )
    a = (first[:, :WIN], first[:, WIN:])
    b = (second[:, :WIN], second[:, WIN:])
    product = (a[0] * b[0] + a[1] * b[1], a[1] * b[0] - a[0] * b[1])
    product = [bf16(part) for part in product]
    surface = transform(
        [
            jnp.concatenate([part[chip * WIN : (chip + 1) * WIN] for part in product], axis=0)
            for chip in range(CHIPS)
        ],
        left3_ref[...],
        right3_ref[...],
    )
    for chip in range(CHIPS):
        out_ref[0, chip] = surface[chip * CHIP : (chip + 1) * CHIP]


def correlate(date, offsets, own, theirs):
    table = dft(WIN, -1)
    left, right = from_left(table), from_right(table)
    factor = WIN // CHIP
    keep = np.concatenate([np.arange(CHIP), WIN + np.arange(CHIP)])
    vmem = pl.BlockSpec(memory_space=pltpu.VMEM)
    return pl.pallas_call(
        correlate_kernel,
        in_specs=[pl.BlockSpec(memory_space=pltpu.SMEM)] * 2 + [vmem] * (5 + CHIPS),
        out_specs=vmem,
        out_shape=jax.ShapeDtypeStruct((1, CHIPS, CHIP, 2 * CHIP), jnp.float32),
        scratch_shapes=[pltpu.VMEM((CHIPS, 2, WIN, WIN), jnp.bfloat16)],
        compiler_params=pltpu.CompilerParams(vmem_limit_bytes=VMEM),
        name="correlate",
    )(
        date,
        offsets,
        own,
        as_bf16(left),
        as_bf16(right),
        as_bf16(left[keep]),
        as_bf16(right[:, keep] * factor),
        *theirs,
    )


def to_blocks(x):
    return lax.all_to_all(x, "rng", split_axis=0, concat_axis=0, tiled=True)


def local(
    raw_echoes, range_filter, azimuth_filter, partner_date, chip_lines, chip_bins, chip_offsets
):
    me = lax.axis_index("rng").astype(jnp.int32).reshape(1)
    date = lax.axis_index("date").astype(jnp.int32).reshape(1)
    bins = all_bins(chip_bins)
    (early,) = compress_range(raw_echoes, range_filter, 0, EARLY)
    early, bins, offsets = lax.optimization_barrier((early, bins, chip_offsets.reshape(-1)))
    early = to_blocks(early)
    swaps, own, picks = plan(me, bins)
    late, late_two = compress_range(raw_echoes, range_filter, EARLY, LATE, swaps)
    late, own, early = lax.optimization_barrier((late, own, early))
    late = to_blocks(late)
    early, early_two = order_bins(own, early)
    response, response_two = regroup_filter(azimuth_filter, own)
    late_two, early, early_two, response, response_two = lax.optimization_barrier(
        (late_two, early, early_two, response, response_two)
    )
    late_two = to_blocks(late_two)
    first, *chips, windows = focus_azimuth(
        me, date, chip_lines, chip_bins, picks, early, late, response
    )
    theirs = exchange(date, partner_date, chips)
    correlation = correlate(date, offsets, windows, theirs)
    return (finish(own, early_two, late_two, response_two, first), correlation)


def solution(mesh):
    in_specs = (
        P("date", None, "rng", None),
        P(),
        P(None, None, "rng"),
        P(),
        P("rng"),
        P("rng"),
        P("rng", None),
    )
    out_specs = (P("date", None, None, "rng"), P("date", "rng", None, None))
    return jax.shard_map(local, mesh=mesh, in_specs=in_specs, out_specs=out_specs, check_vma=False)
```

```python
import functools
import math

import jax
import jax.numpy as jnp
import ml_dtypes
import numpy as np
from jax import lax
from jax.experimental import pallas as pl
from jax.experimental.pallas import tpu as pltpu
from jax.sharding import PartitionSpec as P

LINES = 1024
BINS = 16384
CHIP = 64
CHIPS = 4
WIN = 128
DATES = 8
N_RNG = 16
SIDE = 128
FAN = 8
BLOCK = BINS // N_RNG
OWN = LINES // N_RNG
SLOTS = 8
HALF = 4
PART = HALF * 128
SORT = ((0, 1), (2, 3), (0, 2), (1, 3), (1, 2))
NETWORK = SORT + tuple((i + 4, j + 4) for i, j in SORT) + ((0, 7), (1, 6), (2, 5), (3, 4))
EARLY = 16
LATE = OWN - EARLY
ORDER = 4
GROUP = 16
BATCH = 16
SPAN = 256
WIDE = GROUP + 8
LONG = SIDE + 8
VMEM = 56 * 1024 * 1024


def dft(length, sign):
    phase = np.outer(np.arange(length), np.arange(length)) % length
    return np.exp(sign * 2j * math.pi * phase / length) / math.sqrt(length)


def twiddles(count, other, sign):
    phase = np.outer(np.arange(count), np.arange(other))
    return np.exp(sign * 2j * math.pi * phase / (count * other))


def from_left(table):
    return np.block([[table.real, -table.imag], [table.imag, table.real]])


def from_right(table):
    return np.block([[table.real, table.imag], [-table.imag, table.real]])


def as_bf16(table):
    return jnp.asarray(np.asarray(table, np.float32).astype(ml_dtypes.bfloat16))


def parts_of(table):
    return jnp.asarray(np.stack([table.real, table.imag]).astype(np.float32))


def times(a, b):
    return (a[0] * b[0] - a[1] * b[1], a[0] * b[1] + a[1] * b[0])


def dot(a, b):
    return jnp.dot(a, b, preferred_element_type=jnp.float32)


def bf16(x):
    return x.astype(jnp.bfloat16)


def swapped(slots, swaps, pairs):
    slots = list(slots)
    for swap, (i, j) in zip(swaps, pairs):
        slots[i], slots[j] = (
            jnp.where(swap, slots[j], slots[i]),
            jnp.where(swap, slots[i], slots[j]),
        )
    return slots


def masks(ref):
    rows = [jnp.broadcast_to(ref[at : at + 1, :], (16, SIDE)) for at in range(len(NETWORK))]
    return [bf16(row) > jnp.bfloat16(0.5) for row in rows]


def plan_kernel(me_ref, near_ref, *refs):
    far_refs, (swap_ref, own_ref, pick_ref) = refs[:3], refs[3:]
    me = me_ref[0]
    lane = lax.broadcasted_iota(jnp.int32, (N_RNG, SIDE), 1)
    device = lax.broadcasted_iota(jnp.int32, (N_RNG, SIDE), 0)
    runs = []
    for chip in range(CHIPS):
        first = jnp.zeros((N_RNG, SIDE), jnp.int32)
        for far, ref in zip((0, *FAR), (near_ref, *far_refs)):
            for at, near in enumerate((0, *NEAR)):
                first = jnp.where(device == (me ^ far ^ near), ref[at * CHIPS + chip], first)
        runs.append(first // SIDE + jnp.where(lane < first % SIDE, 1, 0))
    holds = [[jnp.where(run == slot, 1.0, 0.0) for slot in range(SLOTS)] for run in runs]
    wanted = [functools.reduce(jnp.maximum, [hold[slot] for hold in holds]) for slot in range(SLOTS)]
    for at, (i, j) in enumerate(NETWORK):
        swap = wanted[j] > wanted[i]
        swap_ref[at] = jnp.where(swap, 1.0, 0.0)
        wanted = swapped(wanted, [swap], [(i, j)])
        holds = [swapped(hold, [swap], [(i, j)]) for hold in holds]
    for at in range(len(NETWORK)):
        own_ref[at : at + 1, :] = swap_ref[at, pl.ds(me, 1), :]
    for chip in range(CHIPS):
        for slot in range(HALF):
            at = chip * HALF + slot
            pick_ref[at] = holds[chip][slot]


NEAR = (1, 8, 9)
FAR = (2, 4, 6)


def from_ways(x, axis, size, ways):
    return [lax.ppermute(x, axis, [(i, i ^ way) for i in range(size)]) for way in ways]


def all_bins(chip_bins):
    near = jnp.concatenate([chip_bins] + from_ways(chip_bins, "rng", N_RNG, NEAR))
    return [near] + from_ways(near, "rng", N_RNG, FAR)


def plan(me, bins):
    smem, vmem = pl.BlockSpec(memory_space=pltpu.SMEM), pl.BlockSpec(memory_space=pltpu.VMEM)
    return pl.pallas_call(
        plan_kernel,
        in_specs=[smem] * 5,
        out_specs=[vmem] * 3,
        out_shape=[
            jax.ShapeDtypeStruct((len(NETWORK), N_RNG, SIDE), jnp.float32),
            jax.ShapeDtypeStruct((len(NETWORK) + 2, SIDE), jnp.float32),
            jax.ShapeDtypeStruct((CHIPS * HALF, N_RNG, SIDE), jnp.float32),
        ],
        name="plan",
    )(me, *bins)


def range_kernel(x_ref, h_ref, w_ref, t1_ref, t2_ref, t3_ref, t4_ref, *refs, ordered):
    s = SIDE
    *refs, xs, ys, hs = refs

    @pl.when(pl.program_id(0) == 0)
    def _():
        for part in range(2):
            for j in range(s):
                ys[j : j + 1, :] = h_ref[part : part + 1, j * s : (j + 1) * s]
            hs[part] = ys[:s, :].T

    for part in range(2):
        for n in range(s):
            row = (part * s + n) * WIDE
            xs[row : row + GROUP, :] = x_ref[0, part, :, n * s : (n + 1) * s].astype(jnp.float32)
    w = (w_ref[0], w_ref[1])
    wc = (w[0], -w[1])
    h = (hs[0], hs[1])
    for line in range(0, GROUP, BATCH):
        batch = range(line, line + BATCH)
        x = [
            jnp.concatenate(
                [bf16(xs[pl.ds(part * s * WIDE + one, s, stride=WIDE), :]) for part in (0, 1)],
                axis=0,
            )
            for one in batch
        ]
        y = dot(t1_ref[...], jnp.concatenate(x, axis=1))
        x = []
        for one in range(BATCH):
            cut = y[:, one * s : (one + 1) * s]
            z = times((cut[:s], cut[s:]), w)
            x.append(jnp.concatenate([bf16(z[0]), bf16(z[1])], axis=1))
        y = dot(jnp.concatenate(x, axis=0), t2_ref[...])
        x = []
        for one in range(BATCH):
            cut = y[one * s : (one + 1) * s]
            z = times((cut[:, :s], cut[:, s:]), h)
            x.append(jnp.concatenate([bf16(z[0]), bf16(z[1])], axis=1))
        y = dot(jnp.concatenate(x, axis=0), t3_ref[...])
        x = []
        for one in range(BATCH):
            cut = y[one * s : (one + 1) * s]
            z = times((cut[:, :s], cut[:, s:]), wc)
            x.append(jnp.concatenate([bf16(z[0]), bf16(z[1])], axis=0))
        y = dot(t4_ref[...], jnp.concatenate(x, axis=1))
        for one in range(BATCH):
            for part in (0, 1):
                row = (part * GROUP + line + one) * LONG
                ys[row : row + s, :] = y[
                    part * s : (part + 1) * s, one * s : (one + 1) * s
                ]
    for dest in range(N_RNG):
        if ordered:
            swap_ref, out1_ref, out2_ref = refs
            swaps = masks(swap_ref.at[:, dest])
        else:
            (out_ref,) = refs
        for part in (0, 1):
            slots = []
            for slot in range(SLOTS):
                row = part * GROUP * LONG + dest * SLOTS + slot
                slots.append(bf16(ys[pl.ds(row, GROUP, stride=LONG), :]))
            if not ordered:
                for slot in range(SLOTS):
                    out_ref[dest, part, :, slot * s : (slot + 1) * s] = slots[slot]
                continue
            slots = swapped(slots, swaps, NETWORK)
            for slot in range(HALF):
                lanes = slice(slot * s, (slot + 1) * s)
                out1_ref[dest, part, :, lanes] = slots[slot]
                out2_ref[dest, part, :, lanes] = slots[slot + HALF]


def whole(shape):
    return pl.BlockSpec(shape, lambda *_: (0,) * len(shape))


def compress_range(raw_echoes, range_filter, first, lines, swaps=None):
    forward = dft(SIDE, -1)
    backward = dft(SIDE, 1)
    tables = [
        as_bf16(from_left(forward)),
        as_bf16(from_right(forward)),
        as_bf16(from_right(backward)),
        as_bf16(from_left(backward)),
    ]
    turn = parts_of(twiddles(SIDE, SIDE, -1))
    table = whole((2 * SIDE, 2 * SIDE))
    ordered = swaps is not None
    width, count = (PART, 2) if ordered else (BLOCK, 1)
    outs = pl.pallas_call(
        functools.partial(range_kernel, ordered=ordered),
        grid=(lines // GROUP,),
        in_specs=[
            pl.BlockSpec((1, 2, GROUP, BINS), lambda i: (0, 0, i + first // GROUP, 0)),
            whole((2, BINS)),
            whole((2, SIDE, SIDE)),
            table,
            table,
            table,
            table,
        ]
        + [whole((len(NETWORK), N_RNG, SIDE))] * ordered,
        out_specs=[pl.BlockSpec((N_RNG, 2, GROUP, width), lambda i: (0, 0, i, 0))] * count,
        out_shape=[jax.ShapeDtypeStruct((N_RNG, 2, lines, width), jnp.bfloat16)] * count,
        scratch_shapes=[
            pltpu.VMEM((2 * SIDE * WIDE, SIDE), jnp.float32),
            pltpu.VMEM((2 * LONG * GROUP, SIDE), jnp.float32),
            pltpu.VMEM((2, SIDE, SIDE), jnp.float32),
        ],
        compiler_params=pltpu.CompilerParams(vmem_limit_bytes=VMEM),
        cost_estimate=pl.CostEstimate(flops=4 * 10**9, bytes_accessed=2**22, transcendentals=0),
        name="compress_range",
    )(raw_echoes, range_filter, turn, *tables, *([swaps] * ordered))
    return [out.reshape(N_RNG, 2 * lines, width) for out in outs]


def order_kernel(own_ref, x_ref, out1_ref, out2_ref):
    swaps = masks(own_ref)
    for device in range(ORDER):
        for row in range(0, 2 * EARLY, 16):
            rows = slice(row, row + 16)
            slots = [
                x_ref[device, rows, slot * SIDE : (slot + 1) * SIDE] for slot in range(SLOTS)
            ]
            slots = swapped(slots, swaps, NETWORK)
            for slot in range(HALF):
                lanes = slice(slot * SIDE, (slot + 1) * SIDE)
                out1_ref[device, rows, lanes] = slots[slot]
                out2_ref[device, rows, lanes] = slots[slot + HALF]


def order_bins(own, x):
    return pl.pallas_call(
        order_kernel,
        grid=(N_RNG // ORDER,),
        in_specs=[
            whole((len(NETWORK) + 2, SIDE)),
            pl.BlockSpec((ORDER, 2 * EARLY, BLOCK), lambda i: (i, 0, 0)),
        ],
        out_specs=[pl.BlockSpec((ORDER, 2 * EARLY, PART), lambda i: (i, 0, 0))] * 2,
        out_shape=[jax.ShapeDtypeStruct((N_RNG, 2 * EARLY, PART), jnp.bfloat16)] * 2,
        compiler_params=pltpu.CompilerParams(vmem_limit_bytes=VMEM),
        cost_estimate=pl.CostEstimate(flops=10**7, bytes_accessed=2**22, transcendentals=0),
        name="order_bins",
    )(own, x)


def add(a, b):
    return (a[0] + b[0], a[1] + b[1])


def sub(a, b):
    return (a[0] - b[0], a[1] - b[1])


def fan_dft(x, sign):
    root = math.sqrt(0.5)

    def quarter(a):
        return (-sign * a[1], sign * a[0]) if sign > 0 else (a[1], -a[0])

    def eighth(a):
        if sign > 0:
            return ((a[0] - a[1]) * root, (a[0] + a[1]) * root)
        return ((a[0] + a[1]) * root, (a[1] - a[0]) * root)

    def four(a, b, c, d):
        e, f, g, h = add(a, c), sub(a, c), add(b, d), quarter(sub(b, d))
        return add(e, g), add(f, h), sub(e, g), sub(f, h)

    even = four(x[0], x[2], x[4], x[6])
    odd = four(x[1], x[3], x[5], x[7])
    odd = (odd[0], eighth(odd[1]), quarter(odd[2]), quarter(eighth(odd[3])))
    return [add(p, q) for p, q in zip(even, odd)] + [sub(p, q) for p, q in zip(even, odd)]


def azimuth_step(a_ref, b_ref, f_ref, w_ref, t5_ref, t6_ref, spread, mixed, put):
    m = LINES // FAN
    tiles = [(t, slice(lane * 128, (lane + 1) * 128)) for t in range(m // 16) for lane in range(SPAN // 128)]
    for tile, lanes in tiles:
        half, line = divmod(tile * 16, OWN)
        points = []
        for n in range(FAN):
            ref, row, lines = (a_ref, line, EARLY) if line < EARLY else (b_ref, line - EARLY, LATE)
            rows = [slice(part * lines + row, part * lines + row + 16) for part in (0, 1)]
            points.append(tuple(ref[2 * n + half, row, lanes].astype(jnp.float32) for row in rows))
        for k, value in enumerate(fan_dft(points, -1)):
            if k:
                row = k * m + tile * 16
                value = times(value, (w_ref[0, row : row + 16], w_ref[1, row : row + 16]))
            for part in (0, 1):
                row = (half * 2 + part) * OWN + line
                at = k * SPAN + lanes.start
                spread[row : row + 16, at : at + 128] = bf16(value[part])
    y = dot(t5_ref[...], spread[...])
    x = []
    for k in range(FAN):
        cut = y[:, k * SPAN : (k + 1) * SPAN]
        f = (f_ref[k, 0].astype(jnp.float32), f_ref[k, 1].astype(jnp.float32))
        z = times((cut[:m], cut[m:]), f)
        x.append(jnp.concatenate([bf16(z[0]), bf16(z[1])], axis=0))
    mixed[...] = dot(t6_ref[...], jnp.concatenate(x, axis=1))
    for tile, lanes in tiles:
        points = []
        for k in range(FAN):
            at = k * SPAN + lanes.start
            row = tile * 16
            value = tuple(mixed[part * m + row : part * m + row + 16, at : at + 128] for part in (0, 1))
            if k:
                row += k * m
                value = times(value, (w_ref[0, row : row + 16], -w_ref[1, row : row + 16]))
            points.append(value)
        for p, value in enumerate(fan_dft(points, 1)):
            row = p * m + tile * 16
            for part in (0, 1):
                put(part, row, lanes, bf16(value[part]))


ROWS = WIN + 16
STEPS = PART // SPAN


def azimuth_kernel(
    me_ref, date_ref, lines_ref, bins_ref, pick_ref, a_ref, b_ref, f_ref, w_ref, t5_ref, t6_ref, *refs
):
    out_ref, *outs, slices, spread, mixed, held = refs
    step = pl.program_id(0)

    def put(part, row, lanes, value):
        out_ref[part, row : row + 16, lanes] = value
        held[step, part, row : row + 16, lanes] = value

    azimuth_step(a_ref, b_ref, f_ref, w_ref, t5_ref, t6_ref, spread, mixed, put)

    @pl.when(step == STEPS - 1)
    def _():
        me, date = me_ref[0], date_ref[0]
        for chip in range(CHIPS):
            line = lines_ref[chip]
            row = jnp.minimum(line // 16 * 16, LINES - ROWS)
            picks = [pick_ref[chip * HALF + slot, pl.ds(me, 1), :] > 0.5 for slot in range(HALF)]
            for part in (0, 1):
                for slot in range(HALF):
                    at, lane = divmod(slot * SIDE, SPAN)
                    other = held[at, part, pl.ds(pl.multiple_of(row, 16), ROWS), lane : lane + SIDE]
                    other = other.astype(jnp.float32)
                    cut = jnp.where(picks[slot], other, cut) if slot else other
                cut = pltpu.roll(cut, lax.rem(ROWS - (line - row), ROWS), 0)[:WIN]
                cut = pltpu.roll(cut, lax.rem(WIN - lax.rem(bins_ref[chip], WIN), WIN), 1)
                slices[chip * 2 + part] = bf16(cut)
        for way in range(CHIPS):
            for part in (0, 1):
                outs[way][part] = slices[2 * (way ^ (date // 2)) + part]


def azimuth_tables():
    m = LINES // FAN
    forward = np.exp(-2j * math.pi * np.outer(np.arange(m), np.arange(m)) / m) / math.sqrt(LINES)
    backward = forward.conj()
    first = from_left(forward).reshape(2 * m, 2, 2, OWN).transpose(0, 2, 1, 3).reshape(2 * m, 2 * m)
    turn = twiddles(FAN, m, -1).reshape(LINES, 1) * np.ones((1, 128))
    return parts_of(turn), as_bf16(first), as_bf16(from_left(backward))


AZIMUTH_SCRATCH = [
    pltpu.VMEM((2 * LINES // FAN, FAN * SPAN), jnp.bfloat16),
    pltpu.VMEM((2 * LINES // FAN, FAN * SPAN), jnp.float32),
]


def focus_azimuth(me, date, chip_lines, chip_bins, picks, early, late, response):
    m = LINES // FAN
    table = whole((2 * m, 2 * m))
    smem = pl.BlockSpec(memory_space=pltpu.SMEM)
    counts = (2, 2, 2, 2, 2 * CHIPS)
    return pl.pallas_call(
        azimuth_kernel,
        grid=(STEPS,),
        in_specs=[
            smem,
            smem,
            smem,
            smem,
            whole((CHIPS * HALF, N_RNG, SIDE)),
            pl.BlockSpec((N_RNG, 2 * EARLY, SPAN), lambda i: (0, 0, i)),
            pl.BlockSpec((N_RNG, 2 * LATE, SPAN), lambda i: (0, 0, i)),
            pl.BlockSpec((FAN, 2, m, SPAN), lambda i: (0, 0, 0, i)),
            whole((2, LINES, 128)),
            table,
            table,
        ],
        out_specs=[pl.BlockSpec((2, LINES, SPAN), lambda i: (0, 0, i))]
        + [whole((count, WIN, WIN)) for count in counts],
        out_shape=[jax.ShapeDtypeStruct((2, LINES, PART), jnp.bfloat16)]
        + [jax.ShapeDtypeStruct((count, WIN, WIN), jnp.bfloat16) for count in counts],
        scratch_shapes=AZIMUTH_SCRATCH + [pltpu.VMEM((STEPS, 2, LINES, SPAN), jnp.bfloat16)],
        compiler_params=pltpu.CompilerParams(vmem_limit_bytes=VMEM),
        name="focus_azimuth",
    )(me, date, chip_lines, chip_bins, picks, early, late, response, *azimuth_tables())


def regroup_kernel(f_ref, own_ref, out1_ref, out2_ref, wide):
    swaps = masks(own_ref)
    for part in (0, 1):
        for slot in range(SLOTS):
            wide[slot] = f_ref[part, :, slot * SIDE : (slot + 1) * SIDE].astype(jnp.float32)
        for k in range(FAN):
            slots = [bf16(wide[slot, pl.ds(k, 16, stride=FAN), :]) for slot in range(SLOTS)]
            slots = swapped(slots, swaps, NETWORK)
            for slot in range(HALF):
                lanes = slice(slot * SIDE, (slot + 1) * SIDE)
                out1_ref[k, part, :, lanes] = slots[slot]
                out2_ref[k, part, :, lanes] = slots[slot + HALF]


def regroup_filter(azimuth_filter, own):
    m = LINES // FAN
    return pl.pallas_call(
        regroup_kernel,
        grid=(FAN,),
        in_specs=[
            pl.BlockSpec((2, 16 * FAN, BLOCK), lambda i: (0, i, 0)),
            whole((len(NETWORK) + 2, SIDE)),
        ],
        out_specs=[pl.BlockSpec((FAN, 2, 16, PART), lambda i: (0, 0, i, 0))] * 2,
        out_shape=[jax.ShapeDtypeStruct((FAN, 2, m, PART), jnp.bfloat16)] * 2,
        scratch_shapes=[pltpu.VMEM((SLOTS, 16 * FAN, SIDE), jnp.float32)],
        compiler_params=pltpu.CompilerParams(vmem_limit_bytes=VMEM),
        cost_estimate=pl.CostEstimate(flops=10**7, bytes_accessed=2**23, transcendentals=0),
        name="regroup_filter",
    )(azimuth_filter, own)


MERGE = 512


def finish_kernel(
    own_ref, a_ref, b_ref, f_ref, w_ref, t5_ref, t6_ref, first_ref, out_ref, spread, mixed, held
):
    step = pl.program_id(0)

    @pl.when(step < STEPS)
    def _():
        def put(part, row, lanes, value):
            held[step, part, row : row + 16, lanes] = value

        azimuth_step(a_ref, b_ref, f_ref, w_ref, t5_ref, t6_ref, spread, mixed, put)

    @pl.when(step >= STEPS)
    def _():
        swaps = masks(own_ref)
        first = (step - STEPS) * MERGE
        for part in (0, 1):
            for row in range(0, MERGE, 16):
                rows = slice(row, row + 16)
                slots = [
                    first_ref[part, rows, slot * SIDE : (slot + 1) * SIDE] for slot in range(HALF)
                ]
                for slot in range(HALF):
                    at, lane = divmod(slot * SIDE, SPAN)
                    from_row = pl.ds(pl.multiple_of(first + row, 16), 16)
                    slots.append(held[at, part, from_row, lane : lane + SIDE])
                slots = swapped(slots, swaps[::-1], NETWORK[::-1])
                for slot in range(SLOTS):
                    out_ref[0, part, rows, slot * SIDE : (slot + 1) * SIDE] = slots[slot]


def finish(own, early, late, response, image):
    m = LINES // FAN
    table = whole((2 * m, 2 * m))
    return pl.pallas_call(
        finish_kernel,
        grid=(STEPS + LINES // MERGE,),
        in_specs=[
            whole((len(NETWORK) + 2, SIDE)),
            pl.BlockSpec((N_RNG, 2 * EARLY, SPAN), lambda i: (0, 0, jnp.minimum(i, STEPS - 1))),
            pl.BlockSpec((N_RNG, 2 * LATE, SPAN), lambda i: (0, 0, jnp.minimum(i, STEPS - 1))),
            pl.BlockSpec((FAN, 2, m, SPAN), lambda i: (0, 0, 0, jnp.minimum(i, STEPS - 1))),
            whole((2, LINES, 128)),
            table,
            table,
            pl.BlockSpec((2, MERGE, PART), lambda i: (0, jnp.maximum(i - STEPS, 0), 0)),
        ],
        out_specs=pl.BlockSpec(
            (1, 2, MERGE, BLOCK), lambda i: (0, 0, jnp.maximum(i - STEPS, 0), 0)
        ),
        out_shape=jax.ShapeDtypeStruct((1, 2, LINES, BLOCK), jnp.bfloat16),
        scratch_shapes=AZIMUTH_SCRATCH + [pltpu.VMEM((STEPS, 2, LINES, SPAN), jnp.bfloat16)],
        compiler_params=pltpu.CompilerParams(vmem_limit_bytes=VMEM),
        name="finish",
    )(own, early, late, response, *azimuth_tables(), image)


def pass_kernel(date_ref, mate_ref, *refs):
    ins, outs, (held,) = refs[:DATES], refs[DATES : DATES + CHIPS], refs[DATES + CHIPS :]
    date = date_ref[0]
    for way in range(CHIPS):
        for other in (0, 1):
            held[2 * way + other] = ins[CHIPS * other + way][...]
    for way in range(CHIPS):
        outs[way][...] = held[mate_ref[(2 * way) ^ date] ^ date]


def pass_on(date, partner_date, held):
    smem, vmem = pl.BlockSpec(memory_space=pltpu.SMEM), pl.BlockSpec(memory_space=pltpu.VMEM)
    return pl.pallas_call(
        pass_kernel,
        in_specs=[smem] * 2 + [vmem] * DATES,
        out_specs=[vmem] * CHIPS,
        out_shape=[jax.ShapeDtypeStruct((2, WIN, WIN), jnp.bfloat16)] * CHIPS,
        scratch_shapes=[pltpu.VMEM((DATES, 2, WIN, WIN), jnp.bfloat16)],
        name="pass_on",
    )(date, partner_date, *held)


def along_y(chips):
    return [chips[0]] + [from_ways(chips[way], "date", DATES, (2 * way,))[0] for way in (1, 2, 3)]


def exchange(date, partner_date, chips):
    held = along_y(chips)
    held += [from_ways(chip, "date", DATES, (1,))[0] for chip in held]
    return along_y(pass_on(date, partner_date, held))


def transform(stacked, left, right):
    y = dot(left, jnp.concatenate(stacked, axis=1))
    half = y.shape[0] // 2
    rows = []
    for chip in range(CHIPS):
        cut = y[:, chip * WIN : (chip + 1) * WIN]
        rows.append(jnp.concatenate([bf16(cut[:half]), bf16(cut[half:])], axis=1))
    return dot(jnp.concatenate(rows, axis=0), right)


def primary_kernel(offsets_ref, own_ref, left_ref, right_ref, out_ref):
    inside = lax.broadcasted_iota(jnp.int32, (CHIP, WIN), 1) < CHIP
    empty = jnp.zeros((WIN - CHIP, WIN), jnp.bfloat16)
    primary = []
    for chip in range(CHIPS):
        row, col = offsets_ref[2 * chip], offsets_ref[2 * chip + 1]
        pieces = []
        for part in (0, 1):
            cut = own_ref[chip * 2 + part].astype(jnp.float32)
            cut = pltpu.roll(cut, lax.rem(WIN - row, WIN), 0)[:CHIP]
            cut = pltpu.roll(cut, lax.rem(WIN - col, WIN), 1)
            pieces += [bf16(jnp.where(inside, cut, 0.0)), empty]
        primary.append(jnp.concatenate(pieces, axis=0))
    out_ref[...] = transform(primary, left_ref[...], right_ref[...])


def correlate_kernel(
    date_ref, first_ref, left_ref, right_ref, left3_ref, right3_ref, *refs
):
    ins, (out_ref, their_ref) = refs[:CHIPS], refs[CHIPS:]
    for way in range(CHIPS):
        their_ref[way ^ (date_ref[0] // 2)] = ins[way][...]
    second = transform(
        [jnp.concatenate([their_ref[chip, 0], their_ref[chip, 1]], axis=0) for chip in range(CHIPS)],
        left_ref[...],
        right_ref[...],
    )
    a = (first_ref[:, :WIN], first_ref[:, WIN:])
    b = (second[:, :WIN], second[:, WIN:])
    product = (a[0] * b[0] + a[1] * b[1], a[1] * b[0] - a[0] * b[1])
    product = [bf16(part) for part in product]
    surface = transform(
        [
            jnp.concatenate([part[chip * WIN : (chip + 1) * WIN] for part in product], axis=0)
            for chip in range(CHIPS)
        ],
        left3_ref[...],
        right3_ref[...],
    )
    for chip in range(CHIPS):
        out_ref[0, chip] = surface[chip * CHIP : (chip + 1) * CHIP]


def correlation_tables():
    table = dft(WIN, -1)
    return from_left(table), from_right(table)


def transform_primary(offsets, own):
    vmem = pl.BlockSpec(memory_space=pltpu.VMEM)
    return pl.pallas_call(
        primary_kernel,
        in_specs=[pl.BlockSpec(memory_space=pltpu.SMEM)] + [vmem] * 3,
        out_specs=vmem,
        out_shape=jax.ShapeDtypeStruct((CHIPS * WIN, 2 * WIN), jnp.float32),
        compiler_params=pltpu.CompilerParams(vmem_limit_bytes=VMEM),
        name="transform_primary",
    )(offsets, own, *map(as_bf16, correlation_tables()))


def correlate(date, first, theirs):
    left, right = correlation_tables()
    factor = WIN // CHIP
    keep = np.concatenate([np.arange(CHIP), WIN + np.arange(CHIP)])
    vmem = pl.BlockSpec(memory_space=pltpu.VMEM)
    return pl.pallas_call(
        correlate_kernel,
        in_specs=[pl.BlockSpec(memory_space=pltpu.SMEM)] + [vmem] * (5 + CHIPS),
        out_specs=vmem,
        out_shape=jax.ShapeDtypeStruct((1, CHIPS, CHIP, 2 * CHIP), jnp.float32),
        scratch_shapes=[pltpu.VMEM((CHIPS, 2, WIN, WIN), jnp.bfloat16)],
        compiler_params=pltpu.CompilerParams(vmem_limit_bytes=VMEM),
        name="correlate",
    )(
        date,
        first,
        as_bf16(left),
        as_bf16(right),
        as_bf16(left[keep]),
        as_bf16(right[:, keep] * factor),
        *theirs,
    )


def to_blocks(x):
    return lax.all_to_all(x, "rng", split_axis=0, concat_axis=0, tiled=True)


def local(
    raw_echoes, range_filter, azimuth_filter, partner_date, chip_lines, chip_bins, chip_offsets
):
    me = lax.axis_index("rng").astype(jnp.int32).reshape(1)
    date = lax.axis_index("date").astype(jnp.int32).reshape(1)
    bins = all_bins(chip_bins)
    (early,) = compress_range(raw_echoes, range_filter, 0, EARLY)
    early, bins = lax.optimization_barrier((early, bins))
    early = to_blocks(early)
    swaps, own, picks = plan(me, bins)
    late, late_two = compress_range(raw_echoes, range_filter, EARLY, LATE, swaps)
    late, own, early = lax.optimization_barrier((late, own, early))
    late = to_blocks(late)
    early, early_two = order_bins(own, early)
    response, response_two = regroup_filter(azimuth_filter, own)
    offsets = chip_offsets.reshape(-1)
    late_two, early, early_two, response, response_two, offsets = lax.optimization_barrier(
        (late_two, early, early_two, response, response_two, offsets)
    )
    late_two = to_blocks(late_two)
    first, *chips, windows = focus_azimuth(
        me, date, chip_lines, chip_bins, picks, early, late, response
    )
    theirs = exchange(date, partner_date, chips)
    correlation = correlate(date, transform_primary(offsets, windows), theirs)
    return (finish(own, early_two, late_two, response_two, first), correlation)


def solution(mesh):
    in_specs = (
        P("date", None, "rng", None),
        P(),
        P(None, None, "rng"),
        P(),
        P("rng"),
        P("rng"),
        P("rng", None),
    )
    out_specs = (P("date", None, None, "rng"), P("date", "rng", None, None))
    return jax.shard_map(local, mesh=mesh, in_specs=in_specs, out_specs=out_specs, check_vma=False)
```

```python
import functools
import math

import jax
import jax.numpy as jnp
import ml_dtypes
import numpy as np
from jax import lax
from jax.experimental import pallas as pl
from jax.experimental.pallas import tpu as pltpu
from jax.sharding import PartitionSpec as P

LINES = 1024
BINS = 16384
CHIP = 64
CHIPS = 4
WIN = 128
DATES = 8
N_RNG = 16
SIDE = 128
FAN = 8
BLOCK = BINS // N_RNG
OWN = LINES // N_RNG
SLOTS = 8
HALF = 4
PART = HALF * 128
SORT = ((0, 1), (2, 3), (0, 2), (1, 3), (1, 2))
NETWORK = SORT + tuple((i + 4, j + 4) for i, j in SORT) + ((0, 7), (1, 6), (2, 5), (3, 4))
EARLY = 16
LATE = OWN - EARLY
ORDER = 4
GROUP = 16
BATCH = 16
SPAN = 256
WIDE = GROUP + 8
LONG = SIDE + 8
VMEM = 56 * 1024 * 1024


def dft(length, sign):
    phase = np.outer(np.arange(length), np.arange(length)) % length
    return np.exp(sign * 2j * math.pi * phase / length) / math.sqrt(length)


def twiddles(count, other, sign):
    phase = np.outer(np.arange(count), np.arange(other))
    return np.exp(sign * 2j * math.pi * phase / (count * other))


def from_left(table):
    return np.block([[table.real, -table.imag], [table.imag, table.real]])


def from_right(table):
    return np.block([[table.real, table.imag], [-table.imag, table.real]])


def as_bf16(table):
    return jnp.asarray(np.asarray(table, np.float32).astype(ml_dtypes.bfloat16))


def parts_of(table):
    return jnp.asarray(np.stack([table.real, table.imag]).astype(np.float32))


def times(a, b):
    return (a[0] * b[0] - a[1] * b[1], a[0] * b[1] + a[1] * b[0])


def dot(a, b):
    return jnp.dot(a, b, preferred_element_type=jnp.float32)


def bf16(x):
    return x.astype(jnp.bfloat16)


def swapped(slots, swaps, pairs):
    slots = list(slots)
    for swap, (i, j) in zip(swaps, pairs):
        slots[i], slots[j] = (
            jnp.where(swap, slots[j], slots[i]),
            jnp.where(swap, slots[i], slots[j]),
        )
    return slots


def masks(ref):
    rows = [jnp.broadcast_to(ref[at : at + 1, :], (16, SIDE)) for at in range(len(NETWORK))]
    return [bf16(row) > jnp.bfloat16(0.5) for row in rows]


def plan_kernel(me_ref, near_ref, *refs):
    far_refs, (swap_ref, own_ref, pick_ref) = refs[:3], refs[3:]
    me = me_ref[0]
    lane = lax.broadcasted_iota(jnp.int32, (N_RNG, SIDE), 1)
    device = lax.broadcasted_iota(jnp.int32, (N_RNG, SIDE), 0)
    runs = []
    for chip in range(CHIPS):
        first = jnp.zeros((N_RNG, SIDE), jnp.int32)
        for far, ref in zip((0, *FAR), (near_ref, *far_refs)):
            for at, near in enumerate((0, *NEAR)):
                first = jnp.where(device == (me ^ far ^ near), ref[at * CHIPS + chip], first)
        runs.append(first // SIDE + jnp.where(lane < first % SIDE, 1, 0))
    holds = [[jnp.where(run == slot, 1.0, 0.0) for slot in range(SLOTS)] for run in runs]
    wanted = [functools.reduce(jnp.maximum, [hold[slot] for hold in holds]) for slot in range(SLOTS)]
    for at, (i, j) in enumerate(NETWORK):
        swap = wanted[j] > wanted[i]
        swap_ref[at] = jnp.where(swap, 1.0, 0.0)
        wanted = swapped(wanted, [swap], [(i, j)])
        holds = [swapped(hold, [swap], [(i, j)]) for hold in holds]
    for at in range(len(NETWORK)):
        own_ref[at : at + 1, :] = swap_ref[at, pl.ds(me, 1), :]
    for chip in range(CHIPS):
        for slot in range(HALF):
            at = chip * HALF + slot
            pick_ref[at] = holds[chip][slot]


NEAR = (1, 8, 9)
FAR = (2, 4, 6)


def from_ways(x, axis, size, ways):
    return [lax.ppermute(x, axis, [(i, i ^ way) for i in range(size)]) for way in ways]


def all_bins(chip_bins):
    near = jnp.concatenate([chip_bins] + from_ways(chip_bins, "rng", N_RNG, NEAR))
    return [near] + from_ways(near, "rng", N_RNG, FAR)


def plan(me, bins):
    smem, vmem = pl.BlockSpec(memory_space=pltpu.SMEM), pl.BlockSpec(memory_space=pltpu.VMEM)
    return pl.pallas_call(
        plan_kernel,
        in_specs=[smem] * 5,
        out_specs=[vmem] * 3,
        out_shape=[
            jax.ShapeDtypeStruct((len(NETWORK), N_RNG, SIDE), jnp.float32),
            jax.ShapeDtypeStruct((len(NETWORK) + 2, SIDE), jnp.float32),
            jax.ShapeDtypeStruct((CHIPS * HALF, N_RNG, SIDE), jnp.float32),
        ],
        name="plan",
    )(me, *bins)


def range_kernel(x_ref, h_ref, w_ref, t1_ref, t2_ref, t3_ref, t4_ref, *refs, ordered):
    s = SIDE
    *refs, xs, ys, hs = refs

    @pl.when(pl.program_id(0) == 0)
    def _():
        for part in range(2):
            for j in range(s):
                ys[j : j + 1, :] = h_ref[part : part + 1, j * s : (j + 1) * s]
            hs[part] = ys[:s, :].T

    for part in range(2):
        for n in range(s):
            row = (part * s + n) * WIDE
            xs[row : row + GROUP, :] = x_ref[0, part, :, n * s : (n + 1) * s].astype(jnp.float32)
    w = (w_ref[0], w_ref[1])
    wc = (w[0], -w[1])
    h = (hs[0], hs[1])
    for line in range(0, GROUP, BATCH):
        batch = range(line, line + BATCH)
        x = [
            jnp.concatenate(
                [bf16(xs[pl.ds(part * s * WIDE + one, s, stride=WIDE), :]) for part in (0, 1)],
                axis=0,
            )
            for one in batch
        ]
        y = dot(t1_ref[...], jnp.concatenate(x, axis=1))
        x = []
        for one in range(BATCH):
            cut = y[:, one * s : (one + 1) * s]
            z = times((cut[:s], cut[s:]), w)
            x.append(jnp.concatenate([bf16(z[0]), bf16(z[1])], axis=1))
        y = dot(jnp.concatenate(x, axis=0), t2_ref[...])
        x = []
        for one in range(BATCH):
            cut = y[one * s : (one + 1) * s]
            z = times((cut[:, :s], cut[:, s:]), h)
            x.append(jnp.concatenate([bf16(z[0]), bf16(z[1])], axis=1))
        y = dot(jnp.concatenate(x, axis=0), t3_ref[...])
        x = []
        for one in range(BATCH):
            cut = y[one * s : (one + 1) * s]
            z = times((cut[:, :s], cut[:, s:]), wc)
            x.append(jnp.concatenate([bf16(z[0]), bf16(z[1])], axis=0))
        y = dot(t4_ref[...], jnp.concatenate(x, axis=1))
        for one in range(BATCH):
            for part in (0, 1):
                row = (part * GROUP + line + one) * LONG
                ys[row : row + s, :] = y[
                    part * s : (part + 1) * s, one * s : (one + 1) * s
                ]
    for dest in range(N_RNG):
        if ordered:
            swap_ref, out1_ref, out2_ref = refs
            swaps = masks(swap_ref.at[:, dest])
        else:
            (out_ref,) = refs
        for part in (0, 1):
            slots = []
            for slot in range(SLOTS):
                row = part * GROUP * LONG + dest * SLOTS + slot
                slots.append(bf16(ys[pl.ds(row, GROUP, stride=LONG), :]))
            if not ordered:
                for slot in range(SLOTS):
                    out_ref[dest, part, :, slot * s : (slot + 1) * s] = slots[slot]
                continue
            slots = swapped(slots, swaps, NETWORK)
            for slot in range(HALF):
                lanes = slice(slot * s, (slot + 1) * s)
                out1_ref[dest, part, :, lanes] = slots[slot]
                out2_ref[dest, part, :, lanes] = slots[slot + HALF]


def whole(shape):
    return pl.BlockSpec(shape, lambda *_: (0,) * len(shape))


def compress_range(raw_echoes, range_filter, first, lines, swaps=None):
    forward = dft(SIDE, -1)
    backward = dft(SIDE, 1)
    tables = [
        as_bf16(from_left(forward)),
        as_bf16(from_right(forward)),
        as_bf16(from_right(backward)),
        as_bf16(from_left(backward)),
    ]
    turn = parts_of(twiddles(SIDE, SIDE, -1))
    table = whole((2 * SIDE, 2 * SIDE))
    ordered = swaps is not None
    width, count = (PART, 2) if ordered else (BLOCK, 1)
    outs = pl.pallas_call(
        functools.partial(range_kernel, ordered=ordered),
        grid=(lines // GROUP,),
        in_specs=[
            pl.BlockSpec((1, 2, GROUP, BINS), lambda i: (0, 0, i + first // GROUP, 0)),
            whole((2, BINS)),
            whole((2, SIDE, SIDE)),
            table,
            table,
            table,
            table,
        ]
        + [whole((len(NETWORK), N_RNG, SIDE))] * ordered,
        out_specs=[pl.BlockSpec((N_RNG, 2, GROUP, width), lambda i: (0, 0, i, 0))] * count,
        out_shape=[jax.ShapeDtypeStruct((N_RNG, 2, lines, width), jnp.bfloat16)] * count,
        scratch_shapes=[
            pltpu.VMEM((2 * SIDE * WIDE, SIDE), jnp.float32),
            pltpu.VMEM((2 * LONG * GROUP, SIDE), jnp.float32),
            pltpu.VMEM((2, SIDE, SIDE), jnp.float32),
        ],
        compiler_params=pltpu.CompilerParams(vmem_limit_bytes=VMEM),
        cost_estimate=pl.CostEstimate(flops=4 * 10**9, bytes_accessed=2**22, transcendentals=0),
        name="compress_range",
    )(raw_echoes, range_filter, turn, *tables, *([swaps] * ordered))
    return [out.reshape(N_RNG, 2 * lines, width) for out in outs]


def order_kernel(own_ref, x_ref, out1_ref, out2_ref):
    swaps = masks(own_ref)
    for device in range(ORDER):
        for row in range(0, 2 * EARLY, 16):
            rows = slice(row, row + 16)
            slots = [
                x_ref[device, rows, slot * SIDE : (slot + 1) * SIDE] for slot in range(SLOTS)
            ]
            slots = swapped(slots, swaps, NETWORK)
            for slot in range(HALF):
                lanes = slice(slot * SIDE, (slot + 1) * SIDE)
                out1_ref[device, rows, lanes] = slots[slot]
                out2_ref[device, rows, lanes] = slots[slot + HALF]


def order_bins(own, x):
    return pl.pallas_call(
        order_kernel,
        grid=(N_RNG // ORDER,),
        in_specs=[
            whole((len(NETWORK) + 2, SIDE)),
            pl.BlockSpec((ORDER, 2 * EARLY, BLOCK), lambda i: (i, 0, 0)),
        ],
        out_specs=[pl.BlockSpec((ORDER, 2 * EARLY, PART), lambda i: (i, 0, 0))] * 2,
        out_shape=[jax.ShapeDtypeStruct((N_RNG, 2 * EARLY, PART), jnp.bfloat16)] * 2,
        compiler_params=pltpu.CompilerParams(vmem_limit_bytes=VMEM),
        cost_estimate=pl.CostEstimate(flops=10**7, bytes_accessed=2**22, transcendentals=0),
        name="order_bins",
    )(own, x)


def add(a, b):
    return (a[0] + b[0], a[1] + b[1])


def sub(a, b):
    return (a[0] - b[0], a[1] - b[1])


def fan_dft(x, sign):
    root = math.sqrt(0.5)

    def quarter(a):
        return (-sign * a[1], sign * a[0]) if sign > 0 else (a[1], -a[0])

    def eighth(a):
        if sign > 0:
            return ((a[0] - a[1]) * root, (a[0] + a[1]) * root)
        return ((a[0] + a[1]) * root, (a[1] - a[0]) * root)

    def four(a, b, c, d):
        e, f, g, h = add(a, c), sub(a, c), add(b, d), quarter(sub(b, d))
        return add(e, g), add(f, h), sub(e, g), sub(f, h)

    even = four(x[0], x[2], x[4], x[6])
    odd = four(x[1], x[3], x[5], x[7])
    odd = (odd[0], eighth(odd[1]), quarter(odd[2]), quarter(eighth(odd[3])))
    return [add(p, q) for p, q in zip(even, odd)] + [sub(p, q) for p, q in zip(even, odd)]


def azimuth_step(a_ref, b_ref, f_ref, w_ref, t5_ref, t6_ref, spread, mixed, put):
    m = LINES // FAN
    tiles = [(t, slice(lane * 128, (lane + 1) * 128)) for t in range(m // 16) for lane in range(SPAN // 128)]
    for tile, lanes in tiles:
        half, line = divmod(tile * 16, OWN)
        points = []
        for n in range(FAN):
            ref, row, lines = (a_ref, line, EARLY) if line < EARLY else (b_ref, line - EARLY, LATE)
            rows = [slice(part * lines + row, part * lines + row + 16) for part in (0, 1)]
            points.append(tuple(ref[2 * n + half, row, lanes].astype(jnp.float32) for row in rows))
        for k, value in enumerate(fan_dft(points, -1)):
            if k:
                row = k * m + tile * 16
                value = times(value, (w_ref[0, row : row + 16], w_ref[1, row : row + 16]))
            for part in (0, 1):
                row = (half * 2 + part) * OWN + line
                at = k * SPAN + lanes.start
                spread[row : row + 16, at : at + 128] = bf16(value[part])
    y = dot(t5_ref[...], spread[...])
    x = []
    for k in range(FAN):
        cut = y[:, k * SPAN : (k + 1) * SPAN]
        f = (f_ref[k, 0].astype(jnp.float32), f_ref[k, 1].astype(jnp.float32))
        z = times((cut[:m], cut[m:]), f)
        x.append(jnp.concatenate([bf16(z[0]), bf16(z[1])], axis=0))
    mixed[...] = dot(t6_ref[...], jnp.concatenate(x, axis=1))
    for tile, lanes in tiles:
        points = []
        for k in range(FAN):
            at = k * SPAN + lanes.start
            row = tile * 16
            value = tuple(mixed[part * m + row : part * m + row + 16, at : at + 128] for part in (0, 1))
            if k:
                row += k * m
                value = times(value, (w_ref[0, row : row + 16], -w_ref[1, row : row + 16]))
            points.append(value)
        for p, value in enumerate(fan_dft(points, 1)):
            row = p * m + tile * 16
            for part in (0, 1):
                put(part, row, lanes, bf16(value[part]))


ROWS = WIN + 16
STEPS = PART // SPAN


def azimuth_kernel(
    me_ref, date_ref, lines_ref, bins_ref, pick_ref, a_ref, b_ref, f_ref, w_ref, t5_ref, t6_ref, *refs
):
    out_ref, *outs, slices, spread, mixed, held = refs
    step = pl.program_id(0)

    def put(part, row, lanes, value):
        out_ref[part, row : row + 16, lanes] = value
        held[step, part, row : row + 16, lanes] = value

    azimuth_step(a_ref, b_ref, f_ref, w_ref, t5_ref, t6_ref, spread, mixed, put)

    @pl.when(step == STEPS - 1)
    def _():
        me, date = me_ref[0], date_ref[0]
        for chip in range(CHIPS):
            line = lines_ref[chip]
            row = jnp.minimum(line // 16 * 16, LINES - ROWS)
            picks = [pick_ref[chip * HALF + slot, pl.ds(me, 1), :] > 0.5 for slot in range(HALF)]
            for part in (0, 1):
                for slot in range(HALF):
                    at, lane = divmod(slot * SIDE, SPAN)
                    other = held[at, part, pl.ds(pl.multiple_of(row, 16), ROWS), lane : lane + SIDE]
                    other = other.astype(jnp.float32)
                    cut = jnp.where(picks[slot], other, cut) if slot else other
                cut = pltpu.roll(cut, lax.rem(ROWS - (line - row), ROWS), 0)[:WIN]
                cut = pltpu.roll(cut, lax.rem(WIN - lax.rem(bins_ref[chip], WIN), WIN), 1)
                slices[chip * 2 + part] = bf16(cut)
        for way in range(CHIPS):
            for part in (0, 1):
                outs[way][part] = slices[2 * (way ^ (date // 2)) + part]


def azimuth_tables():
    m = LINES // FAN
    forward = np.exp(-2j * math.pi * np.outer(np.arange(m), np.arange(m)) / m) / math.sqrt(LINES)
    backward = forward.conj()
    first = from_left(forward).reshape(2 * m, 2, 2, OWN).transpose(0, 2, 1, 3).reshape(2 * m, 2 * m)
    turn = twiddles(FAN, m, -1).reshape(LINES, 1) * np.ones((1, 128))
    return parts_of(turn), as_bf16(first), as_bf16(from_left(backward))


AZIMUTH_SCRATCH = [
    pltpu.VMEM((2 * LINES // FAN, FAN * SPAN), jnp.bfloat16),
    pltpu.VMEM((2 * LINES // FAN, FAN * SPAN), jnp.float32),
]


def focus_azimuth(me, date, chip_lines, chip_bins, picks, early, late, response):
    m = LINES // FAN
    table = whole((2 * m, 2 * m))
    smem = pl.BlockSpec(memory_space=pltpu.SMEM)
    counts = (2, 2, 2, 2, 2 * CHIPS)
    return pl.pallas_call(
        azimuth_kernel,
        grid=(STEPS,),
        in_specs=[
            smem,
            smem,
            smem,
            smem,
            whole((CHIPS * HALF, N_RNG, SIDE)),
            pl.BlockSpec((N_RNG, 2 * EARLY, SPAN), lambda i: (0, 0, i)),
            pl.BlockSpec((N_RNG, 2 * LATE, SPAN), lambda i: (0, 0, i)),
            pl.BlockSpec((FAN, 2, m, SPAN), lambda i: (0, 0, 0, i)),
            whole((2, LINES, 128)),
            table,
            table,
        ],
        out_specs=[pl.BlockSpec((2, LINES, SPAN), lambda i: (0, 0, i))]
        + [whole((count, WIN, WIN)) for count in counts],
        out_shape=[jax.ShapeDtypeStruct((2, LINES, PART), jnp.bfloat16)]
        + [jax.ShapeDtypeStruct((count, WIN, WIN), jnp.bfloat16) for count in counts],
        scratch_shapes=AZIMUTH_SCRATCH + [pltpu.VMEM((STEPS, 2, LINES, SPAN), jnp.bfloat16)],
        compiler_params=pltpu.CompilerParams(vmem_limit_bytes=VMEM),
        name="focus_azimuth",
    )(me, date, chip_lines, chip_bins, picks, early, late, response, *azimuth_tables())


def regroup_kernel(f_ref, own_ref, out1_ref, out2_ref, wide):
    swaps = masks(own_ref)
    for part in (0, 1):
        for slot in range(SLOTS):
            wide[slot] = f_ref[part, :, slot * SIDE : (slot + 1) * SIDE].astype(jnp.float32)
        for k in range(FAN):
            slots = [bf16(wide[slot, pl.ds(k, 16, stride=FAN), :]) for slot in range(SLOTS)]
            slots = swapped(slots, swaps, NETWORK)
            for slot in range(HALF):
                lanes = slice(slot * SIDE, (slot + 1) * SIDE)
                out1_ref[k, part, :, lanes] = slots[slot]
                out2_ref[k, part, :, lanes] = slots[slot + HALF]


def regroup_filter(azimuth_filter, own):
    m = LINES // FAN
    return pl.pallas_call(
        regroup_kernel,
        grid=(FAN,),
        in_specs=[
            pl.BlockSpec((2, 16 * FAN, BLOCK), lambda i: (0, i, 0)),
            whole((len(NETWORK) + 2, SIDE)),
        ],
        out_specs=[pl.BlockSpec((FAN, 2, 16, PART), lambda i: (0, 0, i, 0))] * 2,
        out_shape=[jax.ShapeDtypeStruct((FAN, 2, m, PART), jnp.bfloat16)] * 2,
        scratch_shapes=[pltpu.VMEM((SLOTS, 16 * FAN, SIDE), jnp.float32)],
        compiler_params=pltpu.CompilerParams(vmem_limit_bytes=VMEM),
        cost_estimate=pl.CostEstimate(flops=10**7, bytes_accessed=2**23, transcendentals=0),
        name="regroup_filter",
    )(azimuth_filter, own)


MERGE = 512


def finish_kernel(
    own_ref, a_ref, b_ref, f_ref, w_ref, t5_ref, t6_ref, first_ref, out_ref, spread, mixed, held
):
    step = pl.program_id(0)

    @pl.when(step < STEPS)
    def _():
        def put(part, row, lanes, value):
            held[step, part, row : row + 16, lanes] = value

        azimuth_step(a_ref, b_ref, f_ref, w_ref, t5_ref, t6_ref, spread, mixed, put)

    @pl.when(step >= STEPS)
    def _():
        swaps = masks(own_ref)
        first = (step - STEPS) * MERGE
        for part in (0, 1):
            for row in range(0, MERGE, 16):
                rows = slice(row, row + 16)
                slots = [
                    first_ref[part, rows, slot * SIDE : (slot + 1) * SIDE] for slot in range(HALF)
                ]
                for slot in range(HALF):
                    at, lane = divmod(slot * SIDE, SPAN)
                    from_row = pl.ds(pl.multiple_of(first + row, 16), 16)
                    slots.append(held[at, part, from_row, lane : lane + SIDE])
                slots = swapped(slots, swaps[::-1], NETWORK[::-1])
                for slot in range(SLOTS):
                    out_ref[0, part, rows, slot * SIDE : (slot + 1) * SIDE] = slots[slot]


def finish(own, early, late, response, image):
    m = LINES // FAN
    table = whole((2 * m, 2 * m))
    return pl.pallas_call(
        finish_kernel,
        grid=(STEPS + LINES // MERGE,),
        in_specs=[
            whole((len(NETWORK) + 2, SIDE)),
            pl.BlockSpec((N_RNG, 2 * EARLY, SPAN), lambda i: (0, 0, jnp.minimum(i, STEPS - 1))),
            pl.BlockSpec((N_RNG, 2 * LATE, SPAN), lambda i: (0, 0, jnp.minimum(i, STEPS - 1))),
            pl.BlockSpec((FAN, 2, m, SPAN), lambda i: (0, 0, 0, jnp.minimum(i, STEPS - 1))),
            whole((2, LINES, 128)),
            table,
            table,
            pl.BlockSpec((2, MERGE, PART), lambda i: (0, jnp.maximum(i - STEPS, 0), 0)),
        ],
        out_specs=pl.BlockSpec(
            (1, 2, MERGE, BLOCK), lambda i: (0, 0, jnp.maximum(i - STEPS, 0), 0)
        ),
        out_shape=jax.ShapeDtypeStruct((1, 2, LINES, BLOCK), jnp.bfloat16),
        scratch_shapes=AZIMUTH_SCRATCH + [pltpu.VMEM((STEPS, 2, LINES, SPAN), jnp.bfloat16)],
        compiler_params=pltpu.CompilerParams(vmem_limit_bytes=VMEM),
        name="finish",
    )(own, early, late, response, *azimuth_tables(), image)


def pass_kernel(date_ref, mate_ref, *refs):
    ins, outs, (held,) = refs[:DATES], refs[DATES : DATES + CHIPS], refs[DATES + CHIPS :]
    date = date_ref[0]
    for way in range(CHIPS):
        for other in (0, 1):
            held[2 * way + other] = ins[CHIPS * other + way][...]
    for way in range(CHIPS):
        outs[way][...] = held[mate_ref[(2 * way) ^ date] ^ date]


def pass_on(date, partner_date, held):
    smem, vmem = pl.BlockSpec(memory_space=pltpu.SMEM), pl.BlockSpec(memory_space=pltpu.VMEM)
    return pl.pallas_call(
        pass_kernel,
        in_specs=[smem] * 2 + [vmem] * DATES,
        out_specs=[vmem] * CHIPS,
        out_shape=[jax.ShapeDtypeStruct((2, WIN, WIN), jnp.bfloat16)] * CHIPS,
        scratch_shapes=[pltpu.VMEM((DATES, 2, WIN, WIN), jnp.bfloat16)],
        name="pass_on",
    )(date, partner_date, *held)


def along_y(chips):
    return [chips[0]] + [from_ways(chips[way], "date", DATES, (2 * way,))[0] for way in (1, 2, 3)]


def exchange(date, partner_date, chips):
    held = along_y(chips)
    held += [from_ways(chip, "date", DATES, (1,))[0] for chip in held]
    return along_y(pass_on(date, partner_date, held))


def transform(stacked, left, right):
    y = dot(left, jnp.concatenate(stacked, axis=1))
    half = y.shape[0] // 2
    rows = []
    for chip in range(CHIPS):
        cut = y[:, chip * WIN : (chip + 1) * WIN]
        rows.append(jnp.concatenate([bf16(cut[:half]), bf16(cut[half:])], axis=1))
    return dot(jnp.concatenate(rows, axis=0), right)


def correlate_kernel(
    date_ref, offsets_ref, own_ref, left_ref, right_ref, left3_ref, right3_ref, *refs
):
    ins, (out_ref, their_ref) = refs[:CHIPS], refs[CHIPS:]
    for way in range(CHIPS):
        their_ref[way ^ (date_ref[0] // 2)] = ins[way][...]
    left, right = left_ref[...], right_ref[...]
    inside = lax.broadcasted_iota(jnp.int32, (CHIP, WIN), 1) < CHIP
    empty = jnp.zeros((WIN - CHIP, WIN), jnp.bfloat16)
    primary = []
    for chip in range(CHIPS):
        row, col = offsets_ref[2 * chip], offsets_ref[2 * chip + 1]
        pieces = []
        for part in (0, 1):
            cut = own_ref[chip * 2 + part].astype(jnp.float32)
            cut = pltpu.roll(cut, lax.rem(WIN - row, WIN), 0)[:CHIP]
            cut = pltpu.roll(cut, lax.rem(WIN - col, WIN), 1)
            pieces += [bf16(jnp.where(inside, cut, 0.0)), empty]
        primary.append(jnp.concatenate(pieces, axis=0))
    first = transform(primary, left, right)
    second = transform(
        [jnp.concatenate([their_ref[chip, 0], their_ref[chip, 1]], axis=0) for chip in range(CHIPS)],
        left,
        right,
    )
    a = (first[:, :WIN], first[:, WIN:])
    b = (second[:, :WIN], second[:, WIN:])
    product = (a[0] * b[0] + a[1] * b[1], a[1] * b[0] - a[0] * b[1])
    product = [bf16(part) for part in product]
    surface = transform(
        [
            jnp.concatenate([part[chip * WIN : (chip + 1) * WIN] for part in product], axis=0)
            for chip in range(CHIPS)
        ],
        left3_ref[...],
        right3_ref[...],
    )
    for chip in range(CHIPS):
        out_ref[0, chip] = surface[chip * CHIP : (chip + 1) * CHIP]


def correlate(date, offsets, own, theirs):
    table = dft(WIN, -1)
    left, right = from_left(table), from_right(table)
    factor = WIN // CHIP
    keep = np.concatenate([np.arange(CHIP), WIN + np.arange(CHIP)])
    vmem = pl.BlockSpec(memory_space=pltpu.VMEM)
    return pl.pallas_call(
        correlate_kernel,
        in_specs=[pl.BlockSpec(memory_space=pltpu.SMEM)] * 2 + [vmem] * (5 + CHIPS),
        out_specs=vmem,
        out_shape=jax.ShapeDtypeStruct((1, CHIPS, CHIP, 2 * CHIP), jnp.float32),
        scratch_shapes=[pltpu.VMEM((CHIPS, 2, WIN, WIN), jnp.bfloat16)],
        compiler_params=pltpu.CompilerParams(vmem_limit_bytes=VMEM),
        name="correlate",
    )(
        date,
        offsets,
        own,
        as_bf16(left),
        as_bf16(right),
        as_bf16(left[keep]),
        as_bf16(right[:, keep] * factor),
        *theirs,
    )


def to_blocks(x):
    return lax.all_to_all(x, "rng", split_axis=0, concat_axis=0, tiled=True)


def local(
    raw_echoes, range_filter, azimuth_filter, partner_date, chip_lines, chip_bins, chip_offsets
):
    me = lax.axis_index("rng").astype(jnp.int32).reshape(1)
    date = lax.axis_index("date").astype(jnp.int32).reshape(1)
    bins = all_bins(chip_bins)
    (early,) = compress_range(raw_echoes, range_filter, 0, EARLY)
    early, bins = lax.optimization_barrier((early, bins))
    early = to_blocks(early)
    swaps, own, picks = plan(me, bins)
    late, late_two = compress_range(raw_echoes, range_filter, EARLY, LATE, swaps)
    late, own, early = lax.optimization_barrier((late, own, early))
    late = to_blocks(late)
    early, early_two = order_bins(own, early)
    response, response_two = regroup_filter(azimuth_filter, own)
    offsets = chip_offsets.reshape(-1)
    late_two, early, early_two, response, response_two, offsets = lax.optimization_barrier(
        (late_two, early, early_two, response, response_two, offsets)
    )
    late_two = to_blocks(late_two)
    first, *chips, windows = focus_azimuth(
        me, date, chip_lines, chip_bins, picks, early, late, response
    )
    theirs = exchange(date, partner_date, chips)
    correlation = correlate(date, offsets, windows, theirs)
    return (finish(own, early_two, late_two, response_two, first), correlation)


def solution(mesh):
    in_specs = (
        P("date", None, "rng", None),
        P(),
        P(None, None, "rng"),
        P(),
        P("rng"),
        P("rng"),
        P("rng", None),
    )
    out_specs = (P("date", None, None, "rng"), P("date", "rng", None, None))
    return jax.shard_map(local, mesh=mesh, in_specs=in_specs, out_specs=out_specs, check_vma=False)
```

```python
import functools
import math

import jax
import jax.numpy as jnp
import ml_dtypes
import numpy as np
from jax import lax
from jax.experimental import pallas as pl
from jax.experimental.pallas import tpu as pltpu
from jax.sharding import PartitionSpec as P

LINES = 1024
BINS = 16384
CHIP = 64
CHIPS = 4
WIN = 128
DATES = 8
N_RNG = 16
SIDE = 128
FAN = 8
BLOCK = BINS // N_RNG
OWN = LINES // N_RNG
SLOTS = 8
HALF = 4
PART = HALF * 128
SORT = ((0, 1), (2, 3), (0, 2), (1, 3), (1, 2))
NETWORK = SORT + tuple((i + 4, j + 4) for i, j in SORT) + ((0, 7), (1, 6), (2, 5), (3, 4))
EARLY = 16
LATE = OWN - EARLY
ORDER = 4
GROUP = 16
BATCH = 16
SPAN = 256
WIDE = GROUP + 8
LONG = SIDE + 8
VMEM = 56 * 1024 * 1024


def dft(length, sign):
    phase = np.outer(np.arange(length), np.arange(length)) % length
    return np.exp(sign * 2j * math.pi * phase / length) / math.sqrt(length)


def twiddles(count, other, sign):
    phase = np.outer(np.arange(count), np.arange(other))
    return np.exp(sign * 2j * math.pi * phase / (count * other))


def from_left(table):
    return np.block([[table.real, -table.imag], [table.imag, table.real]])


def from_right(table):
    return np.block([[table.real, table.imag], [-table.imag, table.real]])


def as_bf16(table):
    return jnp.asarray(np.asarray(table, np.float32).astype(ml_dtypes.bfloat16))


def parts_of(table):
    return jnp.asarray(np.stack([table.real, table.imag]).astype(np.float32))


def times(a, b):
    return (a[0] * b[0] - a[1] * b[1], a[0] * b[1] + a[1] * b[0])


def dot(a, b):
    return jnp.dot(a, b, preferred_element_type=jnp.float32)


def bf16(x):
    return x.astype(jnp.bfloat16)


def swapped(slots, swaps, pairs):
    slots = list(slots)
    for swap, (i, j) in zip(swaps, pairs):
        slots[i], slots[j] = (
            jnp.where(swap, slots[j], slots[i]),
            jnp.where(swap, slots[i], slots[j]),
        )
    return slots


def masks(ref):
    rows = [jnp.broadcast_to(ref[at : at + 1, :], (16, SIDE)) for at in range(len(NETWORK))]
    return [bf16(row) > jnp.bfloat16(0.5) for row in rows]


def plan_kernel(me_ref, near_ref, *refs):
    far_refs, (swap_ref, own_ref, pick_ref) = refs[:3], refs[3:]
    me = me_ref[0]
    lane = lax.broadcasted_iota(jnp.int32, (N_RNG, SIDE), 1)
    device = lax.broadcasted_iota(jnp.int32, (N_RNG, SIDE), 0)
    runs = []
    for chip in range(CHIPS):
        first = jnp.zeros((N_RNG, SIDE), jnp.int32)
        for far, ref in zip((0, *FAR), (near_ref, *far_refs)):
            for at, near in enumerate((0, *NEAR)):
                first = jnp.where(device == (me ^ far ^ near), ref[at * CHIPS + chip], first)
        runs.append(first // SIDE + jnp.where(lane < first % SIDE, 1, 0))
    holds = [[jnp.where(run == slot, 1.0, 0.0) for slot in range(SLOTS)] for run in runs]
    wanted = [functools.reduce(jnp.maximum, [hold[slot] for hold in holds]) for slot in range(SLOTS)]
    for at, (i, j) in enumerate(NETWORK):
        swap = wanted[j] > wanted[i]
        swap_ref[at] = jnp.where(swap, 1.0, 0.0)
        wanted = swapped(wanted, [swap], [(i, j)])
        holds = [swapped(hold, [swap], [(i, j)]) for hold in holds]
    for at in range(len(NETWORK)):
        own_ref[at : at + 1, :] = swap_ref[at, pl.ds(me, 1), :]
    for chip in range(CHIPS):
        for slot in range(HALF):
            at = chip * HALF + slot
            pick_ref[at] = holds[chip][slot]


NEAR = (1, 8, 9)
FAR = (2, 4, 6)


def from_ways(x, axis, size, ways):
    return [lax.ppermute(x, axis, [(i, i ^ way) for i in range(size)]) for way in ways]


def all_bins(chip_bins):
    near = jnp.concatenate([chip_bins] + from_ways(chip_bins, "rng", N_RNG, NEAR))
    return [near] + from_ways(near, "rng", N_RNG, FAR)


def plan(me, bins):
    smem, vmem = pl.BlockSpec(memory_space=pltpu.SMEM), pl.BlockSpec(memory_space=pltpu.VMEM)
    return pl.pallas_call(
        plan_kernel,
        in_specs=[smem] * 5,
        out_specs=[vmem] * 3,
        out_shape=[
            jax.ShapeDtypeStruct((len(NETWORK), N_RNG, SIDE), jnp.float32),
            jax.ShapeDtypeStruct((len(NETWORK) + 2, SIDE), jnp.float32),
            jax.ShapeDtypeStruct((CHIPS * HALF, N_RNG, SIDE), jnp.float32),
        ],
        name="plan",
    )(me, *bins)


def range_kernel(x_ref, h_ref, w_ref, t1_ref, t2_ref, t3_ref, t4_ref, *refs, ordered):
    s = SIDE
    *refs, xs, ys, hs = refs

    @pl.when(pl.program_id(0) == 0)
    def _():
        for part in range(2):
            for j in range(s):
                ys[j : j + 1, :] = h_ref[part : part + 1, j * s : (j + 1) * s]
            hs[part] = ys[:s, :].T

    for part in range(2):
        for n in range(s):
            row = (part * s + n) * WIDE
            xs[row : row + GROUP, :] = x_ref[0, part, :, n * s : (n + 1) * s].astype(jnp.float32)
    w = (w_ref[0], w_ref[1])
    wc = (w[0], -w[1])
    h = (hs[0], hs[1])
    for line in range(0, GROUP, BATCH):
        batch = range(line, line + BATCH)
        x = [
            jnp.concatenate(
                [bf16(xs[pl.ds(part * s * WIDE + one, s, stride=WIDE), :]) for part in (0, 1)],
                axis=0,
            )
            for one in batch
        ]
        y = dot(t1_ref[...], jnp.concatenate(x, axis=1))
        x = []
        for one in range(BATCH):
            cut = y[:, one * s : (one + 1) * s]
            z = times((cut[:s], cut[s:]), w)
            x.append(jnp.concatenate([bf16(z[0]), bf16(z[1])], axis=1))
        y = dot(jnp.concatenate(x, axis=0), t2_ref[...])
        x = []
        for one in range(BATCH):
            cut = y[one * s : (one + 1) * s]
            z = times((cut[:, :s], cut[:, s:]), h)
            x.append(jnp.concatenate([bf16(z[0]), bf16(z[1])], axis=1))
        y = dot(jnp.concatenate(x, axis=0), t3_ref[...])
        x = []
        for one in range(BATCH):
            cut = y[one * s : (one + 1) * s]
            z = times((cut[:, :s], cut[:, s:]), wc)
            x.append(jnp.concatenate([bf16(z[0]), bf16(z[1])], axis=0))
        y = dot(t4_ref[...], jnp.concatenate(x, axis=1))
        for one in range(BATCH):
            for part in (0, 1):
                row = (part * GROUP + line + one) * LONG
                ys[row : row + s, :] = y[
                    part * s : (part + 1) * s, one * s : (one + 1) * s
                ]
    for dest in range(N_RNG):
        if ordered:
            swap_ref, out1_ref, out2_ref = refs
            swaps = masks(swap_ref.at[:, dest])
        else:
            (out_ref,) = refs
        for part in (0, 1):
            slots = []
            for slot in range(SLOTS):
                row = part * GROUP * LONG + dest * SLOTS + slot
                slots.append(bf16(ys[pl.ds(row, GROUP, stride=LONG), :]))
            if not ordered:
                for slot in range(SLOTS):
                    out_ref[dest, part, :, slot * s : (slot + 1) * s] = slots[slot]
                continue
            slots = swapped(slots, swaps, NETWORK)
            for slot in range(HALF):
                lanes = slice(slot * s, (slot + 1) * s)
                out1_ref[dest, part, :, lanes] = slots[slot]
                out2_ref[dest, part, :, lanes] = slots[slot + HALF]


def whole(shape):
    return pl.BlockSpec(shape, lambda *_: (0,) * len(shape))


def compress_range(raw_echoes, range_filter, first, lines, swaps=None):
    forward = dft(SIDE, -1)
    backward = dft(SIDE, 1)
    tables = [
        as_bf16(from_left(forward)),
        as_bf16(from_right(forward)),
        as_bf16(from_right(backward)),
        as_bf16(from_left(backward)),
    ]
    turn = parts_of(twiddles(SIDE, SIDE, -1))
    table = whole((2 * SIDE, 2 * SIDE))
    ordered = swaps is not None
    width, count = (PART, 2) if ordered else (BLOCK, 1)
    outs = pl.pallas_call(
        functools.partial(range_kernel, ordered=ordered),
        grid=(lines // GROUP,),
        in_specs=[
            pl.BlockSpec((1, 2, GROUP, BINS), lambda i: (0, 0, i + first // GROUP, 0)),
            whole((2, BINS)),
            whole((2, SIDE, SIDE)),
            table,
            table,
            table,
            table,
        ]
        + [whole((len(NETWORK), N_RNG, SIDE))] * ordered,
        out_specs=[pl.BlockSpec((N_RNG, 2, GROUP, width), lambda i: (0, 0, i, 0))] * count,
        out_shape=[jax.ShapeDtypeStruct((N_RNG, 2, lines, width), jnp.bfloat16)] * count,
        scratch_shapes=[
            pltpu.VMEM((2 * SIDE * WIDE, SIDE), jnp.float32),
            pltpu.VMEM((2 * LONG * GROUP, SIDE), jnp.float32),
            pltpu.VMEM((2, SIDE, SIDE), jnp.float32),
        ],
        compiler_params=pltpu.CompilerParams(vmem_limit_bytes=VMEM),
        cost_estimate=pl.CostEstimate(flops=4 * 10**9, bytes_accessed=2**22, transcendentals=0),
        name="compress_range",
    )(raw_echoes, range_filter, turn, *tables, *([swaps] * ordered))
    return [out.reshape(N_RNG, 2 * lines, width) for out in outs]


def order_kernel(own_ref, x_ref, out1_ref, out2_ref):
    swaps = masks(own_ref)
    for device in range(ORDER):
        for row in range(0, 2 * EARLY, 16):
            rows = slice(row, row + 16)
            slots = [
                x_ref[device, rows, slot * SIDE : (slot + 1) * SIDE] for slot in range(SLOTS)
            ]
            slots = swapped(slots, swaps, NETWORK)
            for slot in range(HALF):
                lanes = slice(slot * SIDE, (slot + 1) * SIDE)
                out1_ref[device, rows, lanes] = slots[slot]
                out2_ref[device, rows, lanes] = slots[slot + HALF]


def order_bins(own, x):
    return pl.pallas_call(
        order_kernel,
        grid=(N_RNG // ORDER,),
        in_specs=[
            whole((len(NETWORK) + 2, SIDE)),
            pl.BlockSpec((ORDER, 2 * EARLY, BLOCK), lambda i: (i, 0, 0)),
        ],
        out_specs=[pl.BlockSpec((ORDER, 2 * EARLY, PART), lambda i: (i, 0, 0))] * 2,
        out_shape=[jax.ShapeDtypeStruct((N_RNG, 2 * EARLY, PART), jnp.bfloat16)] * 2,
        compiler_params=pltpu.CompilerParams(vmem_limit_bytes=VMEM),
        cost_estimate=pl.CostEstimate(flops=10**7, bytes_accessed=2**22, transcendentals=0),
        name="order_bins",
    )(own, x)


def add(a, b):
    return (a[0] + b[0], a[1] + b[1])


def sub(a, b):
    return (a[0] - b[0], a[1] - b[1])


def fan_dft(x, sign):
    root = math.sqrt(0.5)

    def quarter(a):
        return (-sign * a[1], sign * a[0]) if sign > 0 else (a[1], -a[0])

    def eighth(a):
        if sign > 0:
            return ((a[0] - a[1]) * root, (a[0] + a[1]) * root)
        return ((a[0] + a[1]) * root, (a[1] - a[0]) * root)

    def four(a, b, c, d):
        e, f, g, h = add(a, c), sub(a, c), add(b, d), quarter(sub(b, d))
        return add(e, g), add(f, h), sub(e, g), sub(f, h)

    even = four(x[0], x[2], x[4], x[6])
    odd = four(x[1], x[3], x[5], x[7])
    odd = (odd[0], eighth(odd[1]), quarter(odd[2]), quarter(eighth(odd[3])))
    return [add(p, q) for p, q in zip(even, odd)] + [sub(p, q) for p, q in zip(even, odd)]


def azimuth_step(a_ref, b_ref, f_ref, w_ref, t5_ref, t6_ref, spread, mixed, put):
    m = LINES // FAN
    tiles = [(t, slice(lane * 128, (lane + 1) * 128)) for t in range(m // 16) for lane in range(SPAN // 128)]
    for tile, lanes in tiles:
        half, line = divmod(tile * 16, OWN)
        points = []
        for n in range(FAN):
            ref, row, lines = (a_ref, line, EARLY) if line < EARLY else (b_ref, line - EARLY, LATE)
            rows = [slice(part * lines + row, part * lines + row + 16) for part in (0, 1)]
            points.append(tuple(ref[2 * n + half, row, lanes].astype(jnp.float32) for row in rows))
        for k, value in enumerate(fan_dft(points, -1)):
            if k:
                row = k * m + tile * 16
                value = times(value, (w_ref[0, row : row + 16], w_ref[1, row : row + 16]))
            for part in (0, 1):
                row = (half * 2 + part) * OWN + line
                at = k * SPAN + lanes.start
                spread[row : row + 16, at : at + 128] = bf16(value[part])
    y = dot(t5_ref[...], spread[...])
    x = []
    for k in range(FAN):
        cut = y[:, k * SPAN : (k + 1) * SPAN]
        f = (f_ref[k, 0].astype(jnp.float32), f_ref[k, 1].astype(jnp.float32))
        z = times((cut[:m], cut[m:]), f)
        x.append(jnp.concatenate([bf16(z[0]), bf16(z[1])], axis=0))
    mixed[...] = dot(t6_ref[...], jnp.concatenate(x, axis=1))
    for tile, lanes in tiles:
        points = []
        for k in range(FAN):
            at = k * SPAN + lanes.start
            row = tile * 16
            value = tuple(mixed[part * m + row : part * m + row + 16, at : at + 128] for part in (0, 1))
            if k:
                row += k * m
                value = times(value, (w_ref[0, row : row + 16], -w_ref[1, row : row + 16]))
            points.append(value)
        for p, value in enumerate(fan_dft(points, 1)):
            row = p * m + tile * 16
            for part in (0, 1):
                put(part, row, lanes, bf16(value[part]))


ROWS = WIN + 16
STEPS = PART // SPAN


def azimuth_kernel(
    me_ref, date_ref, lines_ref, bins_ref, pick_ref, a_ref, b_ref, f_ref, w_ref, t5_ref, t6_ref, *refs
):
    out_ref, *outs, slices, spread, mixed, held = refs
    step = pl.program_id(0)

    def put(part, row, lanes, value):
        out_ref[part, row : row + 16, lanes] = value
        held[step, part, row : row + 16, lanes] = value

    azimuth_step(a_ref, b_ref, f_ref, w_ref, t5_ref, t6_ref, spread, mixed, put)

    @pl.when(step == STEPS - 1)
    def _():
        me, date = me_ref[0], date_ref[0]
        for chip in range(CHIPS):
            line = lines_ref[chip]
            row = jnp.minimum(line // 16 * 16, LINES - ROWS)
            picks = [pick_ref[chip * HALF + slot, pl.ds(me, 1), :] > 0.5 for slot in range(HALF)]
            for part in (0, 1):
                for slot in range(HALF):
                    at, lane = divmod(slot * SIDE, SPAN)
                    other = held[at, part, pl.ds(pl.multiple_of(row, 16), ROWS), lane : lane + SIDE]
                    other = other.astype(jnp.float32)
                    cut = jnp.where(picks[slot], other, cut) if slot else other
                cut = pltpu.roll(cut, lax.rem(ROWS - (line - row), ROWS), 0)[:WIN]
                cut = pltpu.roll(cut, lax.rem(WIN - lax.rem(bins_ref[chip], WIN), WIN), 1)
                slices[chip * 2 + part] = bf16(cut)
        for way in range(CHIPS):
            for part in (0, 1):
                outs[way][part] = slices[2 * (way ^ (date // 2)) + part]


def azimuth_tables():
    m = LINES // FAN
    forward = np.exp(-2j * math.pi * np.outer(np.arange(m), np.arange(m)) / m) / math.sqrt(LINES)
    backward = forward.conj()
    first = from_left(forward).reshape(2 * m, 2, 2, OWN).transpose(0, 2, 1, 3).reshape(2 * m, 2 * m)
    turn = twiddles(FAN, m, -1).reshape(LINES, 1) * np.ones((1, 128))
    return parts_of(turn), as_bf16(first), as_bf16(from_left(backward))


AZIMUTH_SCRATCH = [
    pltpu.VMEM((2 * LINES // FAN, FAN * SPAN), jnp.bfloat16),
    pltpu.VMEM((2 * LINES // FAN, FAN * SPAN), jnp.float32),
]


def focus_azimuth(me, date, chip_lines, chip_bins, picks, early, late, response):
    m = LINES // FAN
    table = whole((2 * m, 2 * m))
    smem = pl.BlockSpec(memory_space=pltpu.SMEM)
    counts = (2, 2, 2, 2, 2 * CHIPS)
    return pl.pallas_call(
        azimuth_kernel,
        grid=(STEPS,),
        in_specs=[
            smem,
            smem,
            smem,
            smem,
            whole((CHIPS * HALF, N_RNG, SIDE)),
            pl.BlockSpec((N_RNG, 2 * EARLY, SPAN), lambda i: (0, 0, i)),
            pl.BlockSpec((N_RNG, 2 * LATE, SPAN), lambda i: (0, 0, i)),
            pl.BlockSpec((FAN, 2, m, SPAN), lambda i: (0, 0, 0, i)),
            whole((2, LINES, 128)),
            table,
            table,
        ],
        out_specs=[pl.BlockSpec((2, LINES, SPAN), lambda i: (0, 0, i))]
        + [whole((count, WIN, WIN)) for count in counts],
        out_shape=[jax.ShapeDtypeStruct((2, LINES, PART), jnp.bfloat16)]
        + [jax.ShapeDtypeStruct((count, WIN, WIN), jnp.bfloat16) for count in counts],
        scratch_shapes=AZIMUTH_SCRATCH + [pltpu.VMEM((STEPS, 2, LINES, SPAN), jnp.bfloat16)],
        compiler_params=pltpu.CompilerParams(vmem_limit_bytes=VMEM),
        name="focus_azimuth",
    )(me, date, chip_lines, chip_bins, picks, early, late, response, *azimuth_tables())


def regroup_kernel(f_ref, own_ref, out1_ref, out2_ref, wide):
    swaps = masks(own_ref)
    for part in (0, 1):
        for slot in range(SLOTS):
            wide[slot] = f_ref[part, :, slot * SIDE : (slot + 1) * SIDE].astype(jnp.float32)
        for k in range(FAN):
            slots = [bf16(wide[slot, pl.ds(k, 16, stride=FAN), :]) for slot in range(SLOTS)]
            slots = swapped(slots, swaps, NETWORK)
            for slot in range(HALF):
                lanes = slice(slot * SIDE, (slot + 1) * SIDE)
                out1_ref[k, part, :, lanes] = slots[slot]
                out2_ref[k, part, :, lanes] = slots[slot + HALF]


def regroup_filter(azimuth_filter, own):
    m = LINES // FAN
    return pl.pallas_call(
        regroup_kernel,
        grid=(FAN,),
        in_specs=[
            pl.BlockSpec((2, 16 * FAN, BLOCK), lambda i: (0, i, 0)),
            whole((len(NETWORK) + 2, SIDE)),
        ],
        out_specs=[pl.BlockSpec((FAN, 2, 16, PART), lambda i: (0, 0, i, 0))] * 2,
        out_shape=[jax.ShapeDtypeStruct((FAN, 2, m, PART), jnp.bfloat16)] * 2,
        scratch_shapes=[pltpu.VMEM((SLOTS, 16 * FAN, SIDE), jnp.float32)],
        compiler_params=pltpu.CompilerParams(vmem_limit_bytes=VMEM),
        cost_estimate=pl.CostEstimate(flops=10**7, bytes_accessed=2**23, transcendentals=0),
        name="regroup_filter",
    )(azimuth_filter, own)


MERGE = 512


def finish_kernel(
    own_ref, a_ref, b_ref, f_ref, w_ref, t5_ref, t6_ref, first_ref, out_ref, spread, mixed, held
):
    step = pl.program_id(0)

    @pl.when(step < STEPS)
    def _():
        def put(part, row, lanes, value):
            held[step, part, row : row + 16, lanes] = value

        azimuth_step(a_ref, b_ref, f_ref, w_ref, t5_ref, t6_ref, spread, mixed, put)

    @pl.when(step >= STEPS)
    def _():
        swaps = masks(own_ref)
        first = (step - STEPS) * MERGE
        for part in (0, 1):
            for row in range(0, MERGE, 16):
                rows = slice(row, row + 16)
                slots = [
                    first_ref[part, rows, slot * SIDE : (slot + 1) * SIDE] for slot in range(HALF)
                ]
                for slot in range(HALF):
                    at, lane = divmod(slot * SIDE, SPAN)
                    from_row = pl.ds(pl.multiple_of(first + row, 16), 16)
                    slots.append(held[at, part, from_row, lane : lane + SIDE])
                slots = swapped(slots, swaps[::-1], NETWORK[::-1])
                for slot in range(SLOTS):
                    out_ref[0, part, rows, slot * SIDE : (slot + 1) * SIDE] = slots[slot]


def finish(own, early, late, response, image):
    m = LINES // FAN
    table = whole((2 * m, 2 * m))
    return pl.pallas_call(
        finish_kernel,
        grid=(STEPS + LINES // MERGE,),
        in_specs=[
            whole((len(NETWORK) + 2, SIDE)),
            pl.BlockSpec((N_RNG, 2 * EARLY, SPAN), lambda i: (0, 0, jnp.minimum(i, STEPS - 1))),
            pl.BlockSpec((N_RNG, 2 * LATE, SPAN), lambda i: (0, 0, jnp.minimum(i, STEPS - 1))),
            pl.BlockSpec((FAN, 2, m, SPAN), lambda i: (0, 0, 0, jnp.minimum(i, STEPS - 1))),
            whole((2, LINES, 128)),
            table,
            table,
            pl.BlockSpec((2, MERGE, PART), lambda i: (0, jnp.maximum(i - STEPS, 0), 0)),
        ],
        out_specs=pl.BlockSpec(
            (1, 2, MERGE, BLOCK), lambda i: (0, 0, jnp.maximum(i - STEPS, 0), 0)
        ),
        out_shape=jax.ShapeDtypeStruct((1, 2, LINES, BLOCK), jnp.bfloat16),
        scratch_shapes=AZIMUTH_SCRATCH + [pltpu.VMEM((STEPS, 2, LINES, SPAN), jnp.bfloat16)],
        compiler_params=pltpu.CompilerParams(vmem_limit_bytes=VMEM),
        name="finish",
    )(own, early, late, response, *azimuth_tables(), image)


def pass_kernel(date_ref, mate_ref, *refs):
    ins, outs, (held,) = refs[:DATES], refs[DATES : DATES + CHIPS], refs[DATES + CHIPS :]
    date = date_ref[0]
    for way in range(CHIPS):
        for other in (0, 1):
            held[2 * way + other] = ins[CHIPS * other + way][...]
    for way in range(CHIPS):
        outs[way][...] = held[mate_ref[(2 * way) ^ date] ^ date]


def pass_on(date, partner_date, held):
    smem, vmem = pl.BlockSpec(memory_space=pltpu.SMEM), pl.BlockSpec(memory_space=pltpu.VMEM)
    return pl.pallas_call(
        pass_kernel,
        in_specs=[smem] * 2 + [vmem] * DATES,
        out_specs=[vmem] * CHIPS,
        out_shape=[jax.ShapeDtypeStruct((2, WIN, WIN), jnp.bfloat16)] * CHIPS,
        scratch_shapes=[pltpu.VMEM((DATES, 2, WIN, WIN), jnp.bfloat16)],
        name="pass_on",
    )(date, partner_date, *held)


def along_y(chips):
    return [chips[0]] + [from_ways(chips[way], "date", DATES, (2 * way,))[0] for way in (1, 2, 3)]


def gather_chip(chips):
    held = along_y(chips)
    return held + [from_ways(chip, "date", DATES, (1,))[0] for chip in held]


def transform(stacked, left, right):
    y = dot(left, jnp.concatenate(stacked, axis=1))
    half = y.shape[0] // 2
    rows = []
    for chip in range(CHIPS):
        cut = y[:, chip * WIN : (chip + 1) * WIN]
        rows.append(jnp.concatenate([bf16(cut[:half]), bf16(cut[half:])], axis=1))
    return dot(jnp.concatenate(rows, axis=0), right)


def correlate_kernel(
    date_ref, offsets_ref, own_ref, left_ref, right_ref, left3_ref, right3_ref, *refs
):
    ins, (out_ref, their_ref) = refs[:CHIPS], refs[CHIPS:]
    for way in range(CHIPS):
        their_ref[way ^ (date_ref[0] // 2)] = ins[way][...]
    left, right = left_ref[...], right_ref[...]
    inside = lax.broadcasted_iota(jnp.int32, (CHIP, WIN), 1) < CHIP
    empty = jnp.zeros((WIN - CHIP, WIN), jnp.bfloat16)
    primary = []
    for chip in range(CHIPS):
        row, col = offsets_ref[2 * chip], offsets_ref[2 * chip + 1]
        pieces = []
        for part in (0, 1):
            cut = own_ref[chip * 2 + part].astype(jnp.float32)
            cut = pltpu.roll(cut, lax.rem(WIN - row, WIN), 0)[:CHIP]
            cut = pltpu.roll(cut, lax.rem(WIN - col, WIN), 1)
            pieces += [bf16(jnp.where(inside, cut, 0.0)), empty]
        primary.append(jnp.concatenate(pieces, axis=0))
    first = transform(primary, left, right)
    second = transform(
        [jnp.concatenate([their_ref[chip, 0], their_ref[chip, 1]], axis=0) for chip in range(CHIPS)],
        left,
        right,
    )
    a = (first[:, :WIN], first[:, WIN:])
    b = (second[:, :WIN], second[:, WIN:])
    product = (a[0] * b[0] + a[1] * b[1], a[1] * b[0] - a[0] * b[1])
    product = [bf16(part) for part in product]
    surface = transform(
        [
            jnp.concatenate([part[chip * WIN : (chip + 1) * WIN] for part in product], axis=0)
            for chip in range(CHIPS)
        ],
        left3_ref[...],
        right3_ref[...],
    )
    for chip in range(CHIPS):
        out_ref[0, chip] = surface[chip * CHIP : (chip + 1) * CHIP]


def correlate(date, offsets, own, theirs):
    table = dft(WIN, -1)
    left, right = from_left(table), from_right(table)
    factor = WIN // CHIP
    keep = np.concatenate([np.arange(CHIP), WIN + np.arange(CHIP)])
    vmem = pl.BlockSpec(memory_space=pltpu.VMEM)
    return pl.pallas_call(
        correlate_kernel,
        in_specs=[pl.BlockSpec(memory_space=pltpu.SMEM)] * 2 + [vmem] * (5 + CHIPS),
        out_specs=vmem,
        out_shape=jax.ShapeDtypeStruct((1, CHIPS, CHIP, 2 * CHIP), jnp.float32),
        scratch_shapes=[pltpu.VMEM((CHIPS, 2, WIN, WIN), jnp.bfloat16)],
        compiler_params=pltpu.CompilerParams(vmem_limit_bytes=VMEM),
        name="correlate",
    )(
        date,
        offsets,
        own,
        as_bf16(left),
        as_bf16(right),
        as_bf16(left[keep]),
        as_bf16(right[:, keep] * factor),
        *theirs,
    )


def to_blocks(x):
    return lax.all_to_all(x, "rng", split_axis=0, concat_axis=0, tiled=True)


def local(
    raw_echoes, range_filter, azimuth_filter, partner_date, chip_lines, chip_bins, chip_offsets
):
    me = lax.axis_index("rng").astype(jnp.int32).reshape(1)
    date = lax.axis_index("date").astype(jnp.int32).reshape(1)
    bins = all_bins(chip_bins)
    (early,) = compress_range(raw_echoes, range_filter, 0, EARLY)
    early, bins = lax.optimization_barrier((early, bins))
    early = to_blocks(early)
    swaps, own, picks = plan(me, bins)
    late, late_two = compress_range(raw_echoes, range_filter, EARLY, LATE, swaps)
    late, own, early = lax.optimization_barrier((late, own, early))
    late = to_blocks(late)
    early, early_two = order_bins(own, early)
    response, response_two = regroup_filter(azimuth_filter, own)
    offsets = chip_offsets.reshape(-1)
    late_two, early, early_two, response, response_two, offsets = lax.optimization_barrier(
        (late_two, early, early_two, response, response_two, offsets)
    )
    late_two = to_blocks(late_two)
    first, *chips, windows = focus_azimuth(
        me, date, chip_lines, chip_bins, picks, early, late, response
    )
    held, late_two = lax.optimization_barrier((gather_chip(chips), late_two))
    theirs = along_y(pass_on(date, partner_date, held))
    correlation = correlate(date, offsets, windows, theirs)
    return (finish(own, early_two, late_two, response_two, first), correlation)


def solution(mesh):
    in_specs = (
        P("date", None, "rng", None),
        P(),
        P(None, None, "rng"),
        P(),
        P("rng"),
        P("rng"),
        P("rng", None),
    )
    out_specs = (P("date", None, None, "rng"), P("date", "rng", None, None))
    return jax.shard_map(local, mesh=mesh, in_specs=in_specs, out_specs=out_specs, check_vma=False)
```

```python
import functools
import math

import jax
import jax.numpy as jnp
import ml_dtypes
import numpy as np
from jax import lax
from jax.experimental import pallas as pl
from jax.experimental.pallas import tpu as pltpu
from jax.sharding import PartitionSpec as P

LINES = 1024
BINS = 16384
CHIP = 64
CHIPS = 4
WIN = 128
DATES = 8
N_RNG = 16
SIDE = 128
FAN = 8
BLOCK = BINS // N_RNG
OWN = LINES // N_RNG
SLOTS = 8
HALF = 4
PART = HALF * 128
SORT = ((0, 1), (2, 3), (0, 2), (1, 3), (1, 2))
NETWORK = SORT + tuple((i + 4, j + 4) for i, j in SORT) + ((0, 7), (1, 6), (2, 5), (3, 4))
EARLY = 16
LATE = OWN - EARLY
ORDER = 4
GROUP = 16
BATCH = 16
SPAN = 256
WIDE = GROUP + 8
LONG = SIDE + 8
VMEM = 56 * 1024 * 1024


def dft(length, sign):
    phase = np.outer(np.arange(length), np.arange(length)) % length
    return np.exp(sign * 2j * math.pi * phase / length) / math.sqrt(length)


def twiddles(count, other, sign):
    phase = np.outer(np.arange(count), np.arange(other))
    return np.exp(sign * 2j * math.pi * phase / (count * other))


def from_left(table):
    return np.block([[table.real, -table.imag], [table.imag, table.real]])


def from_right(table):
    return np.block([[table.real, table.imag], [-table.imag, table.real]])


def as_bf16(table):
    return jnp.asarray(np.asarray(table, np.float32).astype(ml_dtypes.bfloat16))


def parts_of(table):
    return jnp.asarray(np.stack([table.real, table.imag]).astype(np.float32))


def times(a, b):
    return (a[0] * b[0] - a[1] * b[1], a[0] * b[1] + a[1] * b[0])


def dot(a, b):
    return jnp.dot(a, b, preferred_element_type=jnp.float32)


def bf16(x):
    return x.astype(jnp.bfloat16)


def swapped(slots, swaps, pairs):
    slots = list(slots)
    for swap, (i, j) in zip(swaps, pairs):
        slots[i], slots[j] = (
            jnp.where(swap, slots[j], slots[i]),
            jnp.where(swap, slots[i], slots[j]),
        )
    return slots


def masks(ref):
    rows = [jnp.broadcast_to(ref[at : at + 1, :], (16, SIDE)) for at in range(len(NETWORK))]
    return [bf16(row) > jnp.bfloat16(0.5) for row in rows]


def plan_kernel(me_ref, near_ref, *refs):
    far_refs, (swap_ref, own_ref, pick_ref) = refs[:3], refs[3:]
    me = me_ref[0]
    lane = lax.broadcasted_iota(jnp.int32, (N_RNG, SIDE), 1)
    device = lax.broadcasted_iota(jnp.int32, (N_RNG, SIDE), 0)
    runs = []
    for chip in range(CHIPS):
        first = jnp.zeros((N_RNG, SIDE), jnp.int32)
        for far, ref in zip((0, *FAR), (near_ref, *far_refs)):
            for at, near in enumerate((0, *NEAR)):
                first = jnp.where(device == (me ^ far ^ near), ref[at * CHIPS + chip], first)
        runs.append(first // SIDE + jnp.where(lane < first % SIDE, 1, 0))
    holds = [[jnp.where(run == slot, 1.0, 0.0) for slot in range(SLOTS)] for run in runs]
    wanted = [functools.reduce(jnp.maximum, [hold[slot] for hold in holds]) for slot in range(SLOTS)]
    for at, (i, j) in enumerate(NETWORK):
        swap = wanted[j] > wanted[i]
        swap_ref[at] = jnp.where(swap, 1.0, 0.0)
        wanted = swapped(wanted, [swap], [(i, j)])
        holds = [swapped(hold, [swap], [(i, j)]) for hold in holds]
    for at in range(len(NETWORK)):
        own_ref[at : at + 1, :] = swap_ref[at, pl.ds(me, 1), :]
    for chip in range(CHIPS):
        for slot in range(HALF):
            at = chip * HALF + slot
            pick_ref[at] = holds[chip][slot]


NEAR = (1, 8, 9)
FAR = (2, 4, 6)


def from_ways(x, axis, size, ways):
    return [lax.ppermute(x, axis, [(i, i ^ way) for i in range(size)]) for way in ways]


def all_bins(chip_bins):
    near = jnp.concatenate([chip_bins] + from_ways(chip_bins, "rng", N_RNG, NEAR))
    return [near] + from_ways(near, "rng", N_RNG, FAR)


def plan(me, bins):
    smem, vmem = pl.BlockSpec(memory_space=pltpu.SMEM), pl.BlockSpec(memory_space=pltpu.VMEM)
    return pl.pallas_call(
        plan_kernel,
        in_specs=[smem] * 5,
        out_specs=[vmem] * 3,
        out_shape=[
            jax.ShapeDtypeStruct((len(NETWORK), N_RNG, SIDE), jnp.float32),
            jax.ShapeDtypeStruct((len(NETWORK) + 2, SIDE), jnp.float32),
            jax.ShapeDtypeStruct((CHIPS * HALF, N_RNG, SIDE), jnp.float32),
        ],
        name="plan",
    )(me, *bins)


def range_kernel(x_ref, h_ref, w_ref, t1_ref, t2_ref, t3_ref, t4_ref, *refs, ordered):
    s = SIDE
    *refs, xs, ys, hs = refs

    @pl.when(pl.program_id(0) == 0)
    def _():
        for part in range(2):
            for j in range(s):
                ys[j : j + 1, :] = h_ref[part : part + 1, j * s : (j + 1) * s]
            hs[part] = ys[:s, :].T

    for part in range(2):
        for n in range(s):
            row = (part * s + n) * WIDE
            xs[row : row + GROUP, :] = x_ref[0, part, :, n * s : (n + 1) * s].astype(jnp.float32)
    w = (w_ref[0], w_ref[1])
    wc = (w[0], -w[1])
    h = (hs[0], hs[1])
    for line in range(0, GROUP, BATCH):
        batch = range(line, line + BATCH)
        x = [
            jnp.concatenate(
                [bf16(xs[pl.ds(part * s * WIDE + one, s, stride=WIDE), :]) for part in (0, 1)],
                axis=0,
            )
            for one in batch
        ]
        y = dot(t1_ref[...], jnp.concatenate(x, axis=1))
        x = []
        for one in range(BATCH):
            cut = y[:, one * s : (one + 1) * s]
            z = times((cut[:s], cut[s:]), w)
            x.append(jnp.concatenate([bf16(z[0]), bf16(z[1])], axis=1))
        y = dot(jnp.concatenate(x, axis=0), t2_ref[...])
        x = []
        for one in range(BATCH):
            cut = y[one * s : (one + 1) * s]
            z = times((cut[:, :s], cut[:, s:]), h)
            x.append(jnp.concatenate([bf16(z[0]), bf16(z[1])], axis=1))
        y = dot(jnp.concatenate(x, axis=0), t3_ref[...])
        x = []
        for one in range(BATCH):
            cut = y[one * s : (one + 1) * s]
            z = times((cut[:, :s], cut[:, s:]), wc)
            x.append(jnp.concatenate([bf16(z[0]), bf16(z[1])], axis=0))
        y = dot(t4_ref[...], jnp.concatenate(x, axis=1))
        for one in range(BATCH):
            for part in (0, 1):
                row = (part * GROUP + line + one) * LONG
                ys[row : row + s, :] = y[
                    part * s : (part + 1) * s, one * s : (one + 1) * s
                ]
    for dest in range(N_RNG):
        if ordered:
            swap_ref, out1_ref, out2_ref = refs
            swaps = masks(swap_ref.at[:, dest])
        else:
            (out_ref,) = refs
        for part in (0, 1):
            slots = []
            for slot in range(SLOTS):
                row = part * GROUP * LONG + dest * SLOTS + slot
                slots.append(bf16(ys[pl.ds(row, GROUP, stride=LONG), :]))
            if not ordered:
                for slot in range(SLOTS):
                    out_ref[dest, part, :, slot * s : (slot + 1) * s] = slots[slot]
                continue
            slots = swapped(slots, swaps, NETWORK)
            for slot in range(HALF):
                lanes = slice(slot * s, (slot + 1) * s)
                out1_ref[dest, part, :, lanes] = slots[slot]
                out2_ref[dest, part, :, lanes] = slots[slot + HALF]


def whole(shape):
    return pl.BlockSpec(shape, lambda *_: (0,) * len(shape))


def compress_range(raw_echoes, range_filter, first, lines, swaps=None):
    forward = dft(SIDE, -1)
    backward = dft(SIDE, 1)
    tables = [
        as_bf16(from_left(forward)),
        as_bf16(from_right(forward)),
        as_bf16(from_right(backward)),
        as_bf16(from_left(backward)),
    ]
    turn = parts_of(twiddles(SIDE, SIDE, -1))
    table = whole((2 * SIDE, 2 * SIDE))
    ordered = swaps is not None
    width, count = (PART, 2) if ordered else (BLOCK, 1)
    outs = pl.pallas_call(
        functools.partial(range_kernel, ordered=ordered),
        grid=(lines // GROUP,),
        in_specs=[
            pl.BlockSpec((1, 2, GROUP, BINS), lambda i: (0, 0, i + first // GROUP, 0)),
            whole((2, BINS)),
            whole((2, SIDE, SIDE)),
            table,
            table,
            table,
            table,
        ]
        + [whole((len(NETWORK), N_RNG, SIDE))] * ordered,
        out_specs=[pl.BlockSpec((N_RNG, 2, GROUP, width), lambda i: (0, 0, i, 0))] * count,
        out_shape=[jax.ShapeDtypeStruct((N_RNG, 2, lines, width), jnp.bfloat16)] * count,
        scratch_shapes=[
            pltpu.VMEM((2 * SIDE * WIDE, SIDE), jnp.float32),
            pltpu.VMEM((2 * LONG * GROUP, SIDE), jnp.float32),
            pltpu.VMEM((2, SIDE, SIDE), jnp.float32),
        ],
        compiler_params=pltpu.CompilerParams(vmem_limit_bytes=VMEM),
        cost_estimate=pl.CostEstimate(flops=4 * 10**9, bytes_accessed=2**22, transcendentals=0),
        name="compress_range",
    )(raw_echoes, range_filter, turn, *tables, *([swaps] * ordered))
    return [out.reshape(N_RNG, 2 * lines, width) for out in outs]


def order_kernel(own_ref, x_ref, out1_ref, out2_ref):
    swaps = masks(own_ref)
    for device in range(ORDER):
        for row in range(0, 2 * EARLY, 16):
            rows = slice(row, row + 16)
            slots = [
                x_ref[device, rows, slot * SIDE : (slot + 1) * SIDE] for slot in range(SLOTS)
            ]
            slots = swapped(slots, swaps, NETWORK)
            for slot in range(HALF):
                lanes = slice(slot * SIDE, (slot + 1) * SIDE)
                out1_ref[device, rows, lanes] = slots[slot]
                out2_ref[device, rows, lanes] = slots[slot + HALF]


def order_bins(own, x):
    return pl.pallas_call(
        order_kernel,
        grid=(N_RNG // ORDER,),
        in_specs=[
            whole((len(NETWORK) + 2, SIDE)),
            pl.BlockSpec((ORDER, 2 * EARLY, BLOCK), lambda i: (i, 0, 0)),
        ],
        out_specs=[pl.BlockSpec((ORDER, 2 * EARLY, PART), lambda i: (i, 0, 0))] * 2,
        out_shape=[jax.ShapeDtypeStruct((N_RNG, 2 * EARLY, PART), jnp.bfloat16)] * 2,
        compiler_params=pltpu.CompilerParams(vmem_limit_bytes=VMEM),
        cost_estimate=pl.CostEstimate(flops=10**7, bytes_accessed=2**22, transcendentals=0),
        name="order_bins",
    )(own, x)


def add(a, b):
    return (a[0] + b[0], a[1] + b[1])


def sub(a, b):
    return (a[0] - b[0], a[1] - b[1])


def fan_dft(x, sign):
    root = math.sqrt(0.5)

    def quarter(a):
        return (-sign * a[1], sign * a[0]) if sign > 0 else (a[1], -a[0])

    def eighth(a):
        if sign > 0:
            return ((a[0] - a[1]) * root, (a[0] + a[1]) * root)
        return ((a[0] + a[1]) * root, (a[1] - a[0]) * root)

    def four(a, b, c, d):
        e, f, g, h = add(a, c), sub(a, c), add(b, d), quarter(sub(b, d))
        return add(e, g), add(f, h), sub(e, g), sub(f, h)

    even = four(x[0], x[2], x[4], x[6])
    odd = four(x[1], x[3], x[5], x[7])
    odd = (odd[0], eighth(odd[1]), quarter(odd[2]), quarter(eighth(odd[3])))
    return [add(p, q) for p, q in zip(even, odd)] + [sub(p, q) for p, q in zip(even, odd)]


def azimuth_step(a_ref, b_ref, f_ref, w_ref, t5_ref, t6_ref, spread, mixed, put):
    m = LINES // FAN
    tiles = [(t, slice(lane * 128, (lane + 1) * 128)) for t in range(m // 16) for lane in range(SPAN // 128)]
    for tile, lanes in tiles:
        half, line = divmod(tile * 16, OWN)
        points = []
        for n in range(FAN):
            ref, row, lines = (a_ref, line, EARLY) if line < EARLY else (b_ref, line - EARLY, LATE)
            rows = [slice(part * lines + row, part * lines + row + 16) for part in (0, 1)]
            points.append(tuple(ref[2 * n + half, row, lanes].astype(jnp.float32) for row in rows))
        for k, value in enumerate(fan_dft(points, -1)):
            if k:
                row = k * m + tile * 16
                value = times(value, (w_ref[0, row : row + 16], w_ref[1, row : row + 16]))
            for part in (0, 1):
                row = (half * 2 + part) * OWN + line
                at = k * SPAN + lanes.start
                spread[row : row + 16, at : at + 128] = bf16(value[part])
    y = dot(t5_ref[...], spread[...])
    x = []
    for k in range(FAN):
        cut = y[:, k * SPAN : (k + 1) * SPAN]
        f = (f_ref[k, 0].astype(jnp.float32), f_ref[k, 1].astype(jnp.float32))
        z = times((cut[:m], cut[m:]), f)
        x.append(jnp.concatenate([bf16(z[0]), bf16(z[1])], axis=0))
    mixed[...] = dot(t6_ref[...], jnp.concatenate(x, axis=1))
    for tile, lanes in tiles:
        points = []
        for k in range(FAN):
            at = k * SPAN + lanes.start
            row = tile * 16
            value = tuple(mixed[part * m + row : part * m + row + 16, at : at + 128] for part in (0, 1))
            if k:
                row += k * m
                value = times(value, (w_ref[0, row : row + 16], -w_ref[1, row : row + 16]))
            points.append(value)
        for p, value in enumerate(fan_dft(points, 1)):
            row = p * m + tile * 16
            for part in (0, 1):
                put(part, row, lanes, bf16(value[part]))


ROWS = WIN + 16
STEPS = PART // SPAN


def azimuth_kernel(
    me_ref, date_ref, lines_ref, bins_ref, pick_ref, a_ref, b_ref, f_ref, w_ref, t5_ref, t6_ref, *refs
):
    out_ref, *outs, slices, spread, mixed, held = refs
    step = pl.program_id(0)

    def put(part, row, lanes, value):
        out_ref[part, row : row + 16, lanes] = value
        held[step, part, row : row + 16, lanes] = value

    azimuth_step(a_ref, b_ref, f_ref, w_ref, t5_ref, t6_ref, spread, mixed, put)

    @pl.when(step == STEPS - 1)
    def _():
        me, date = me_ref[0], date_ref[0]
        for chip in range(CHIPS):
            line = lines_ref[chip]
            row = jnp.minimum(line // 16 * 16, LINES - ROWS)
            picks = [pick_ref[chip * HALF + slot, pl.ds(me, 1), :] > 0.5 for slot in range(HALF)]
            for part in (0, 1):
                for slot in range(HALF):
                    at, lane = divmod(slot * SIDE, SPAN)
                    other = held[at, part, pl.ds(pl.multiple_of(row, 16), ROWS), lane : lane + SIDE]
                    other = other.astype(jnp.float32)
                    cut = jnp.where(picks[slot], other, cut) if slot else other
                cut = pltpu.roll(cut, lax.rem(ROWS - (line - row), ROWS), 0)[:WIN]
                cut = pltpu.roll(cut, lax.rem(WIN - lax.rem(bins_ref[chip], WIN), WIN), 1)
                slices[chip * 2 + part] = bf16(cut)
        for way in range(CHIPS):
            for part in (0, 1):
                outs[way][part] = slices[2 * (way ^ (date // 2)) + part]


def azimuth_tables():
    m = LINES // FAN
    forward = np.exp(-2j * math.pi * np.outer(np.arange(m), np.arange(m)) / m) / math.sqrt(LINES)
    backward = forward.conj()
    first = from_left(forward).reshape(2 * m, 2, 2, OWN).transpose(0, 2, 1, 3).reshape(2 * m, 2 * m)
    turn = twiddles(FAN, m, -1).reshape(LINES, 1) * np.ones((1, 128))
    return parts_of(turn), as_bf16(first), as_bf16(from_left(backward))


AZIMUTH_SCRATCH = [
    pltpu.VMEM((2 * LINES // FAN, FAN * SPAN), jnp.bfloat16),
    pltpu.VMEM((2 * LINES // FAN, FAN * SPAN), jnp.float32),
]


def focus_azimuth(me, date, chip_lines, chip_bins, picks, early, late, response):
    m = LINES // FAN
    table = whole((2 * m, 2 * m))
    smem = pl.BlockSpec(memory_space=pltpu.SMEM)
    counts = (2, 2, 2, 2, 2 * CHIPS)
    return pl.pallas_call(
        azimuth_kernel,
        grid=(STEPS,),
        in_specs=[
            smem,
            smem,
            smem,
            smem,
            whole((CHIPS * HALF, N_RNG, SIDE)),
            pl.BlockSpec((N_RNG, 2 * EARLY, SPAN), lambda i: (0, 0, i)),
            pl.BlockSpec((N_RNG, 2 * LATE, SPAN), lambda i: (0, 0, i)),
            pl.BlockSpec((FAN, 2, m, SPAN), lambda i: (0, 0, 0, i)),
            whole((2, LINES, 128)),
            table,
            table,
        ],
        out_specs=[pl.BlockSpec((2, LINES, SPAN), lambda i: (0, 0, i))]
        + [whole((count, WIN, WIN)) for count in counts],
        out_shape=[jax.ShapeDtypeStruct((2, LINES, PART), jnp.bfloat16)]
        + [jax.ShapeDtypeStruct((count, WIN, WIN), jnp.bfloat16) for count in counts],
        scratch_shapes=AZIMUTH_SCRATCH + [pltpu.VMEM((STEPS, 2, LINES, SPAN), jnp.bfloat16)],
        compiler_params=pltpu.CompilerParams(vmem_limit_bytes=VMEM),
        name="focus_azimuth",
    )(me, date, chip_lines, chip_bins, picks, early, late, response, *azimuth_tables())


def regroup_kernel(f_ref, own_ref, out1_ref, out2_ref, wide):
    swaps = masks(own_ref)
    for part in (0, 1):
        for slot in range(SLOTS):
            wide[slot] = f_ref[part, :, slot * SIDE : (slot + 1) * SIDE].astype(jnp.float32)
        for k in range(FAN):
            slots = [bf16(wide[slot, pl.ds(k, 16, stride=FAN), :]) for slot in range(SLOTS)]
            slots = swapped(slots, swaps, NETWORK)
            for slot in range(HALF):
                lanes = slice(slot * SIDE, (slot + 1) * SIDE)
                out1_ref[k, part, :, lanes] = slots[slot]
                out2_ref[k, part, :, lanes] = slots[slot + HALF]


def regroup_filter(azimuth_filter, own):
    m = LINES // FAN
    return pl.pallas_call(
        regroup_kernel,
        grid=(FAN,),
        in_specs=[
            pl.BlockSpec((2, 16 * FAN, BLOCK), lambda i: (0, i, 0)),
            whole((len(NETWORK) + 2, SIDE)),
        ],
        out_specs=[pl.BlockSpec((FAN, 2, 16, PART), lambda i: (0, 0, i, 0))] * 2,
        out_shape=[jax.ShapeDtypeStruct((FAN, 2, m, PART), jnp.bfloat16)] * 2,
        scratch_shapes=[pltpu.VMEM((SLOTS, 16 * FAN, SIDE), jnp.float32)],
        compiler_params=pltpu.CompilerParams(vmem_limit_bytes=VMEM),
        cost_estimate=pl.CostEstimate(flops=10**7, bytes_accessed=2**23, transcendentals=0),
        name="regroup_filter",
    )(azimuth_filter, own)


MERGE = 512


def finish_kernel(
    own_ref, a_ref, b_ref, f_ref, w_ref, t5_ref, t6_ref, first_ref, out_ref, spread, mixed, held
):
    step = pl.program_id(0)

    @pl.when(step < STEPS)
    def _():
        def put(part, row, lanes, value):
            held[step, part, row : row + 16, lanes] = value

        azimuth_step(a_ref, b_ref, f_ref, w_ref, t5_ref, t6_ref, spread, mixed, put)

    @pl.when(step >= STEPS)
    def _():
        swaps = masks(own_ref)
        first = (step - STEPS) * MERGE
        for part in (0, 1):
            for row in range(0, MERGE, 16):
                rows = slice(row, row + 16)
                slots = [
                    first_ref[part, rows, slot * SIDE : (slot + 1) * SIDE] for slot in range(HALF)
                ]
                for slot in range(HALF):
                    at, lane = divmod(slot * SIDE, SPAN)
                    from_row = pl.ds(pl.multiple_of(first + row, 16), 16)
                    slots.append(held[at, part, from_row, lane : lane + SIDE])
                slots = swapped(slots, swaps[::-1], NETWORK[::-1])
                for slot in range(SLOTS):
                    out_ref[0, part, rows, slot * SIDE : (slot + 1) * SIDE] = slots[slot]


def finish(own, early, late, response, image):
    m = LINES // FAN
    table = whole((2 * m, 2 * m))
    return pl.pallas_call(
        finish_kernel,
        grid=(STEPS + LINES // MERGE,),
        in_specs=[
            whole((len(NETWORK) + 2, SIDE)),
            pl.BlockSpec((N_RNG, 2 * EARLY, SPAN), lambda i: (0, 0, jnp.minimum(i, STEPS - 1))),
            pl.BlockSpec((N_RNG, 2 * LATE, SPAN), lambda i: (0, 0, jnp.minimum(i, STEPS - 1))),
            pl.BlockSpec((FAN, 2, m, SPAN), lambda i: (0, 0, 0, jnp.minimum(i, STEPS - 1))),
            whole((2, LINES, 128)),
            table,
            table,
            pl.BlockSpec((2, MERGE, PART), lambda i: (0, jnp.maximum(i - STEPS, 0), 0)),
        ],
        out_specs=pl.BlockSpec(
            (1, 2, MERGE, BLOCK), lambda i: (0, 0, jnp.maximum(i - STEPS, 0), 0)
        ),
        out_shape=jax.ShapeDtypeStruct((1, 2, LINES, BLOCK), jnp.bfloat16),
        scratch_shapes=AZIMUTH_SCRATCH + [pltpu.VMEM((STEPS, 2, LINES, SPAN), jnp.bfloat16)],
        compiler_params=pltpu.CompilerParams(vmem_limit_bytes=VMEM),
        name="finish",
    )(own, early, late, response, *azimuth_tables(), image)


def pass_kernel(date_ref, mate_ref, *refs):
    ins, outs, (held,) = refs[:DATES], refs[DATES : DATES + CHIPS], refs[DATES + CHIPS :]
    date = date_ref[0]
    for way in range(CHIPS):
        for other in (0, 1):
            held[2 * way + other] = ins[CHIPS * other + way][...]
    for way in range(CHIPS):
        outs[way][...] = held[mate_ref[(2 * way) ^ date] ^ date]


def pass_on(date, partner_date, held):
    smem, vmem = pl.BlockSpec(memory_space=pltpu.SMEM), pl.BlockSpec(memory_space=pltpu.VMEM)
    return pl.pallas_call(
        pass_kernel,
        in_specs=[smem] * 2 + [vmem] * DATES,
        out_specs=[vmem] * CHIPS,
        out_shape=[jax.ShapeDtypeStruct((2, WIN, WIN), jnp.bfloat16)] * CHIPS,
        scratch_shapes=[pltpu.VMEM((DATES, 2, WIN, WIN), jnp.bfloat16)],
        name="pass_on",
    )(date, partner_date, *held)


def along_y(chips):
    return [chips[0]] + [from_ways(chips[way], "date", DATES, (2 * way,))[0] for way in (1, 2, 3)]


def gather_chip(chips):
    held = along_y(chips)
    return held + [from_ways(chip, "date", DATES, (1,))[0] for chip in held]


def transform(stacked, left, right):
    y = dot(left, jnp.concatenate(stacked, axis=1))
    half = y.shape[0] // 2
    rows = []
    for chip in range(CHIPS):
        cut = y[:, chip * WIN : (chip + 1) * WIN]
        rows.append(jnp.concatenate([bf16(cut[:half]), bf16(cut[half:])], axis=1))
    return dot(jnp.concatenate(rows, axis=0), right)


def correlate_kernel(
    date_ref, offsets_ref, own_ref, left_ref, right_ref, left3_ref, right3_ref, *refs
):
    ins, (out_ref, their_ref) = refs[:CHIPS], refs[CHIPS:]
    for way in range(CHIPS):
        their_ref[way ^ (date_ref[0] // 2)] = ins[way][...]
    left, right = left_ref[...], right_ref[...]
    inside = lax.broadcasted_iota(jnp.int32, (CHIP, WIN), 1) < CHIP
    empty = jnp.zeros((WIN - CHIP, WIN), jnp.bfloat16)
    primary = []
    for chip in range(CHIPS):
        row, col = offsets_ref[2 * chip], offsets_ref[2 * chip + 1]
        pieces = []
        for part in (0, 1):
            cut = own_ref[chip * 2 + part].astype(jnp.float32)
            cut = pltpu.roll(cut, lax.rem(WIN - row, WIN), 0)[:CHIP]
            cut = pltpu.roll(cut, lax.rem(WIN - col, WIN), 1)
            pieces += [bf16(jnp.where(inside, cut, 0.0)), empty]
        primary.append(jnp.concatenate(pieces, axis=0))
    first = transform(primary, left, right)
    second = transform(
        [jnp.concatenate([their_ref[chip, 0], their_ref[chip, 1]], axis=0) for chip in range(CHIPS)],
        left,
        right,
    )
    a = (first[:, :WIN], first[:, WIN:])
    b = (second[:, :WIN], second[:, WIN:])
    product = (a[0] * b[0] + a[1] * b[1], a[1] * b[0] - a[0] * b[1])
    product = [bf16(part) for part in product]
    surface = transform(
        [
            jnp.concatenate([part[chip * WIN : (chip + 1) * WIN] for part in product], axis=0)
            for chip in range(CHIPS)
        ],
        left3_ref[...],
        right3_ref[...],
    )
    for chip in range(CHIPS):
        out_ref[0, chip] = surface[chip * CHIP : (chip + 1) * CHIP]


def correlate(date, offsets, own, theirs):
    table = dft(WIN, -1)
    left, right = from_left(table), from_right(table)
    factor = WIN // CHIP
    keep = np.concatenate([np.arange(CHIP), WIN + np.arange(CHIP)])
    vmem = pl.BlockSpec(memory_space=pltpu.VMEM)
    return pl.pallas_call(
        correlate_kernel,
        in_specs=[pl.BlockSpec(memory_space=pltpu.SMEM)] * 2 + [vmem] * (5 + CHIPS),
        out_specs=vmem,
        out_shape=jax.ShapeDtypeStruct((1, CHIPS, CHIP, 2 * CHIP), jnp.float32),
        scratch_shapes=[pltpu.VMEM((CHIPS, 2, WIN, WIN), jnp.bfloat16)],
        compiler_params=pltpu.CompilerParams(vmem_limit_bytes=VMEM),
        name="correlate",
    )(
        date,
        offsets,
        own,
        as_bf16(left),
        as_bf16(right),
        as_bf16(left[keep]),
        as_bf16(right[:, keep] * factor),
        *theirs,
    )


def to_blocks(x):
    return lax.all_to_all(x, "rng", split_axis=0, concat_axis=0, tiled=True)


def local(
    raw_echoes, range_filter, azimuth_filter, partner_date, chip_lines, chip_bins, chip_offsets
):
    me = lax.axis_index("rng").astype(jnp.int32).reshape(1)
    date = lax.axis_index("date").astype(jnp.int32).reshape(1)
    bins = all_bins(chip_bins)
    (early,) = compress_range(raw_echoes, range_filter, 0, EARLY)
    early, bins[3] = lax.optimization_barrier((early, bins[3]))
    early = to_blocks(early)
    swaps, own, picks = plan(me, bins)
    late, late_two = compress_range(raw_echoes, range_filter, EARLY, LATE, swaps)
    late, own, early = lax.optimization_barrier((late, own, early))
    late = to_blocks(late)
    early, early_two = order_bins(own, early)
    response, response_two = regroup_filter(azimuth_filter, own)
    offsets = chip_offsets.reshape(-1)
    late_two, early, early_two, response, response_two, offsets = lax.optimization_barrier(
        (late_two, early, early_two, response, response_two, offsets)
    )
    late_two = to_blocks(late_two)
    first, *chips, windows = focus_azimuth(
        me, date, chip_lines, chip_bins, picks, early, late, response
    )
    held, late_two = lax.optimization_barrier((gather_chip(chips), late_two))
    theirs = along_y(pass_on(date, partner_date, held))
    correlation = correlate(date, offsets, windows, theirs)
    return (finish(own, early_two, late_two, response_two, first), correlation)


def solution(mesh):
    in_specs = (
        P("date", None, "rng", None),
        P(),
        P(None, None, "rng"),
        P(),
        P("rng"),
        P("rng"),
        P("rng", None),
    )
    out_specs = (P("date", None, None, "rng"), P("date", "rng", None, None))
    return jax.shard_map(local, mesh=mesh, in_specs=in_specs, out_specs=out_specs, check_vma=False)
```
